128 devices in a mesh: row: 16 (over x, z_hi, core), col: 8 (over y, z_lo).
Axes of the slice: x: 4, y: 4, z: 4 (z_hi: 2, z_lo: 2; z = z_hi * 2 + z_lo), core: 2. Of those that a mesh axis runs over, the one named last changes fastest.
Arguments:
- front: float32 [48, 16, 128, 2, 8, 128], P(None, 'row', None, None, 'col')
- child_tiles: float32 [16, 8, 128, 128, 128], P('row', 'col'), may hold values from -1.5 to 1.5
- child_rows: int32 [16, 8, 128], P('row', 'col'), may hold values from 0 to 767, as said below
- child_cols: int32 [16, 8, 128], P('row', 'col'), may hold values from 0 to 15, as said below
Outputs:
- factored: float32 [48, 16, 128, 2, 8, 128], P(None, 'row', None, None, 'col')
The draws below stay inside these ranges and needn't reach their ends.
Inputs may be any that keep to these rules, and one draw needn't show every extreme that they name: `child_rows`: parent block row of each child block. The owner of front block (i, j) is device (i mod 16, j mod 8); from one device at most 2 child blocks go to one owner, and some owners receive exactly 2 from every device. `child_cols`: parent block column of each child block, among the 2048 columns held; same owner bound as for child_rows.
All inputs are finite; a program needn't handle non-finite values.
Results may differ from the reference program's by a relative error of at most 0.00005.
Values sent between devices are 32-bit elements; how exact they have to be, the bound alone decides.
No kernel may reach another device: no remote copies, remote signals or barrier semaphores. Data moves between devices by JAX's collectives and lax.ppermute only.
A program may use at most 192 MiB of HBM per device.

```python
import jax
import jax.numpy as jnp
from jax import lax

B = 128
F = 98304
CBD = 2
CAP = 2
RBD = 48
W = 2048
TILES = 128
N_ROW = 16
N_COL = 8


def child_map(key):
    hot_key, cold_key, order_key, row_key, col_key = jax.random.split(key, 5)
    devices = N_ROW * N_COL
    slot_total = devices * CAP
    hot_count = TILES // (2 * CAP)
    ranking = jax.random.permutation(hot_key, devices)
    hot_owner = ranking[:hot_count].astype(jnp.int32)
    hot_flag = jnp.zeros((devices,), jnp.int32).at[hot_owner].set(1)
    slot_ids = jnp.arange(slot_total, dtype=jnp.int32)
    scores = jax.random.randint(cold_key, (devices, slot_total), 0, 2 ** 20) * slot_total + slot_ids[None, :]
    scores = jnp.where(hot_flag[slot_ids // CAP][None, :] == 1, -1, scores)
    cold_slots = lax.top_k(scores, TILES - hot_count * CAP)[1].astype(jnp.int32)
    hot_list = jnp.broadcast_to(jnp.repeat(hot_owner, CAP)[None, :], (devices, hot_count * CAP))
    owners = jnp.concatenate([hot_list, cold_slots // CAP], axis=1)
    owners = jax.random.permutation(order_key, owners, axis=1, independent=True)
    parent_rows = owners // N_COL + N_ROW * jax.random.randint(row_key, owners.shape, 0, RBD)
    parent_cols = owners % N_COL + N_COL * jax.random.randint(col_key, owners.shape, 0, CBD)
    return (parent_rows.reshape(N_ROW, N_COL, TILES).astype(jnp.int32), parent_cols.reshape(N_ROW, N_COL, TILES).astype(jnp.int32))


def draw_child_rows(key, part):
    parent_rows, parent_cols = child_map(key)
    return parent_rows


def draw_child_cols(key, part):
    parent_rows, parent_cols = child_map(key)
    return parent_cols


def draw_front(key, part):
    key = jax.random.fold_in(key, 3)
    noise_key, diag_key = jax.random.split(key)
    noise_part = 0.05 * jax.random.normal(noise_key, (F, W), jnp.float32)
    diag_lift = 8.0 + 4.0 * jax.random.uniform(diag_key, (F, W), jnp.float32)
    row_ids = jnp.arange(F, dtype=jnp.int32)[:, None]
    col_ids = jnp.arange(W, dtype=jnp.int32)[None, :]
    matrix = noise_part + jnp.where(row_ids == col_ids, diag_lift, 0.0)
    return matrix.reshape(RBD, N_ROW, B, CBD, N_COL, B).astype(jnp.float32)


def block_levels(rng, dims, cuts, smallest, top_value):
    def one(position, shards_of):
        heights = jax.random.uniform(jax.random.fold_in(jax.random.fold_in(rng, 6), position), (shards_of,), jnp.float32, smallest / len(cuts), top_value / len(cuts))
        return jnp.repeat(jnp.exp(heights), dims[position] // shards_of).reshape((-1,) + (1,) * (len(dims) - position - 1))

    level = one(*cuts[0])
    for cut in cuts[1:]:
        level = level * one(*cut)
    return level


def centred(key, extent, spread, limit, shards=(), kind=jnp.bfloat16):
    entries = jax.random.normal(key, extent, jnp.float32) * spread
    if len(shards) > 0:
        entries = block_levels(key, extent, shards, -0.22, 0.18) * entries
    return jnp.clip(entries, min=-limit, max=limit).astype(kind)


def setup_inputs(seed: int = 0) -> dict:
    seeds = jax.random.split(jax.random.key(seed), 5)
    return {
        "front": draw_front(jax.random.fold_in(seeds[4], 71), 0),
        "child_tiles": centred(seeds[1], (N_ROW, N_COL, TILES, B, B), 0.1, 1.5, ((0, 16), (1, 8)), jnp.float32),
        "child_rows": draw_child_rows(jax.random.fold_in(seeds[4], 71), 0),
        "child_cols": draw_child_cols(jax.random.fold_in(seeds[4], 71), 0),
    }


def reference(front, child_tiles, child_rows, child_cols):
    block_rows = F // B
    block_cols = W // B
    blocks = front.reshape(block_rows, B, block_cols, B)
    flat_tiles = child_tiles.reshape(-1, B, B)
    parent_rows = child_rows.reshape(-1)
    parent_cols = child_cols.reshape(-1)
    blocks = blocks.at[parent_rows, :, parent_cols, :].add(flat_tiles)
    assembled = blocks.reshape(F, W)
    column = assembled[:, :B]
    corner = column[:B]
    pivot_block = 0.5 * (corner + corner.T)
    factor = jnp.linalg.cholesky(pivot_block)
    panel_rows = jax.scipy.linalg.solve_triangular(factor, column.T, lower=True).T
    update = jnp.dot(panel_rows, panel_rows[:W].T, precision=lax.Precision.HIGHEST)
    row_ids = jnp.arange(F, dtype=jnp.int32)[:, None]
    col_ids = jnp.arange(W, dtype=jnp.int32)[None, :]
    result = assembled - jnp.where(row_ids >= B, update, jnp.zeros_like(update))
    result = jnp.where(col_ids < B, jnp.pad(panel_rows, ((0, 0), (0, W - B))), result)
    return result.reshape(RBD, N_ROW, B, CBD, N_COL, B)
```

```python
import functools

import jax
import jax.numpy as jnp
from jax import lax
from jax.experimental import pallas as pl
from jax.experimental.pallas import tpu as pltpu
from jax.sharding import PartitionSpec as P

CAP = 2
HIGH = lax.Precision.HIGHEST
SMEM = pltpu.SMEM
VMEM = pltpu.VMEM


def tables(parent_rows, parent_cols, row_index, row_count, col_count):
    devices = row_count * col_count
    tiles = parent_rows.shape[0]
    order = jnp.arange(tiles, dtype=jnp.int32)
    row_of = parent_rows % row_count
    owners = row_of * col_count + parent_cols % col_count
    same = (owners[:, None] == owners[None, :]) & (order[None, :] < order[:, None])
    before = jnp.sum(same.astype(jnp.int32), axis=1)
    slot = owners * CAP + before
    block = parent_rows // row_count
    panel = parent_cols == 0
    place = block * (2 * 128) + parent_cols // col_count
    dest = jnp.arange(devices, dtype=jnp.int32)[:, None, None]
    part = jnp.arange(2 * CAP, dtype=jnp.int32)[None, :, None]
    in_main = (part < CAP) & (slot == dest * CAP + part) & ~panel
    in_panel = (part >= CAP) & panel & (row_of == dest // col_count) & (before == part - CAP)
    message = (
        jnp.sum(jnp.where(in_main, place + 1, 0) + jnp.where(in_panel, block + 1, 0), axis=2) - 1
    )
    panel_slot = (row_of ^ row_index) * CAP + before
    wanted = jnp.arange(row_count * CAP, dtype=jnp.int32)[:, None]
    chosen = panel & (panel_slot == wanted)
    panel_tiles = jnp.sum(jnp.where(chosen, order, 0), axis=1)
    return slot, panel_tiles, message


def pack_kernel(slot, panel_tiles, tiles, send, *rest):
    panels, (main_sem, panel_sem) = rest[:-2], rest[-2:]
    for k, panel in enumerate(panels):
        for s in range(CAP):
            pltpu.make_async_copy(
                tiles.at[panel_tiles[k * CAP + s]], panel.at[s], panel_sem.at[k]
            ).start()

    def start(k, carry):
        pltpu.make_async_copy(tiles.at[k], send.at[slot[k]], main_sem).start()
        return carry

    count = tiles.shape[0]
    lax.fori_loop(0, count, start, 0, unroll=8)
    for k, panel in enumerate(panels):
        pltpu.make_async_copy(tiles.at[pl.ds(0, CAP)], panel, panel_sem.at[k]).wait()
    pltpu.make_async_copy(tiles, send.at[pl.ds(0, count)], main_sem).wait()


def pack(slot, panel_tiles, tiles, slots, row_count):
    size = tiles.shape[1]
    out = [jax.ShapeDtypeStruct((slots, size, size), jnp.float32)]
    out += [jax.ShapeDtypeStruct((CAP, size, size), jnp.float32)] * row_count
    result = pl.pallas_call(
        pack_kernel,
        out_shape=out,
        in_specs=[
            pl.BlockSpec(memory_space=SMEM),
            pl.BlockSpec(memory_space=SMEM),
            pl.BlockSpec(memory_space=pl.ANY),
        ],
        out_specs=[pl.BlockSpec(memory_space=pl.ANY)] * len(out),
        scratch_shapes=[pltpu.SemaphoreType.DMA, pltpu.SemaphoreType.DMA((row_count,))],
        name="pack",
    )(slot, panel_tiles, tiles)
    return result[0], result[1:]


def column_kernel(shape, where, message, front, *refs):
    row_count, col_count, row_blocks, share = shape
    arrived = refs[:row_count]
    parts = refs[row_count : row_count + col_count]
    total = refs[-1]
    row_index, col_index = where[0], where[1]
    size = total.shape[1]

    @pl.when(col_index == 0)
    def _():
        def first(a, carry):
            total[a] = front[pl.ds(a * 2 * size, size, stride=2), :]
            return carry

        lax.fori_loop(0, row_blocks, first, 0)

    @pl.when(col_index != 0)
    def _():
        total[...] = jnp.zeros_like(total)

    for k in range(row_count):
        base = ((row_index ^ k) * col_count + col_index) * 2 * CAP + CAP
        for s in range(CAP):
            block = message[base + s]

            @pl.when(block >= 0)
            def _():
                total[block] += arrived[k][s]

    for k in range(col_count):
        parts[k][0] = total[0]
        parts[k][pl.ds(1, share)] = total[pl.ds((col_index ^ k) * share, share)]


def partial_column(where, message, front, arrived, row_count, col_count, row_blocks):
    size = front.shape[1]
    share = row_blocks // col_count
    out = [jax.ShapeDtypeStruct((share + 1, size, size), jnp.float32)] * col_count
    return pl.pallas_call(
        functools.partial(column_kernel, (row_count, col_count, row_blocks, share)),
        out_shape=out,
        in_specs=[pl.BlockSpec(memory_space=SMEM)] * 2
        + [pl.BlockSpec(memory_space=VMEM)] * (1 + row_count),
        out_specs=[pl.BlockSpec(memory_space=VMEM)] * col_count,
        scratch_shapes=[VMEM((row_blocks, size, size), jnp.float32)],
        compiler_params=pltpu.CompilerParams(vmem_limit_bytes=40 << 20),
        name="partial_column",
    )(where, message, front, *arrived)


def update_kernel(shape, where, front, inverse_t, window, *refs):
    row_blocks, share, col_count = shape
    shares = refs[:col_count]
    base, column, sems = refs[col_count:]
    row_index, col_index = where[0], where[1]
    size = inverse_t.shape[0]
    copies = [
        pltpu.make_async_copy(
            shares[k], column.at[pl.ds((col_index ^ k) * share, share)], sems.at[k]
        )
        for k in range(col_count)
    ]
    for copy in copies:
        copy.start()
    held = jnp.dot(
        window[...], inverse_t[...], precision=HIGH, preferred_element_type=jnp.float32
    )
    for copy in copies:
        copy.wait()
    contract = (((1,), (1,)), ((), ()))

    def block(a, carry):
        rows = jnp.dot(
            column[a], inverse_t[...], precision=HIGH, preferred_element_type=jnp.float32
        )
        update = lax.dot_general(
            rows, held, contract, precision=HIGH, preferred_element_type=jnp.float32
        )
        below = a * 16 + row_index > 0
        update = jnp.where(below, update, jnp.zeros_like(update))
        even = pl.ds(a * 2 * size, size, stride=2)
        odd = pl.ds(a * 2 * size + 1, size, stride=2)
        base[even, :] = jnp.where(col_index == 0, rows, front[even, :] - update[:, :size])
        base[odd, :] = front[odd, :] - update[:, size:]
        return carry

    lax.fori_loop(0, row_blocks, block, 0)


def update_front(where, front, inverse_t, window, shares, row_blocks):
    size = front.shape[1]
    col_count = len(shares)
    share = row_blocks // col_count
    return pl.pallas_call(
        functools.partial(update_kernel, (row_blocks, share, col_count)),
        out_shape=jax.ShapeDtypeStruct(front.shape, jnp.float32),
        in_specs=[pl.BlockSpec(memory_space=SMEM)]
        + [pl.BlockSpec(memory_space=VMEM)] * 3
        + [pl.BlockSpec(memory_space=pl.ANY)] * col_count,
        out_specs=pl.BlockSpec(memory_space=VMEM),
        scratch_shapes=[
            VMEM((row_blocks, size, size), jnp.float32),
            pltpu.SemaphoreType.DMA((col_count,)),
        ],
        compiler_params=pltpu.CompilerParams(vmem_limit_bytes=40 << 20),
        name="update_front",
    )(where, front, inverse_t, window, *shares)


def add_kernel(per_step, message, base, tiles, out, sem):
    step = pl.program_id(0)

    @pl.when(step == 0)
    def _():
        copy = pltpu.make_async_copy(base, out, sem)
        copy.start()
        copy.wait()

    size = tiles.shape[1]

    def add(j, carry):
        slot = step * per_step + j
        place = message[slot // CAP * 2 * CAP + slot % CAP]

        @pl.when(place >= 0)
        def _():
            rows = pl.ds(place, size, stride=2)
            out[rows, :] += tiles[j]

        return carry

    lax.fori_loop(0, per_step, add, 0)


def add_tiles(message, base, tiles):
    slots, size = tiles.shape[:2]
    per_step = 32
    return pl.pallas_call(
        functools.partial(add_kernel, per_step),
        out_shape=jax.ShapeDtypeStruct(base.shape, jnp.float32),
        grid=(slots // per_step,),
        in_specs=[
            pl.BlockSpec(memory_space=SMEM),
            pl.BlockSpec(memory_space=pl.ANY),
            pl.BlockSpec((per_step, size, size), lambda i: (i, 0, 0)),
        ],
        out_specs=pl.BlockSpec(base.shape, lambda i: (0, 0)),
        scratch_shapes=[pltpu.SemaphoreType.DMA],
        compiler_params=pltpu.CompilerParams(vmem_limit_bytes=40 << 20),
        name="add_tiles",
    )(message, base, tiles)


def exchange(parts, axis):
    count = len(parts)
    return [parts[0]] + [
        lax.ppermute(parts[k], axis, [(i, i ^ k) for i in range(count)]) for k in range(1, count)
    ]


def per_device(front, child_tiles, child_rows, child_cols):
    row_count = lax.axis_size("row")
    col_count = lax.axis_size("col")
    row_index = lax.axis_index("row")
    col_index = lax.axis_index("col")
    row_blocks, size, col_blocks = (front.shape[0], front.shape[2], front.shape[3])
    share = row_blocks // col_count
    flat_front = front.reshape(row_blocks * size * col_blocks, size)
    tiles = child_tiles.reshape(-1, size, size)
    slots = row_count * col_count * CAP
    where = jnp.stack([row_index, col_index]).astype(jnp.int32)

    slot, panel_tiles, message = tables(
        child_rows.reshape(-1), child_cols.reshape(-1), row_index, row_count, col_count
    )
    both = ("row", "col")
    message = lax.all_to_all(message, both, split_axis=0, concat_axis=0, tiled=True).reshape(-1)
    send, panel_send = pack(slot, panel_tiles, tiles, slots, row_count)
    arrived = lax.all_to_all(send, both, split_axis=0, concat_axis=0, tiled=True)

    panel_arrived = exchange(panel_send, "row")
    parts = partial_column(
        where, message, flat_front, panel_arrived, row_count, col_count, row_blocks
    )
    summed = functools.reduce(jnp.add, exchange(parts, "col"))
    own_share, own_window = summed[1:], summed[0]
    shares = exchange([own_share] * col_count, "col")
    windows = jnp.stack(exchange([own_window] * row_count, "row"))
    corner = lax.dynamic_index_in_dim(windows, row_index, axis=0, keepdims=False)
    held = [
        lax.dynamic_index_in_dim(
            windows, row_index ^ (m * col_count + col_index), axis=0, keepdims=False
        )
        for m in range(col_blocks)
    ]
    factor = jnp.linalg.cholesky(0.5 * (corner + corner.T))
    inverse = jax.scipy.linalg.solve_triangular(
        factor, jnp.eye(size, dtype=jnp.float32), lower=True
    )
    base = update_front(
        where, flat_front, inverse.T, jnp.concatenate(held, axis=0), shares, row_blocks
    )
    return add_tiles(message, base, arrived).reshape(front.shape)


def solution(mesh):
    in_specs = (
        P(None, "row", None, None, "col", None),
        P("row", "col", None, None, None),
        P("row", "col", None),
        P("row", "col", None),
    )
    out_specs = P(None, "row", None, None, "col", None)
    return jax.shard_map(
        per_device, mesh=mesh, in_specs=in_specs, out_specs=out_specs, check_vma=False
    )
```

```python
import functools

import jax
import jax.numpy as jnp
from jax import lax
from jax.experimental import pallas as pl
from jax.experimental.pallas import tpu as pltpu
from jax.sharding import PartitionSpec as P

CAP = 2
HIGH = lax.Precision.HIGHEST
SMEM = pltpu.SMEM
VMEM = pltpu.VMEM
ANY = pl.ANY
LIMIT = pltpu.CompilerParams(vmem_limit_bytes=58 << 20)


def send_tables(parent_rows, parent_cols, row_count, col_count, size):
    tiles = parent_rows.shape[0]
    order = jnp.arange(tiles, dtype=jnp.int32)
    row_of = parent_rows % row_count
    owners = row_of * col_count + parent_cols % col_count
    same = (owners[:, None] == owners[None, :]) & (order[None, :] < order[:, None])
    slot = owners * CAP + jnp.sum(same.astype(jnp.int32), axis=1)
    place = parent_rows // row_count * (2 * size) + parent_cols // col_count
    wanted = jnp.arange(row_count * CAP, dtype=jnp.int32)[:, None]
    chosen = (parent_cols == 0) & (
        slot == wanted // CAP * (col_count * CAP) + wanted % CAP
    )
    panel_tiles = jnp.sum(jnp.where(chosen, order, 0), axis=1)
    return slot, place, panel_tiles


def arrival_tables(slots, places, row_index, col_index, col_count, size):
    panel = (slots // CAP % col_count == 0) & (places % (2 * size) == 0)
    mine = (row_index * col_count + col_index) * CAP
    base = row_index * col_count * CAP

    def pick(hit, value):
        return jnp.sum(jnp.where(hit, value + 1, 0), axis=1) - 1

    main = [pick((slots == mine + s) & ~panel, places) for s in range(CAP)]
    part = [pick((slots == base + s) & panel, places // (2 * size)) for s in range(CAP)]
    return main, part


def pack_kernel(chunks, slot, panel_tiles, tiles, first, second, held, load_sem, main_sem, panel_sem):
    count = tiles.shape[0]
    step = count // chunks
    row_count, col_count = first.shape[:2]

    def load(i):
        part = pl.ds(i * step, step)
        return pltpu.make_async_copy(tiles.at[part], held.at[part], load_sem.at[i])

    for i in range(chunks):
        load(i).start()
    for i in range(chunks):
        load(i).wait()

        def send(k, carry):
            where = slot[k]
            owner = where // CAP

            @pl.when(where % CAP == 0)
            def _():
                pltpu.make_async_copy(
                    held.at[k],
                    first.at[owner // col_count, owner % col_count, pl.ds(CAP, held.shape[1])],
                    main_sem,
                ).start()

            @pl.when(where % CAP == 1)
            def _():
                pltpu.make_async_copy(held.at[k], second.at[owner], main_sem).start()

            return carry

        lax.fori_loop(i * step, (i + 1) * step, send, 0)
    for r in range(row_count):
        for s in range(CAP):
            pltpu.make_async_copy(
                held.at[panel_tiles[r * CAP + s]], first.at[r, :, s], panel_sem
            ).start()
    pltpu.make_async_copy(held, second, main_sem).wait()
    some = pl.ds(0, row_count * CAP)
    pltpu.make_async_copy(held.at[some], second.at[some], panel_sem).wait()


def pack(slot, panel_tiles, tiles, row_count, col_count):
    count, parts, rows, size = tiles.shape
    chunks = 8
    return pl.pallas_call(
        functools.partial(pack_kernel, chunks),
        out_shape=[
            jax.ShapeDtypeStruct((row_count, col_count, CAP + parts, rows, size), jnp.float32),
            jax.ShapeDtypeStruct((row_count * col_count, parts, rows, size), jnp.float32),
        ],
        in_specs=[
            pl.BlockSpec(memory_space=SMEM),
            pl.BlockSpec(memory_space=SMEM),
            pl.BlockSpec(memory_space=ANY),
        ],
        out_specs=[pl.BlockSpec(memory_space=ANY)] * 2,
        scratch_shapes=[
            VMEM(tiles.shape, jnp.float32),
            pltpu.SemaphoreType.DMA((chunks,)),
            pltpu.SemaphoreType.DMA,
            pltpu.SemaphoreType.DMA,
        ],
        compiler_params=LIMIT,
        name="pack",
    )(slot, panel_tiles, tiles)


def split_kernel(rows, front, *outs):
    col_count = len(outs)

    def block(a, carry):
        for q in range(col_count):
            start = (a * col_count + q) * rows * 2
            outs[q][a] = front[pl.ds(start, rows, stride=2), :]
        return carry

    lax.fori_loop(0, outs[0].shape[0], block, 0)


def split_front(front, row_blocks, col_count):
    size = front.shape[1]
    rows = size // col_count
    return pl.pallas_call(
        functools.partial(split_kernel, rows),
        out_shape=[jax.ShapeDtypeStruct((row_blocks, rows, size), jnp.float32)] * col_count,
        compiler_params=LIMIT,
        name="split_front",
    )(front)


def slices_kernel(col_count, where, part_0, part_1, arrived, *refs):
    own = refs[:col_count]
    windows, column, total, sem = refs[col_count:]
    col_index = where[1]
    for k in range(col_count):

        @pl.when(col_index == k)
        def _():
            copy = pltpu.make_async_copy(own[k], total, sem)
            copy.start()
            copy.wait()

    parts = (part_0, part_1)

    def source(d, carry):
        for s in range(CAP):
            block = parts[s][d]

            @pl.when(block >= 0)
            def _():
                total[block] += arrived[d, s]

        return carry

    lax.fori_loop(0, arrived.shape[0], source, 0, unroll=4)
    for k in range(col_count):
        column[k] = total[...]
    windows[...] = jnp.broadcast_to(total[0][None], windows.shape)


def sum_slices(where, parts, arrived, own, row_count, col_count):
    devices, _, rows, size = arrived.shape
    row_blocks = own[0].shape[0]
    outs = [
        jax.ShapeDtypeStruct((devices, rows, size), jnp.float32),
        jax.ShapeDtypeStruct((col_count, row_blocks, rows, size), jnp.float32),
    ]
    return pl.pallas_call(
        functools.partial(slices_kernel, col_count),
        out_shape=outs,
        grid=(1,),
        in_specs=[pl.BlockSpec(memory_space=SMEM)] * 3
        + [pl.BlockSpec((devices, CAP, rows, size), lambda i: (0, 0, 0, 0))]
        + [pl.BlockSpec(memory_space=ANY)] * col_count,
        out_specs=[
            pl.BlockSpec(outs[0].shape, lambda i: (0, 0, 0)),
            pl.BlockSpec(outs[1].shape, lambda i: (0, 0, 0, 0)),
        ],
        scratch_shapes=[
            VMEM((row_blocks, rows, size), jnp.float32),
            pltpu.SemaphoreType.DMA,
        ],
        compiler_params=LIMIT,
        name="sum_slices",
    )(where, *parts, arrived, *own)


def add_kernel(per_step, skip, places, base, tiles, out, sem):
    step = pl.program_id(0)

    @pl.when(step == 0)
    def _():
        copy = pltpu.make_async_copy(base, out, sem)
        copy.start()
        copy.wait()

    parts, rows, size = tiles.shape[1:]

    def add(j, carry):
        place = places[step * per_step + j]

        @pl.when(place >= 0)
        def _():
            tile = tiles[j, pl.ds(skip, parts - skip)].reshape(size, size)
            out[pl.ds(place, size, stride=2), :] += tile

        return carry

    lax.fori_loop(0, per_step, add, 0)


def add_tiles(places, base, tiles, skip):
    slots, parts, rows, size = tiles.shape
    per_step = 16
    return pl.pallas_call(
        functools.partial(add_kernel, per_step, skip),
        out_shape=jax.ShapeDtypeStruct(base.shape, jnp.float32),
        grid=(slots // per_step,),
        in_specs=[
            pl.BlockSpec(memory_space=SMEM),
            pl.BlockSpec(memory_space=ANY),
            pl.BlockSpec((per_step, parts, rows, size), lambda i: (i, 0, 0, 0)),
        ],
        out_specs=pl.BlockSpec(base.shape, lambda i: (0, 0)),
        scratch_shapes=[pltpu.SemaphoreType.DMA],
        compiler_params=LIMIT,
        name="add_tiles",
    )(places, base, tiles)


def update_kernel(row_count, where, front, inverse_t, window, column, base):
    row_index, col_index = where[0], where[1]
    size = inverse_t.shape[0]
    held = jnp.dot(
        window[...], inverse_t[...], precision=HIGH, preferred_element_type=jnp.float32
    )
    contract = (((1,), (1,)), ((), ()))

    def block(a, carry):
        rows = jnp.dot(
            column[:, a].reshape(size, size),
            inverse_t[...],
            precision=HIGH,
            preferred_element_type=jnp.float32,
        )
        update = lax.dot_general(
            rows, held, contract, precision=HIGH, preferred_element_type=jnp.float32
        )
        below = a * row_count + row_index > 0
        update = jnp.where(below, update, jnp.zeros_like(update))
        even = pl.ds(a * 2 * size, size, stride=2)
        odd = pl.ds(a * 2 * size + 1, size, stride=2)
        base[even, :] = jnp.where(col_index == 0, rows, front[even, :] - update[:, :size])
        base[odd, :] = front[odd, :] - update[:, size:]
        return carry

    lax.fori_loop(0, column.shape[1], block, 0)


def update_front(where, front, inverse_t, window, column, row_count):
    return pl.pallas_call(
        functools.partial(update_kernel, row_count),
        out_shape=jax.ShapeDtypeStruct(front.shape, jnp.float32),
        in_specs=[pl.BlockSpec(memory_space=SMEM)] + [pl.BlockSpec(memory_space=VMEM)] * 4,
        out_specs=pl.BlockSpec(memory_space=VMEM),
        compiler_params=LIMIT,
        name="update_front",
    )(where, front, inverse_t, window, column)


def after_kernel(value, other, out):
    pass


def after(value, other):
    return pl.pallas_call(
        after_kernel,
        out_shape=jax.ShapeDtypeStruct(value.shape, value.dtype),
        in_specs=[pl.BlockSpec(memory_space=ANY)] * 2,
        out_specs=pl.BlockSpec(memory_space=ANY),
        input_output_aliases={0: 0},
        name="after",
    )(value, other)


def per_device(front, child_tiles, child_rows, child_cols):
    row_count = lax.axis_size("row")
    col_count = lax.axis_size("col")
    row_index = lax.axis_index("row")
    col_index = lax.axis_index("col")
    both = ("row", "col")
    row_blocks, size, col_blocks = (front.shape[0], front.shape[2], front.shape[3])
    rows = size // col_count
    devices = row_count * col_count
    flat_front = front.reshape(row_blocks * size * col_blocks, size)
    tiles = child_tiles.reshape(-1, col_count, rows, size)
    where = jnp.stack([row_index, col_index]).astype(jnp.int32)

    own = split_front(flat_front, row_blocks, col_count)
    own = [own[0]] + [lax.ppermute(own[k], "col", [(0, k)]) for k in range(1, col_count)]
    slot, place, panel_tiles = send_tables(
        child_rows.reshape(-1), child_cols.reshape(-1), row_count, col_count, size
    )
    gathered = lax.all_gather(jnp.stack([slot, place])[None], both, axis=0, tiled=True)
    first, second = pack(slot, panel_tiles, tiles, row_count, col_count)
    first = first.reshape((devices,) + first.shape[2:])
    arrived = lax.all_to_all(first, both, split_axis=0, concat_axis=0, tiled=True)
    main, part = arrival_tables(
        gathered[:, 0], gathered[:, 1], row_index, col_index, col_count, size
    )
    windows, column = sum_slices(where, part, arrived, own, row_count, col_count)
    windows = lax.all_to_all(windows, both, split_axis=0, concat_axis=0, tiled=True)
    windows = windows.reshape(row_count, size, size)
    column = lax.all_to_all(column, "col", split_axis=0, concat_axis=0, tiled=True)
    second = lax.all_to_all(
        after(second, column), both, split_axis=0, concat_axis=0, tiled=True
    )
    corner = windows[0]
    window = jnp.concatenate(
        [
            lax.dynamic_index_in_dim(windows, m * col_count + col_index, axis=0, keepdims=False)
            for m in range(col_blocks)
        ],
        axis=0,
    )
    factor = jnp.linalg.cholesky(0.5 * (corner + corner.T))
    inverse = jax.scipy.linalg.solve_triangular(
        factor, jnp.eye(size, dtype=jnp.float32), lower=True
    )
    total = add_tiles(main[0], flat_front, arrived, CAP)
    base = update_front(where, total, inverse.T, window, column, row_count)
    return add_tiles(main[1], base, second, 0).reshape(front.shape)


def solution(mesh):
    in_specs = (
        P(None, "row", None, None, "col", None),
        P("row", "col", None, None, None),
        P("row", "col", None),
        P("row", "col", None),
    )
    out_specs = P(None, "row", None, None, "col", None)
    return jax.shard_map(
        per_device, mesh=mesh, in_specs=in_specs, out_specs=out_specs, check_vma=False
    )
```

```python
import functools

import jax
import jax.numpy as jnp
from jax import lax
from jax.experimental import pallas as pl
from jax.experimental.pallas import tpu as pltpu
from jax.sharding import PartitionSpec as P

CAP = 2
HIGH = lax.Precision.HIGHEST
SMEM = pltpu.SMEM
VMEM = pltpu.VMEM
ANY = pl.ANY
LIMIT = pltpu.CompilerParams(vmem_limit_bytes=58 << 20)


def send_tables(parent_rows, parent_cols, row_count, col_count, size):
    tiles = parent_rows.shape[0]
    order = jnp.arange(tiles, dtype=jnp.int32)
    row_of = parent_rows % row_count
    owners = row_of * col_count + parent_cols % col_count
    same = (owners[:, None] == owners[None, :]) & (order[None, :] < order[:, None])
    slot = owners * CAP + jnp.sum(same.astype(jnp.int32), axis=1)
    block = parent_rows // row_count
    place = block * (2 * size) + parent_cols // col_count
    panel = parent_cols == 0
    wanted = jnp.arange(row_count * CAP, dtype=jnp.int32)[:, None]
    chosen = panel & (slot == wanted // CAP * (col_count * CAP) + wanted % CAP)
    panel_tiles = jnp.sum(jnp.where(chosen, order, 0), axis=1)
    dest = jnp.arange(row_count * col_count, dtype=jnp.int32)[:, None, None]
    part = jnp.arange(2 * CAP, dtype=jnp.int32)[None, :, None]
    in_main = (part < CAP) & (slot == dest * CAP + part) & ~panel
    first = dest // col_count * (col_count * CAP)
    in_panel = (part >= CAP) & (slot == first + part - CAP) & panel
    value = jnp.where(in_main, place + 1, 0) + jnp.where(in_panel, block + 1, 0)
    return slot, panel_tiles, jnp.sum(value, axis=2) - 1


def pack_kernel(chunks, slot, panel_tiles, tiles, first, second, held, load_sem, main_sem, panel_sem):
    count = tiles.shape[0]
    step = count // chunks
    row_count, col_count = first.shape[:2]

    def load(i):
        part = pl.ds(i * step, step)
        return pltpu.make_async_copy(tiles.at[part], held.at[part], load_sem.at[i])

    for i in range(chunks):
        load(i).start()
    for i in range(chunks):
        load(i).wait()

        def send(k, carry):
            where = slot[k]
            owner = where // CAP

            @pl.when(where % CAP == 0)
            def _():
                pltpu.make_async_copy(
                    held.at[k],
                    first.at[owner // col_count, owner % col_count, pl.ds(CAP, held.shape[1])],
                    main_sem,
                ).start()

            @pl.when(where % CAP == 1)
            def _():
                pltpu.make_async_copy(held.at[k], second.at[owner], main_sem).start()

            return carry

        lax.fori_loop(i * step, (i + 1) * step, send, 0)
    for r in range(row_count):
        for s in range(CAP):
            pltpu.make_async_copy(
                held.at[panel_tiles[r * CAP + s]], first.at[r, :, s], panel_sem
            ).start()
    pltpu.make_async_copy(held, second, main_sem).wait()
    some = pl.ds(0, row_count * CAP)
    pltpu.make_async_copy(held.at[some], second.at[some], panel_sem).wait()


def pack(slot, panel_tiles, tiles, row_count, col_count):
    count, parts, rows, size = tiles.shape
    chunks = 8
    return pl.pallas_call(
        functools.partial(pack_kernel, chunks),
        out_shape=[
            jax.ShapeDtypeStruct((row_count, col_count, CAP + parts, rows, size), jnp.float32),
            jax.ShapeDtypeStruct((row_count * col_count, parts, rows, size), jnp.float32),
        ],
        in_specs=[
            pl.BlockSpec(memory_space=SMEM),
            pl.BlockSpec(memory_space=SMEM),
            pl.BlockSpec(memory_space=ANY),
        ],
        out_specs=[pl.BlockSpec(memory_space=ANY)] * 2,
        scratch_shapes=[
            VMEM(tiles.shape, jnp.float32),
            pltpu.SemaphoreType.DMA((chunks,)),
            pltpu.SemaphoreType.DMA,
            pltpu.SemaphoreType.DMA,
        ],
        compiler_params=LIMIT,
        name="pack",
    )(slot, panel_tiles, tiles)


def split_kernel(rows, front, *outs):
    col_count = len(outs)

    def block(a, carry):
        for q in range(col_count):
            start = (a * col_count + q) * rows * 2
            outs[q][a] = front[pl.ds(start, rows, stride=2), :]
        return carry

    lax.fori_loop(0, outs[0].shape[0], block, 0)


def split_front(front, row_blocks, col_count):
    size = front.shape[1]
    rows = size // col_count
    return pl.pallas_call(
        functools.partial(split_kernel, rows),
        out_shape=[jax.ShapeDtypeStruct((row_blocks, rows, size), jnp.float32)] * col_count,
        compiler_params=LIMIT,
        name="split_front",
    )(front)


def slices_kernel(col_count, where, part_0, part_1, arrived, *refs):
    own = refs[:col_count]
    windows, column, total, sem = refs[col_count:]
    col_index = where[1]
    for k in range(col_count):

        @pl.when(col_index == k)
        def _():
            copy = pltpu.make_async_copy(own[k], total, sem)
            copy.start()
            copy.wait()

    parts = (part_0, part_1)

    def source(d, carry):
        for s in range(CAP):
            block = parts[s][d]

            @pl.when(block >= 0)
            def _():
                total[block] += arrived[d, s]

        return carry

    lax.fori_loop(0, arrived.shape[0], source, 0, unroll=4)
    for k in range(col_count):
        column[k] = total[...]
    windows[...] = jnp.broadcast_to(total[0][None], windows.shape)


def sum_slices(where, parts, arrived, own, row_count, col_count):
    devices, _, rows, size = arrived.shape
    row_blocks = own[0].shape[0]
    outs = [
        jax.ShapeDtypeStruct((devices, rows, size), jnp.float32),
        jax.ShapeDtypeStruct((col_count, row_blocks, rows, size), jnp.float32),
    ]
    return pl.pallas_call(
        functools.partial(slices_kernel, col_count),
        out_shape=outs,
        grid=(1,),
        in_specs=[pl.BlockSpec(memory_space=SMEM)] * 3
        + [pl.BlockSpec((devices, CAP, rows, size), lambda i: (0, 0, 0, 0))]
        + [pl.BlockSpec(memory_space=ANY)] * col_count,
        out_specs=[
            pl.BlockSpec(outs[0].shape, lambda i: (0, 0, 0)),
            pl.BlockSpec(outs[1].shape, lambda i: (0, 0, 0, 0)),
        ],
        scratch_shapes=[
            VMEM((row_blocks, rows, size), jnp.float32),
            pltpu.SemaphoreType.DMA,
        ],
        compiler_params=LIMIT,
        name="sum_slices",
    )(where, *parts, arrived, *own)


def add_kernel(per_step, skip, places, base, tiles, out, sem):
    step = pl.program_id(0)

    @pl.when(step == 0)
    def _():
        copy = pltpu.make_async_copy(base, out, sem)
        copy.start()
        copy.wait()

    parts, rows, size = tiles.shape[1:]

    def add(j, carry):
        place = places[step * per_step + j]

        @pl.when(place >= 0)
        def _():
            tile = tiles[j, pl.ds(skip, parts - skip)].reshape(size, size)
            out[pl.ds(place, size, stride=2), :] += tile

        return carry

    lax.fori_loop(0, per_step, add, 0)


def add_tiles(places, base, tiles, skip):
    slots, parts, rows, size = tiles.shape
    per_step = 16
    return pl.pallas_call(
        functools.partial(add_kernel, per_step, skip),
        out_shape=jax.ShapeDtypeStruct(base.shape, jnp.float32),
        grid=(slots // per_step,),
        in_specs=[
            pl.BlockSpec(memory_space=SMEM),
            pl.BlockSpec(memory_space=ANY),
            pl.BlockSpec((per_step, parts, rows, size), lambda i: (i, 0, 0, 0)),
        ],
        out_specs=pl.BlockSpec(base.shape, lambda i: (0, 0)),
        scratch_shapes=[pltpu.SemaphoreType.DMA],
        compiler_params=LIMIT,
        name="add_tiles",
    )(places, base, tiles)


def update_kernel(row_count, where, front, inverse_t, window, column, base):
    row_index, col_index = where[0], where[1]
    size = inverse_t.shape[0]
    held = jnp.dot(
        window[...], inverse_t[...], precision=HIGH, preferred_element_type=jnp.float32
    )
    contract = (((1,), (1,)), ((), ()))

    def block(a, carry):
        rows = jnp.dot(
            column[:, a].reshape(size, size),
            inverse_t[...],
            precision=HIGH,
            preferred_element_type=jnp.float32,
        )
        update = lax.dot_general(
            rows, held, contract, precision=HIGH, preferred_element_type=jnp.float32
        )
        below = a * row_count + row_index > 0
        update = jnp.where(below, update, jnp.zeros_like(update))
        even = pl.ds(a * 2 * size, size, stride=2)
        odd = pl.ds(a * 2 * size + 1, size, stride=2)
        base[even, :] = jnp.where(col_index == 0, rows, front[even, :] - update[:, :size])
        base[odd, :] = front[odd, :] - update[:, size:]
        return carry

    lax.fori_loop(0, column.shape[1], block, 0)


def update_front(where, front, inverse_t, window, column, row_count):
    return pl.pallas_call(
        functools.partial(update_kernel, row_count),
        out_shape=jax.ShapeDtypeStruct(front.shape, jnp.float32),
        in_specs=[pl.BlockSpec(memory_space=SMEM)] + [pl.BlockSpec(memory_space=VMEM)] * 4,
        out_specs=pl.BlockSpec(memory_space=VMEM),
        compiler_params=LIMIT,
        name="update_front",
    )(where, front, inverse_t, window, column)


def after_kernel(value, other, out):
    pass


def after(value, other):
    return pl.pallas_call(
        after_kernel,
        out_shape=jax.ShapeDtypeStruct(value.shape, value.dtype),
        in_specs=[pl.BlockSpec(memory_space=ANY)] * 2,
        out_specs=pl.BlockSpec(memory_space=ANY),
        input_output_aliases={0: 0},
        name="after",
    )(value, other)


def per_device(front, child_tiles, child_rows, child_cols):
    row_count = lax.axis_size("row")
    col_count = lax.axis_size("col")
    row_index = lax.axis_index("row")
    col_index = lax.axis_index("col")
    both = ("row", "col")
    row_blocks, size, col_blocks = (front.shape[0], front.shape[2], front.shape[3])
    rows = size // col_count
    devices = row_count * col_count
    flat_front = front.reshape(row_blocks * size * col_blocks, size)
    tiles = child_tiles.reshape(-1, col_count, rows, size)
    where = jnp.stack([row_index, col_index]).astype(jnp.int32)

    own = split_front(flat_front, row_blocks, col_count)
    own = [own[0]] + [lax.ppermute(own[k], "col", [(0, k)]) for k in range(1, col_count)]
    slot, panel_tiles, message = send_tables(
        child_rows.reshape(-1), child_cols.reshape(-1), row_count, col_count, size
    )
    message = lax.all_to_all(message, both, split_axis=0, concat_axis=0, tiled=True)
    main, part = ([message[:, h * CAP + s] for s in range(CAP)] for h in range(2))
    first, second = pack(slot, panel_tiles, tiles, row_count, col_count)
    first = first.reshape((devices,) + first.shape[2:])
    arrived = lax.all_to_all(first, both, split_axis=0, concat_axis=0, tiled=True)
    windows, column = sum_slices(where, part, arrived, own, row_count, col_count)
    windows = lax.all_to_all(windows, both, split_axis=0, concat_axis=0, tiled=True)
    windows = windows.reshape(row_count, size, size)
    column = lax.all_to_all(column, "col", split_axis=0, concat_axis=0, tiled=True)
    second = lax.all_to_all(
        after(second, column), both, split_axis=0, concat_axis=0, tiled=True
    )
    corner = windows[0]
    window = jnp.concatenate(
        [
            lax.dynamic_index_in_dim(windows, m * col_count + col_index, axis=0, keepdims=False)
            for m in range(col_blocks)
        ],
        axis=0,
    )
    factor = jnp.linalg.cholesky(0.5 * (corner + corner.T))
    inverse = jax.scipy.linalg.solve_triangular(
        factor, jnp.eye(size, dtype=jnp.float32), lower=True
    )
    total = add_tiles(main[0], flat_front, arrived, CAP)
    base = update_front(where, total, inverse.T, window, column, row_count)
    return add_tiles(main[1], base, second, 0).reshape(front.shape)


def solution(mesh):
    in_specs = (
        P(None, "row", None, None, "col", None),
        P("row", "col", None, None, None),
        P("row", "col", None),
        P("row", "col", None),
    )
    out_specs = P(None, "row", None, None, "col", None)
    return jax.shard_map(
        per_device, mesh=mesh, in_specs=in_specs, out_specs=out_specs, check_vma=False
    )
```

```python
import functools

import jax
import jax.numpy as jnp
from jax import lax
from jax.experimental import pallas as pl
from jax.experimental.pallas import tpu as pltpu
from jax.sharding import PartitionSpec as P

CAP = 2
HIGH = lax.Precision.HIGHEST
SMEM = pltpu.SMEM
VMEM = pltpu.VMEM
ANY = pl.ANY
LIMIT = pltpu.CompilerParams(vmem_limit_bytes=58 << 20)


def send_tables(parent_rows, parent_cols, row_count, col_count, size):
    tiles = parent_rows.shape[0]
    order = jnp.arange(tiles, dtype=jnp.int32)
    row_of = parent_rows % row_count
    owners = row_of * col_count + parent_cols % col_count
    same = (owners[:, None] == owners[None, :]) & (order[None, :] < order[:, None])
    slot = owners * CAP + jnp.sum(same.astype(jnp.int32), axis=1)
    block = parent_rows // row_count
    place = block * (2 * size) + parent_cols // col_count
    panel = parent_cols == 0
    wanted = jnp.arange(row_count * CAP, dtype=jnp.int32)[:, None]
    chosen = panel & (slot == wanted // CAP * (col_count * CAP) + wanted % CAP)
    panel_tiles = jnp.sum(jnp.where(chosen, order, 0), axis=1)
    dest = jnp.arange(row_count * col_count, dtype=jnp.int32)[:, None, None]
    part = jnp.arange(2 * CAP, dtype=jnp.int32)[None, :, None]
    in_main = (part < CAP) & (slot == dest * CAP + part) & ~panel
    first = dest // col_count * (col_count * CAP)
    in_panel = (part >= CAP) & (slot == first + part - CAP) & panel
    value = jnp.where(in_main, place + 1, 0) + jnp.where(in_panel, block + 1, 0)
    return slot, panel_tiles, jnp.sum(value, axis=2) - 1


def pack_kernel(chunks, slot, panel_tiles, tiles, first, second, held, load_sem, main_sem, panel_sem):
    count = tiles.shape[0]
    step = count // chunks
    row_count, col_count = first.shape[:2]

    def load(i):
        part = pl.ds(i * step, step)
        return pltpu.make_async_copy(tiles.at[part], held.at[part], load_sem.at[i])

    for i in range(chunks):
        load(i).start()
    for i in range(chunks):
        load(i).wait()

        def send(k, carry):
            where = slot[k]
            owner = where // CAP

            @pl.when(where % CAP == 0)
            def _():
                pltpu.make_async_copy(
                    held.at[k],
                    first.at[owner // col_count, owner % col_count, pl.ds(CAP, held.shape[1])],
                    main_sem,
                ).start()

            @pl.when(where % CAP == 1)
            def _():
                pltpu.make_async_copy(held.at[k], second.at[owner], main_sem).start()

            return carry

        lax.fori_loop(i * step, (i + 1) * step, send, 0)
    for r in range(row_count):
        for s in range(CAP):
            pltpu.make_async_copy(
                held.at[panel_tiles[r * CAP + s]], first.at[r, :, s], panel_sem
            ).start()
    pltpu.make_async_copy(held, second, main_sem).wait()
    some = pl.ds(0, row_count * CAP)
    pltpu.make_async_copy(held.at[some], second.at[some], panel_sem).wait()


def pack(slot, panel_tiles, tiles, row_count, col_count):
    count, parts, rows, size = tiles.shape
    chunks = 8
    return pl.pallas_call(
        functools.partial(pack_kernel, chunks),
        out_shape=[
            jax.ShapeDtypeStruct((row_count, col_count, CAP + parts, rows, size), jnp.float32),
            jax.ShapeDtypeStruct((row_count * col_count, parts, rows, size), jnp.float32),
        ],
        in_specs=[
            pl.BlockSpec(memory_space=SMEM),
            pl.BlockSpec(memory_space=SMEM),
            pl.BlockSpec(memory_space=ANY),
        ],
        out_specs=[pl.BlockSpec(memory_space=ANY)] * 2,
        scratch_shapes=[
            VMEM(tiles.shape, jnp.float32),
            pltpu.SemaphoreType.DMA((chunks,)),
            pltpu.SemaphoreType.DMA,
            pltpu.SemaphoreType.DMA,
        ],
        compiler_params=LIMIT,
        name="pack",
    )(slot, panel_tiles, tiles)


def split_kernel(rows, front, *outs):
    col_count = len(outs)

    def block(a, carry):
        for q in range(col_count):
            start = (a * col_count + q) * rows * 2
            outs[q][a] = front[pl.ds(start, rows, stride=2), :]
        return carry

    lax.fori_loop(0, outs[0].shape[0], block, 0, unroll=True)


def split_front(front, row_blocks, col_count):
    size = front.shape[1]
    rows = size // col_count
    steps = 6
    return pl.pallas_call(
        functools.partial(split_kernel, rows),
        out_shape=[jax.ShapeDtypeStruct((row_blocks, rows, size), jnp.float32)] * col_count,
        grid=(steps,),
        in_specs=[pl.BlockSpec((front.shape[0] // steps, size), lambda i: (i, 0))],
        out_specs=[pl.BlockSpec((row_blocks // steps, rows, size), lambda i: (i, 0, 0))]
        * col_count,
        compiler_params=LIMIT,
        name="split_front",
    )(front)


def slices_kernel(col_count, where, part_0, part_1, arrived, *refs):
    own = refs[:col_count]
    windows, column, total, sem = refs[col_count:]
    row_blocks = own[0].shape[0]
    blocks = pl.ds(0, row_blocks)
    col_index = where[1]
    for k in range(col_count):

        @pl.when(col_index == k)
        def _():
            copy = pltpu.make_async_copy(own[k], total.at[blocks], sem)
            copy.start()
            copy.wait()

    parts = (part_0, part_1)

    def source(d, carry):
        for s in range(CAP):
            block = parts[s][d]
            total[jnp.where(block < 0, row_blocks, block)] += arrived[d, s]
        return carry

    lax.fori_loop(0, arrived.shape[0], source, 0, unroll=8)
    for k in range(col_count):
        column[k, blocks] = total[blocks]
    windows[...] = jnp.broadcast_to(total[0][None], windows.shape)


def sum_slices(where, parts, arrived, own, row_count, col_count, extra):
    devices, _, rows, size = arrived.shape
    row_blocks = own[0].shape[0]
    outs = [
        jax.ShapeDtypeStruct((row_count, rows, size), jnp.float32),
        jax.ShapeDtypeStruct((col_count, row_blocks + extra, rows, size), jnp.float32),
    ]
    return pl.pallas_call(
        functools.partial(slices_kernel, col_count),
        out_shape=outs,
        grid=(1,),
        in_specs=[pl.BlockSpec(memory_space=SMEM)] * 3
        + [pl.BlockSpec((devices, CAP, rows, size), lambda i: (0, 0, 0, 0))]
        + [pl.BlockSpec(memory_space=ANY)] * col_count,
        out_specs=[
            pl.BlockSpec(outs[0].shape, lambda i: (0, 0, 0)),
            pl.BlockSpec(outs[1].shape, lambda i: (0, 0, 0, 0)),
        ],
        scratch_shapes=[
            VMEM((row_blocks + 1, rows, size), jnp.float32),
            pltpu.SemaphoreType.DMA,
        ],
        compiler_params=LIMIT,
        name="sum_slices",
    )(where, *parts, arrived, *own)


def windows_kernel(row_blocks, windows, column, out, sem):
    col_count = column.shape[0]
    copies = []
    for k in range(col_count):
        for i, j in enumerate((0, *range(k, windows.shape[0], col_count))):
            copies.append(
                pltpu.make_async_copy(
                    windows.at[j], out.at[k, row_blocks + i], sem.at[len(copies)]
                )
            )
    for copy in copies:
        copy.start()
    for copy in copies:
        copy.wait()


def add_windows(windows, column, row_blocks):
    count = column.shape[0] * (column.shape[1] - row_blocks)
    return pl.pallas_call(
        functools.partial(windows_kernel, row_blocks),
        out_shape=jax.ShapeDtypeStruct(column.shape, column.dtype),
        in_specs=[pl.BlockSpec(memory_space=VMEM), pl.BlockSpec(memory_space=ANY)],
        out_specs=pl.BlockSpec(memory_space=ANY),
        input_output_aliases={1: 0},
        scratch_shapes=[pltpu.SemaphoreType.DMA((count,))],
        compiler_params=LIMIT,
        name="add_windows",
    )(windows, column)


def add_kernel(chunks, places, base, tiles, out, total, held, base_sem, tile_sem):
    slots, parts, rows, size = held.shape
    step = slots // chunks
    last = base.shape[0]
    whole = pl.ds(0, last)
    load_base = pltpu.make_async_copy(base, total.at[whole], base_sem)
    load_base.start()

    def load(i):
        some = pl.ds(i * step, step)
        skip = pl.ds(tiles.shape[1] - parts, parts)
        return pltpu.make_async_copy(tiles.at[some, skip], held.at[some], tile_sem.at[i])

    for i in range(chunks):
        load(i).start()
    load_base.wait()

    def add(j, carry):
        place = places[j]
        start = jnp.where(place < 0, last, place)
        total[pl.ds(start, size, stride=2), :] += held[j].reshape(size, size)
        return carry

    for i in range(chunks):
        load(i).wait()
        lax.fori_loop(i * step, (i + 1) * step, add, 0, unroll=4)
    store = pltpu.make_async_copy(total.at[whole], out, base_sem)
    store.start()
    store.wait()


def add_tiles(places, base, tiles, skip):
    slots, parts, rows, size = tiles.shape
    chunks = 8
    return pl.pallas_call(
        functools.partial(add_kernel, chunks),
        out_shape=jax.ShapeDtypeStruct(base.shape, jnp.float32),
        in_specs=[
            pl.BlockSpec(memory_space=SMEM),
            pl.BlockSpec(memory_space=ANY),
            pl.BlockSpec(memory_space=ANY),
        ],
        out_specs=pl.BlockSpec(memory_space=ANY),
        scratch_shapes=[
            VMEM((base.shape[0] + 2 * size, size), jnp.float32),
            VMEM((slots, parts - skip, rows, size), jnp.float32),
            pltpu.SemaphoreType.DMA,
            pltpu.SemaphoreType.DMA((chunks,)),
        ],
        compiler_params=LIMIT,
        name="add_tiles",
    )(places, base, tiles)


def update_kernel(shape, where, front, inverse_t, window, column, base):
    row_count, row_blocks = shape
    row_index, col_index = where[0], where[1]
    size = inverse_t.shape[0]
    held = jnp.dot(
        window[...], inverse_t[...], precision=HIGH, preferred_element_type=jnp.float32
    )
    contract = (((1,), (1,)), ((), ()))

    def block(a, carry):
        rows = jnp.dot(
            column[:, a].reshape(size, size),
            inverse_t[...],
            precision=HIGH,
            preferred_element_type=jnp.float32,
        )
        update = lax.dot_general(
            rows, held, contract, precision=HIGH, preferred_element_type=jnp.float32
        )
        below = a * row_count + row_index > 0
        update = jnp.where(below, update, jnp.zeros_like(update))
        even = pl.ds(a * 2 * size, size, stride=2)
        odd = pl.ds(a * 2 * size + 1, size, stride=2)
        base[even, :] = jnp.where(col_index == 0, rows, front[even, :] - update[:, :size])
        base[odd, :] = front[odd, :] - update[:, size:]
        return carry

    lax.fori_loop(0, row_blocks, block, 0)


def update_front(where, front, inverse_t, window, column, row_count, row_blocks):
    return pl.pallas_call(
        functools.partial(update_kernel, (row_count, row_blocks)),
        out_shape=jax.ShapeDtypeStruct(front.shape, jnp.float32),
        in_specs=[pl.BlockSpec(memory_space=SMEM)] + [pl.BlockSpec(memory_space=VMEM)] * 4,
        out_specs=pl.BlockSpec(memory_space=VMEM),
        compiler_params=LIMIT,
        name="update_front",
    )(where, front, inverse_t, window, column)


def after_kernel(*refs):
    pass


def after(value, *others):
    return pl.pallas_call(
        after_kernel,
        out_shape=jax.ShapeDtypeStruct(value.shape, value.dtype),
        in_specs=[pl.BlockSpec(memory_space=ANY)] * (1 + len(others)),
        out_specs=pl.BlockSpec(memory_space=ANY),
        input_output_aliases={0: 0},
        name="after",
    )(value, *others)


def per_device(front, child_tiles, child_rows, child_cols):
    row_count = lax.axis_size("row")
    col_count = lax.axis_size("col")
    row_index = lax.axis_index("row")
    col_index = lax.axis_index("col")
    both = ("row", "col")
    row_blocks, size, col_blocks = (front.shape[0], front.shape[2], front.shape[3])
    rows = size // col_count
    devices = row_count * col_count
    flat_front = front.reshape(row_blocks * size * col_blocks, size)
    tiles = child_tiles.reshape(-1, col_count, rows, size)
    where = jnp.stack([row_index, col_index]).astype(jnp.int32)

    own = split_front(flat_front, row_blocks, col_count)
    own = [own[0]] + [lax.ppermute(own[k], "col", [(0, k)]) for k in range(1, col_count)]
    slot, panel_tiles, message = send_tables(
        child_rows.reshape(-1), child_cols.reshape(-1), row_count, col_count, size
    )
    message = lax.all_to_all(message, both, split_axis=0, concat_axis=0, tiled=True)
    main, part = ([message[:, h * CAP + s] for s in range(CAP)] for h in range(2))
    first, second = pack(slot, panel_tiles, tiles, row_count, col_count)
    first = first.reshape((devices,) + first.shape[2:])
    first = after(first, *own[1:])
    arrived = lax.all_to_all(first, both, split_axis=0, concat_axis=0, tiled=True)
    windows, column = sum_slices(
        where, part, arrived, own, row_count, col_count, 1 + col_blocks
    )
    windows = lax.all_to_all(windows, "row", split_axis=0, concat_axis=0, tiled=True)
    column = add_windows(windows, column, row_blocks)
    column = lax.all_to_all(column, "col", split_axis=0, concat_axis=0, tiled=True)
    second = lax.all_to_all(
        after(second, column), both, split_axis=0, concat_axis=0, tiled=True
    )
    corner = column[:, row_blocks].reshape(size, size)
    window = jnp.swapaxes(column[:, row_blocks + 1 :], 0, 1).reshape(-1, size)
    factor = jnp.linalg.cholesky(0.5 * (corner + corner.T))
    inverse = jax.scipy.linalg.solve_triangular(
        factor, jnp.eye(size, dtype=jnp.float32), lower=True
    )
    total = add_tiles(main[0], flat_front, arrived, CAP)
    base = update_front(where, total, inverse.T, window, column, row_count, row_blocks)
    return add_tiles(main[1], base, second, 0).reshape(front.shape)


def solution(mesh):
    in_specs = (
        P(None, "row", None, None, "col", None),
        P("row", "col", None, None, None),
        P("row", "col", None),
        P("row", "col", None),
    )
    out_specs = P(None, "row", None, None, "col", None)
    return jax.shard_map(
        per_device, mesh=mesh, in_specs=in_specs, out_specs=out_specs, check_vma=False
    )
```

```python
import functools

import jax
import jax.numpy as jnp
from jax import lax
from jax.experimental import pallas as pl
from jax.experimental.pallas import tpu as pltpu
from jax.sharding import PartitionSpec as P

CAP = 2
HIGH = lax.Precision.HIGHEST
SMEM = pltpu.SMEM
VMEM = pltpu.VMEM
ANY = pl.ANY
LIMIT = pltpu.CompilerParams(vmem_limit_bytes=58 << 20)


def send_tables(parent_rows, parent_cols, row_index, col_index, row_count, col_count, size):
    tiles = parent_rows.shape[0]
    order = jnp.arange(tiles, dtype=jnp.int32)
    row_of = parent_rows % row_count
    owners = row_of * col_count + parent_cols % col_count
    same = (owners[:, None] == owners[None, :]) & (order[None, :] < order[:, None])
    slot = owners * CAP + jnp.sum(same.astype(jnp.int32), axis=1)
    block = parent_rows // row_count
    place = block * (2 * size) + parent_cols // col_count
    panel = parent_cols == 0
    wanted = jnp.arange(row_count * CAP, dtype=jnp.int32)[:, None]
    chosen = panel & (slot == wanted // CAP * (col_count * CAP) + wanted % CAP)
    panel_tiles = jnp.sum(jnp.where(chosen, order, 0), axis=1)
    dest = jnp.arange(row_count * col_count, dtype=jnp.int32)[:, None, None]
    part = jnp.arange(2 * CAP, dtype=jnp.int32)[None, :, None]
    in_main = (part < CAP) & (slot == dest * CAP + part) & ~panel
    dest_row = dest // col_count
    local = (dest_row == row_index) & (col_index == 0)
    in_panel = (part >= CAP) & (slot == dest_row * (col_count * CAP) + part - CAP) & panel
    value = jnp.where(in_main, place + 1, 0) + jnp.where(in_panel & ~local, block + 1, 0)
    message = jnp.sum(value, axis=2) - 1
    message = jnp.where(local[..., 0] & (part[..., 0] == CAP), 0, message)
    mine = jnp.arange(CAP, dtype=jnp.int32)[:, None]
    stays = panel & (col_index == 0) & (slot == row_index * (col_count * CAP) + mine)
    stay_tiles = jnp.sum(jnp.where(stays, order, 0), axis=1)
    stay_blocks = jnp.sum(jnp.where(stays, block + 1, 0), axis=1) - 1
    where = jnp.stack([row_index, col_index]).astype(jnp.int32)
    return slot, panel_tiles, message, jnp.concatenate([where, stay_tiles, stay_blocks])


def pack_kernel(chunks, slot, panel_tiles, local, tiles, front, first, second, *scratch):
    held, corner, block, load_sem, main_sem, panel_sem, corner_sem = scratch
    count, parts, rows, size = tiles.shape
    step = count // chunks
    row_count, col_count = first.shape[:2]
    row_index, col_index = local[0], local[1]

    def load(i):
        part = pl.ds(i * step, step)
        return pltpu.make_async_copy(tiles.at[part], held.at[part], load_sem.at[i])

    load_corner = pltpu.make_async_copy(front.at[pl.ds(0, 2 * parts * rows)], corner, corner_sem)
    for i in range(chunks):
        load(i).start()
    load_corner.start()
    for i in range(chunks):
        load(i).wait()

        def send(k, carry):
            where = slot[k]
            owner = where // CAP

            @pl.when(where % CAP == 0)
            def _():
                pltpu.make_async_copy(
                    held.at[k],
                    first.at[owner // col_count, owner % col_count, pl.ds(CAP, parts)],
                    main_sem,
                ).start()

            @pl.when(where % CAP == 1)
            def _():
                pltpu.make_async_copy(held.at[k], second.at[owner], main_sem).start()

            return carry

        lax.fori_loop(i * step, (i + 1) * step, send, 0)
    load_corner.wait()
    block[...] = corner[pl.ds(0, parts * rows, stride=2), :].reshape(block.shape)
    for s in range(CAP):

        @pl.when(local[2 + CAP + s] == 0)
        def _():
            block[...] += held[local[2 + s]]

    for r in range(row_count):
        for s in range(CAP):
            own = (row_index == r) & (col_index == 0) & (s == 0)

            @pl.when(own)
            def _():
                pltpu.make_async_copy(block, first.at[r, :, s], panel_sem).start()

            @pl.when(jnp.logical_not(own))
            def _():
                pltpu.make_async_copy(
                    held.at[panel_tiles[r * CAP + s]], first.at[r, :, s], panel_sem
                ).start()

    pltpu.make_async_copy(held, second, main_sem).wait()
    some = pl.ds(0, row_count * CAP)
    pltpu.make_async_copy(held.at[some], second.at[some], panel_sem).wait()


def pack(slot, panel_tiles, local, tiles, front, row_count, col_count):
    count, parts, rows, size = tiles.shape
    chunks = 8
    return pl.pallas_call(
        functools.partial(pack_kernel, chunks),
        out_shape=[
            jax.ShapeDtypeStruct((row_count, col_count, CAP + parts, rows, size), jnp.float32),
            jax.ShapeDtypeStruct((row_count * col_count, parts, rows, size), jnp.float32),
        ],
        in_specs=[pl.BlockSpec(memory_space=SMEM)] * 3 + [pl.BlockSpec(memory_space=ANY)] * 2,
        out_specs=[pl.BlockSpec(memory_space=ANY)] * 2,
        scratch_shapes=[
            VMEM(tiles.shape, jnp.float32),
            VMEM((2 * parts * rows, size), jnp.float32),
            VMEM((parts, rows, size), jnp.float32),
            pltpu.SemaphoreType.DMA((chunks,)),
            pltpu.SemaphoreType.DMA,
            pltpu.SemaphoreType.DMA,
            pltpu.SemaphoreType.DMA,
        ],
        compiler_params=LIMIT,
        name="pack",
    )(slot, panel_tiles, local, tiles, front)


def split_kernel(rows, local, front, tiles, *refs):
    outs, (held, sem) = refs[:-2], refs[-2:]
    col_count = len(outs)
    for s in range(CAP):
        copy = pltpu.make_async_copy(tiles.at[local[2 + s]], held.at[s], sem.at[s])
        copy.start()
        copy.wait()

    def block(a, carry):
        for q in range(col_count):
            start = (a * col_count + q) * rows * 2
            outs[q][a] = front[pl.ds(start, rows, stride=2), :]
        return carry

    lax.fori_loop(0, outs[0].shape[0], block, 0, unroll=4)
    for s in range(CAP):
        place = local[2 + CAP + s]

        @pl.when(place >= 0)
        def _():
            for q in range(col_count):
                outs[q][place] += held[s, q]

    for q in range(col_count):
        outs[q][0] = jnp.zeros_like(outs[q][0])


def split_front(local, front, tiles, row_blocks):
    col_count, rows, size = tiles.shape[1:]
    return pl.pallas_call(
        functools.partial(split_kernel, rows),
        out_shape=[jax.ShapeDtypeStruct((row_blocks, rows, size), jnp.float32)] * col_count,
        in_specs=[
            pl.BlockSpec(memory_space=SMEM),
            pl.BlockSpec(memory_space=VMEM),
            pl.BlockSpec(memory_space=ANY),
        ],
        out_specs=[pl.BlockSpec(memory_space=VMEM)] * col_count,
        scratch_shapes=[
            VMEM((CAP, col_count, rows, size), jnp.float32),
            pltpu.SemaphoreType.DMA((CAP,)),
        ],
        compiler_params=LIMIT,
        name="split_front",
    )(local, front, tiles)


def slices_kernel(row_blocks, part_0, part_1, arrived, windows, column, total):
    total[...] = jnp.zeros_like(total)
    parts = (part_0, part_1)

    def source(d, carry):
        for s in range(CAP):
            block = parts[s][d]
            total[jnp.where(block < 0, row_blocks, block)] += arrived[d, s]
        return carry

    lax.fori_loop(0, arrived.shape[0], source, 0, unroll=8)
    column[...] = total[pl.ds(0, row_blocks)]
    windows[...] = jnp.broadcast_to(total[0][None], windows.shape)


def sum_slices(parts, arrived, row_count, row_blocks):
    devices, _, rows, size = arrived.shape
    outs = [
        jax.ShapeDtypeStruct((row_count, rows, size), jnp.float32),
        jax.ShapeDtypeStruct((row_blocks, rows, size), jnp.float32),
    ]
    return pl.pallas_call(
        functools.partial(slices_kernel, row_blocks),
        out_shape=outs,
        grid=(1,),
        in_specs=[pl.BlockSpec(memory_space=SMEM)] * 2
        + [pl.BlockSpec((devices, CAP, rows, size), lambda i: (0, 0, 0, 0))],
        out_specs=[pl.BlockSpec(out.shape, lambda i: (0, 0, 0)) for out in outs],
        scratch_shapes=[VMEM((row_blocks + 1, rows, size), jnp.float32)],
        compiler_params=LIMIT,
        name="sum_slices",
    )(*parts, arrived)


def spread_kernel(local, windows, column, *refs):
    col_count = len(refs) - 3
    own, (out, held, sem) = refs[:col_count], refs[col_count:]
    row_blocks = column.shape[0]
    for k in range(col_count):

        @pl.when(local[1] == k)
        def _():
            copy = pltpu.make_async_copy(own[k], held, sem)
            copy.start()
            copy.wait()

    total = column[...] + held[...]
    for k in range(col_count):
        out[k, pl.ds(0, row_blocks)] = total
        for i, j in enumerate((0, *range(k, windows.shape[0], col_count))):
            out[k, row_blocks + i] = windows[j]


def spread(local, windows, column, own):
    row_blocks, rows, size = column.shape
    extra = 1 + windows.shape[0] // len(own)
    out = jax.ShapeDtypeStruct((len(own), row_blocks + extra, rows, size), jnp.float32)
    return pl.pallas_call(
        spread_kernel,
        out_shape=out,
        in_specs=[pl.BlockSpec(memory_space=SMEM)]
        + [pl.BlockSpec(memory_space=VMEM)] * 2
        + [pl.BlockSpec(memory_space=ANY)] * len(own),
        out_specs=pl.BlockSpec(memory_space=VMEM),
        scratch_shapes=[VMEM(column.shape, jnp.float32), pltpu.SemaphoreType.DMA],
        compiler_params=LIMIT,
        name="spread",
    )(local, windows, column, *own)


def add_kernel(chunks, places, base, tiles, out, total, held, base_sem, tile_sem):
    slots, parts, rows, size = held.shape
    step = slots // chunks
    last = base.shape[0]
    whole = pl.ds(0, last)
    load_base = pltpu.make_async_copy(base, total.at[whole], base_sem)
    load_base.start()

    def load(i):
        some = pl.ds(i * step, step)
        skip = pl.ds(tiles.shape[1] - parts, parts)
        return pltpu.make_async_copy(tiles.at[some, skip], held.at[some], tile_sem.at[i])

    for i in range(chunks):
        load(i).start()
    load_base.wait()

    def add(j, carry):
        place = places[j]
        start = jnp.where(place < 0, last, place)
        total[pl.ds(start, size, stride=2), :] += held[j].reshape(size, size)
        return carry

    for i in range(chunks):
        load(i).wait()
        lax.fori_loop(i * step, (i + 1) * step, add, 0, unroll=4)
    store = pltpu.make_async_copy(total.at[whole], out, base_sem)
    store.start()
    store.wait()


def add_tiles(places, base, tiles, skip):
    slots, parts, rows, size = tiles.shape
    chunks = 8
    return pl.pallas_call(
        functools.partial(add_kernel, chunks),
        out_shape=jax.ShapeDtypeStruct(base.shape, jnp.float32),
        in_specs=[
            pl.BlockSpec(memory_space=SMEM),
            pl.BlockSpec(memory_space=ANY),
            pl.BlockSpec(memory_space=ANY),
        ],
        out_specs=pl.BlockSpec(memory_space=ANY),
        scratch_shapes=[
            VMEM((base.shape[0] + 2 * size, size), jnp.float32),
            VMEM((slots, parts - skip, rows, size), jnp.float32),
            pltpu.SemaphoreType.DMA,
            pltpu.SemaphoreType.DMA((chunks,)),
        ],
        compiler_params=LIMIT,
        name="add_tiles",
    )(places, base, tiles)


def update_kernel(shape, where, front, inverse_t, window, column, base):
    row_count, row_blocks = shape
    row_index, col_index = where[0], where[1]
    size = inverse_t.shape[0]
    held = jnp.dot(
        window[...], inverse_t[...], precision=HIGH, preferred_element_type=jnp.float32
    )
    contract = (((1,), (1,)), ((), ()))

    def block(a, carry):
        rows = jnp.dot(
            column[:, a].reshape(size, size),
            inverse_t[...],
            precision=HIGH,
            preferred_element_type=jnp.float32,
        )
        update = lax.dot_general(
            rows, held, contract, precision=HIGH, preferred_element_type=jnp.float32
        )
        below = a * row_count + row_index > 0
        update = jnp.where(below, update, jnp.zeros_like(update))
        even = pl.ds(a * 2 * size, size, stride=2)
        odd = pl.ds(a * 2 * size + 1, size, stride=2)
        base[even, :] = jnp.where(col_index == 0, rows, front[even, :] - update[:, :size])
        base[odd, :] = front[odd, :] - update[:, size:]
        return carry

    lax.fori_loop(0, row_blocks, block, 0)


def update_front(where, front, inverse_t, window, column, row_count, row_blocks):
    return pl.pallas_call(
        functools.partial(update_kernel, (row_count, row_blocks)),
        out_shape=jax.ShapeDtypeStruct(front.shape, jnp.float32),
        in_specs=[pl.BlockSpec(memory_space=SMEM)] + [pl.BlockSpec(memory_space=VMEM)] * 4,
        out_specs=pl.BlockSpec(memory_space=VMEM),
        compiler_params=LIMIT,
        name="update_front",
    )(where, front, inverse_t, window, column)


def after_kernel(*refs):
    pass


def after(value, *others):
    return pl.pallas_call(
        after_kernel,
        out_shape=jax.ShapeDtypeStruct(value.shape, value.dtype),
        in_specs=[pl.BlockSpec(memory_space=ANY)] * (1 + len(others)),
        out_specs=pl.BlockSpec(memory_space=ANY),
        input_output_aliases={0: 0},
        name="after",
    )(value, *others)


def per_device(front, child_tiles, child_rows, child_cols):
    row_count = lax.axis_size("row")
    col_count = lax.axis_size("col")
    row_index = lax.axis_index("row")
    col_index = lax.axis_index("col")
    both = ("row", "col")
    row_blocks, size, col_blocks = (front.shape[0], front.shape[2], front.shape[3])
    rows = size // col_count
    devices = row_count * col_count
    flat_front = front.reshape(row_blocks * size * col_blocks, size)
    tiles = child_tiles.reshape(-1, col_count, rows, size)
    slot, panel_tiles, message, local = send_tables(
        child_rows.reshape(-1),
        child_cols.reshape(-1),
        row_index,
        col_index,
        row_count,
        col_count,
        size,
    )
    message = lax.all_to_all(message, both, split_axis=0, concat_axis=0, tiled=True)
    main, part = ([message[:, h * CAP + s] for s in range(CAP)] for h in range(2))
    first, second = pack(slot, panel_tiles, local, tiles, flat_front, row_count, col_count)
    first = first.reshape((devices,) + first.shape[2:])
    own = list(split_front(local, flat_front, tiles, row_blocks))
    for k in (7, 2, 4, 5, 3, 1, 6):
        own[k] = lax.ppermute(own[k], "col", [(0, k)])
    arrived = lax.all_to_all(first, both, split_axis=0, concat_axis=0, tiled=True)
    windows, column = sum_slices(part, arrived, row_count, row_blocks)
    windows = lax.all_to_all(windows, "row", split_axis=0, concat_axis=0, tiled=True)
    column = spread(local, windows, column, own)
    column = lax.all_to_all(column, "col", split_axis=0, concat_axis=0, tiled=True)
    second = lax.all_to_all(
        after(second, column), both, split_axis=0, concat_axis=0, tiled=True
    )
    corner = column[:, row_blocks].reshape(size, size)
    window = jnp.swapaxes(column[:, row_blocks + 1 :], 0, 1).reshape(-1, size)
    factor = jnp.linalg.cholesky(0.5 * (corner + corner.T))
    inverse = jax.scipy.linalg.solve_triangular(
        factor, jnp.eye(size, dtype=jnp.float32), lower=True
    )
    total = add_tiles(main[0], flat_front, arrived, CAP)
    base = update_front(local, total, inverse.T, window, column, row_count, row_blocks)
    return add_tiles(main[1], base, second, 0).reshape(front.shape)


def solution(mesh):
    in_specs = (
        P(None, "row", None, None, "col", None),
        P("row", "col", None, None, None),
        P("row", "col", None),
        P("row", "col", None),
    )
    out_specs = P(None, "row", None, None, "col", None)
    return jax.shard_map(
        per_device, mesh=mesh, in_specs=in_specs, out_specs=out_specs, check_vma=False
    )
```

```python
import functools

import jax
import jax.numpy as jnp
from jax import lax
from jax.experimental import pallas as pl
from jax.experimental.pallas import tpu as pltpu
from jax.sharding import PartitionSpec as P

CAP = 2
HIGH = lax.Precision.HIGHEST
SMEM = pltpu.SMEM
VMEM = pltpu.VMEM
ANY = pl.ANY
LIMIT = pltpu.CompilerParams(vmem_limit_bytes=58 << 20)


def send_tables(parent_rows, parent_cols, row_index, col_index, row_count, col_count, size):
    tiles = parent_rows.shape[0]
    order = jnp.arange(tiles, dtype=jnp.int32)
    row_of = parent_rows % row_count
    owners = row_of * col_count + parent_cols % col_count
    same = (owners[:, None] == owners[None, :]) & (order[None, :] < order[:, None])
    slot = owners * CAP + jnp.sum(same.astype(jnp.int32), axis=1)
    block = parent_rows // row_count
    place = block * (2 * size) + parent_cols // col_count
    panel = parent_cols == 0
    wanted = jnp.arange(row_count * CAP, dtype=jnp.int32)[:, None]
    chosen = panel & (slot == wanted // CAP * (col_count * CAP) + wanted % CAP)
    panel_tiles = jnp.sum(jnp.where(chosen, order, 0), axis=1)
    dest = jnp.arange(row_count * col_count, dtype=jnp.int32)[:, None, None]
    part = jnp.arange(2 * CAP, dtype=jnp.int32)[None, :, None]
    in_main = (part < CAP) & (slot == dest * CAP + part) & ~panel
    dest_row = dest // col_count
    local = (dest_row == row_index) & (col_index == 0)
    in_panel = (part >= CAP) & (slot == dest_row * (col_count * CAP) + part - CAP) & panel
    value = jnp.where(in_main, place + 1, 0) + jnp.where(in_panel & ~local, block + 1, 0)
    message = jnp.sum(value, axis=2) - 1
    message = jnp.where(local[..., 0] & (part[..., 0] == CAP), 0, message)
    mine = jnp.arange(CAP, dtype=jnp.int32)[:, None]
    stays = panel & (col_index == 0) & (slot == row_index * (col_count * CAP) + mine)
    stay_tiles = jnp.sum(jnp.where(stays, order, 0), axis=1)
    stay_blocks = jnp.sum(jnp.where(stays, block + 1, 0), axis=1) - 1
    where = jnp.stack([row_index, col_index]).astype(jnp.int32)
    return slot, panel_tiles, message, jnp.concatenate([where, stay_tiles, stay_blocks])


def pack_panel_kernel(panel_tiles, local, tiles, front, out, held, corner, block, load_sem, corner_sem, sem):
    parts, rows, size = block.shape
    slots = held.shape[0]
    row_count = out.shape[0]
    load_corner = pltpu.make_async_copy(front.at[pl.ds(0, 2 * parts * rows)], corner, corner_sem)
    load_corner.start()
    loads = [
        pltpu.make_async_copy(tiles.at[panel_tiles[i]], held.at[i], load_sem.at[i])
        for i in range(slots)
    ]
    for load in loads:
        load.start()
    load_corner.wait()
    block[...] = corner[pl.ds(0, parts * rows, stride=2), :].reshape(block.shape)
    for r in range(row_count):
        mine = (local[0] == r) & (local[1] == 0)
        for s in range(CAP):
            loads[r * CAP + s].wait()

        @pl.when(mine)
        def _():
            for s in range(CAP):

                @pl.when(local[2 + CAP + s] == 0)
                def _():
                    block[...] += held[r * CAP + s]

            held[r * CAP] = block[...]

        for s in range(CAP):
            pltpu.make_async_copy(held.at[r * CAP + s], out.at[r, :, s], sem).start()
    whole = pltpu.make_async_copy(out, out, sem)
    whole.wait()


def pack_panel(panel_tiles, local, tiles, front, row_count):
    count, parts, rows, size = tiles.shape
    slots = row_count * CAP
    return pl.pallas_call(
        pack_panel_kernel,
        out_shape=jax.ShapeDtypeStruct((row_count, parts, CAP, rows, size), jnp.float32),
        in_specs=[pl.BlockSpec(memory_space=SMEM)] * 2 + [pl.BlockSpec(memory_space=ANY)] * 2,
        out_specs=pl.BlockSpec(memory_space=ANY),
        scratch_shapes=[
            VMEM((slots, parts, rows, size), jnp.float32),
            VMEM((2 * parts * rows, size), jnp.float32),
            VMEM((parts, rows, size), jnp.float32),
            pltpu.SemaphoreType.DMA((slots,)),
            pltpu.SemaphoreType.DMA,
            pltpu.SemaphoreType.DMA,
        ],
        compiler_params=LIMIT,
        name="pack_panel",
    )(panel_tiles, local, tiles, front)


def pack_kernel(chunks, slot, tiles, first, second, held, load_sem, main_sem):
    count = tiles.shape[0]
    step = count // chunks

    def load(i):
        part = pl.ds(i * step, step)
        return pltpu.make_async_copy(tiles.at[part], held.at[part], load_sem.at[i])

    for i in range(chunks):
        load(i).start()
    for i in range(chunks):
        load(i).wait()

        def send(k, carry):
            where = slot[k]
            owner = where // CAP

            @pl.when(where % CAP == 0)
            def _():
                pltpu.make_async_copy(held.at[k], first.at[owner], main_sem).start()

            @pl.when(where % CAP == 1)
            def _():
                pltpu.make_async_copy(held.at[k], second.at[owner], main_sem).start()

            return carry

        lax.fori_loop(i * step, (i + 1) * step, send, 0)
    pltpu.make_async_copy(held, second, main_sem).wait()


def pack(slot, tiles, devices):
    chunks = 8
    out = jax.ShapeDtypeStruct((devices,) + tiles.shape[1:], jnp.float32)
    return pl.pallas_call(
        functools.partial(pack_kernel, chunks),
        out_shape=[out, out],
        in_specs=[pl.BlockSpec(memory_space=SMEM), pl.BlockSpec(memory_space=ANY)],
        out_specs=[pl.BlockSpec(memory_space=ANY)] * 2,
        scratch_shapes=[
            VMEM(tiles.shape, jnp.float32),
            pltpu.SemaphoreType.DMA((chunks,)),
            pltpu.SemaphoreType.DMA,
        ],
        compiler_params=LIMIT,
        name="pack",
    )(slot, tiles)


def split_kernel(rows, local, front, tiles, *refs):
    outs, (held, sem) = refs[:-2], refs[-2:]
    col_count = len(outs)
    for s in range(CAP):
        copy = pltpu.make_async_copy(tiles.at[local[2 + s]], held.at[s], sem.at[s])
        copy.start()
        copy.wait()

    def block(a, carry):
        for q in range(col_count):
            start = (a * col_count + q) * rows * 2
            outs[q][a] = front[pl.ds(start, rows, stride=2), :]
        return carry

    lax.fori_loop(0, outs[0].shape[0], block, 0, unroll=4)
    for s in range(CAP):
        place = local[2 + CAP + s]

        @pl.when(place >= 0)
        def _():
            for q in range(col_count):
                outs[q][place] += held[s, q]

    for q in range(col_count):
        outs[q][0] = jnp.zeros_like(outs[q][0])


def split_front(local, front, tiles, row_blocks):
    col_count, rows, size = tiles.shape[1:]
    return pl.pallas_call(
        functools.partial(split_kernel, rows),
        out_shape=[jax.ShapeDtypeStruct((row_blocks, rows, size), jnp.float32)] * col_count,
        in_specs=[
            pl.BlockSpec(memory_space=SMEM),
            pl.BlockSpec(memory_space=VMEM),
            pl.BlockSpec(memory_space=ANY),
        ],
        out_specs=[pl.BlockSpec(memory_space=VMEM)] * col_count,
        scratch_shapes=[
            VMEM((CAP, col_count, rows, size), jnp.float32),
            pltpu.SemaphoreType.DMA((CAP,)),
        ],
        compiler_params=LIMIT,
        name="split_front",
    )(local, front, tiles)


def slices_kernel(row_blocks, part_0, part_1, arrived, windows, column, total):
    total[...] = jnp.zeros_like(total)
    parts = (part_0, part_1)

    def source(d, carry):
        for s in range(CAP):
            block = parts[s][d]
            total[jnp.where(block < 0, row_blocks, block)] += arrived[d, s]
        return carry

    lax.fori_loop(0, arrived.shape[0], source, 0, unroll=8)
    column[...] = total[pl.ds(0, row_blocks)]
    windows[...] = jnp.broadcast_to(total[0][None], windows.shape)


def sum_slices(parts, arrived, row_count, row_blocks):
    devices, _, rows, size = arrived.shape
    outs = [
        jax.ShapeDtypeStruct((row_count, rows, size), jnp.float32),
        jax.ShapeDtypeStruct((row_blocks, rows, size), jnp.float32),
    ]
    return pl.pallas_call(
        functools.partial(slices_kernel, row_blocks),
        out_shape=outs,
        grid=(1,),
        in_specs=[pl.BlockSpec(memory_space=SMEM)] * 2
        + [pl.BlockSpec((devices, CAP, rows, size), lambda i: (0, 0, 0, 0))],
        out_specs=[pl.BlockSpec(out.shape, lambda i: (0, 0, 0)) for out in outs],
        scratch_shapes=[VMEM((row_blocks + 1, rows, size), jnp.float32)],
        compiler_params=LIMIT,
        name="sum_slices",
    )(*parts, arrived)


def spread_kernel(local, windows, column, *refs):
    col_count = len(refs) - 3
    own, (out, held, sem) = refs[:col_count], refs[col_count:]
    row_blocks = column.shape[0]
    for k in range(col_count):

        @pl.when(local[1] == k)
        def _():
            copy = pltpu.make_async_copy(own[k], held, sem)
            copy.start()
            copy.wait()

    total = column[...] + held[...]
    for k in range(col_count):
        out[k, pl.ds(0, row_blocks)] = total
        for i, j in enumerate((0, *range(k, windows.shape[0], col_count))):
            out[k, row_blocks + i] = windows[j]


def spread(local, windows, column, own):
    row_blocks, rows, size = column.shape
    extra = 1 + windows.shape[0] // len(own)
    out = jax.ShapeDtypeStruct((len(own), row_blocks + extra, rows, size), jnp.float32)
    return pl.pallas_call(
        spread_kernel,
        out_shape=out,
        in_specs=[pl.BlockSpec(memory_space=SMEM)]
        + [pl.BlockSpec(memory_space=VMEM)] * 2
        + [pl.BlockSpec(memory_space=ANY)] * len(own),
        out_specs=pl.BlockSpec(memory_space=VMEM),
        scratch_shapes=[VMEM(column.shape, jnp.float32), pltpu.SemaphoreType.DMA],
        compiler_params=LIMIT,
        name="spread",
    )(local, windows, column, *own)


def add_kernel(chunks, places, base, tiles, out, total, held, base_sem, tile_sem):
    slots, parts, rows, size = held.shape
    step = slots // chunks
    last = base.shape[0]
    whole = pl.ds(0, last)
    load_base = pltpu.make_async_copy(base, total.at[whole], base_sem)
    load_base.start()

    def load(i):
        some = pl.ds(i * step, step)
        return pltpu.make_async_copy(tiles.at[some], held.at[some], tile_sem.at[i])

    for i in range(chunks):
        load(i).start()
    load_base.wait()

    def add(j, carry):
        place = places[j]
        start = jnp.where(place < 0, last, place)
        total[pl.ds(start, size, stride=2), :] += held[j].reshape(size, size)
        return carry

    for i in range(chunks):
        load(i).wait()
        lax.fori_loop(i * step, (i + 1) * step, add, 0, unroll=4)
    store = pltpu.make_async_copy(total.at[whole], out, base_sem)
    store.start()
    store.wait()


def add_tiles(places, base, tiles):
    slots, parts, rows, size = tiles.shape
    chunks = 8
    return pl.pallas_call(
        functools.partial(add_kernel, chunks),
        out_shape=jax.ShapeDtypeStruct(base.shape, jnp.float32),
        in_specs=[
            pl.BlockSpec(memory_space=SMEM),
            pl.BlockSpec(memory_space=ANY),
            pl.BlockSpec(memory_space=ANY),
        ],
        out_specs=pl.BlockSpec(memory_space=ANY),
        scratch_shapes=[
            VMEM((base.shape[0] + 2 * size, size), jnp.float32),
            VMEM(tiles.shape, jnp.float32),
            pltpu.SemaphoreType.DMA,
            pltpu.SemaphoreType.DMA((chunks,)),
        ],
        compiler_params=LIMIT,
        name="add_tiles",
    )(places, base, tiles)


def update_kernel(shape, where, front, inverse_t, window, column, base):
    row_count, row_blocks = shape
    row_index, col_index = where[0], where[1]
    size = inverse_t.shape[0]
    held = jnp.dot(
        window[...], inverse_t[...], precision=HIGH, preferred_element_type=jnp.float32
    )
    contract = (((1,), (1,)), ((), ()))

    def block(a, carry):
        rows = jnp.dot(
            column[:, a].reshape(size, size),
            inverse_t[...],
            precision=HIGH,
            preferred_element_type=jnp.float32,
        )
        update = lax.dot_general(
            rows, held, contract, precision=HIGH, preferred_element_type=jnp.float32
        )
        below = a * row_count + row_index > 0
        update = jnp.where(below, update, jnp.zeros_like(update))
        even = pl.ds(a * 2 * size, size, stride=2)
        odd = pl.ds(a * 2 * size + 1, size, stride=2)
        base[even, :] = jnp.where(col_index == 0, rows, front[even, :] - update[:, :size])
        base[odd, :] = front[odd, :] - update[:, size:]
        return carry

    lax.fori_loop(0, row_blocks, block, 0)


def update_front(where, front, inverse_t, window, column, row_count, row_blocks):
    return pl.pallas_call(
        functools.partial(update_kernel, (row_count, row_blocks)),
        out_shape=jax.ShapeDtypeStruct(front.shape, jnp.float32),
        in_specs=[pl.BlockSpec(memory_space=SMEM)] + [pl.BlockSpec(memory_space=VMEM)] * 4,
        out_specs=pl.BlockSpec(memory_space=VMEM),
        compiler_params=LIMIT,
        name="update_front",
    )(where, front, inverse_t, window, column)


def after_kernel(*refs):
    pass


def after(value, *others):
    return pl.pallas_call(
        after_kernel,
        out_shape=jax.ShapeDtypeStruct(value.shape, value.dtype),
        in_specs=[pl.BlockSpec(memory_space=ANY)] * (1 + len(others)),
        out_specs=pl.BlockSpec(memory_space=ANY),
        input_output_aliases={0: 0},
        name="after",
    )(value, *others)


def per_device(front, child_tiles, child_rows, child_cols):
    row_count = lax.axis_size("row")
    col_count = lax.axis_size("col")
    row_index = lax.axis_index("row")
    col_index = lax.axis_index("col")
    both = ("row", "col")
    row_blocks, size, col_blocks = (front.shape[0], front.shape[2], front.shape[3])
    rows = size // col_count
    devices = row_count * col_count
    flat_front = front.reshape(row_blocks * size * col_blocks, size)
    tiles = child_tiles.reshape(-1, col_count, rows, size)
    slot, panel_tiles, message, local = send_tables(
        child_rows.reshape(-1),
        child_cols.reshape(-1),
        row_index,
        col_index,
        row_count,
        col_count,
        size,
    )
    message = lax.all_to_all(message, both, split_axis=0, concat_axis=0, tiled=True)
    main, part = ([message[:, h * CAP + s] for s in range(CAP)] for h in range(2))
    sliced = pack_panel(panel_tiles, local, tiles, flat_front, row_count)
    sliced = sliced.reshape((devices,) + sliced.shape[2:])
    sliced = lax.all_to_all(sliced, both, split_axis=0, concat_axis=0, tiled=True)
    first, second = pack(slot, tiles, devices)
    own = list(split_front(local, flat_front, tiles, row_blocks))
    order = (1, 7, 4, 5, 2, 3, 6)
    for k in order:
        own[k] = lax.ppermute(own[k], "col", [(0, k)])
    windows, column = sum_slices(part, sliced, row_count, row_blocks)
    windows = lax.all_to_all(windows, "row", split_axis=0, concat_axis=0, tiled=True)
    first = after(first, windows, *(own[k] for k in order))
    first = lax.all_to_all(first, both, split_axis=0, concat_axis=0, tiled=True)
    column = after(spread(local, windows, column, own), first)
    column = lax.all_to_all(column, "col", split_axis=0, concat_axis=0, tiled=True)
    second = lax.all_to_all(
        after(second, column), both, split_axis=0, concat_axis=0, tiled=True
    )
    corner = column[:, row_blocks].reshape(size, size)
    window = jnp.swapaxes(column[:, row_blocks + 1 :], 0, 1).reshape(-1, size)
    factor = jnp.linalg.cholesky(0.5 * (corner + corner.T))
    inverse = jax.scipy.linalg.solve_triangular(
        factor, jnp.eye(size, dtype=jnp.float32), lower=True
    )
    total = add_tiles(main[0], flat_front, first)
    base = update_front(local, total, inverse.T, window, column, row_count, row_blocks)
    return add_tiles(main[1], base, second).reshape(front.shape)


def solution(mesh):
    in_specs = (
        P(None, "row", None, None, "col", None),
        P("row", "col", None, None, None),
        P("row", "col", None),
        P("row", "col", None),
    )
    out_specs = P(None, "row", None, None, "col", None)
    return jax.shard_map(
        per_device, mesh=mesh, in_specs=in_specs, out_specs=out_specs, check_vma=False
    )
```

```python
import functools

import jax
import jax.numpy as jnp
from jax import lax
from jax.experimental import pallas as pl
from jax.experimental.pallas import tpu as pltpu
from jax.sharding import PartitionSpec as P

CAP = 2
HIGH = lax.Precision.HIGHEST
SMEM = pltpu.SMEM
VMEM = pltpu.VMEM
ANY = pl.ANY
LIMIT = pltpu.CompilerParams(vmem_limit_bytes=58 << 20)


def send_tables(parent_rows, parent_cols, row_index, col_index, row_count, col_count, size):
    tiles = parent_rows.shape[0]
    order = jnp.arange(tiles, dtype=jnp.int32)
    row_of = parent_rows % row_count
    owners = row_of * col_count + parent_cols % col_count
    same = (owners[:, None] == owners[None, :]) & (order[None, :] < order[:, None])
    slot = owners * CAP + jnp.sum(same.astype(jnp.int32), axis=1)
    block = parent_rows // row_count
    place = block * (2 * size) + parent_cols // col_count
    panel = parent_cols == 0
    wanted = jnp.arange(row_count * CAP, dtype=jnp.int32)[:, None]
    chosen = panel & (slot == wanted // CAP * (col_count * CAP) + wanted % CAP)
    panel_tiles = jnp.sum(jnp.where(chosen, order, 0), axis=1)
    dest = jnp.arange(row_count * col_count, dtype=jnp.int32)[:, None, None]
    part = jnp.arange(2 * CAP, dtype=jnp.int32)[None, :, None]
    in_main = (part < CAP) & (slot == dest * CAP + part) & ~panel
    dest_row = dest // col_count
    local = (dest_row == row_index) & (col_index == 0)
    in_panel = (part >= CAP) & (slot == dest_row * (col_count * CAP) + part - CAP) & panel
    value = jnp.where(in_main, place + 1, 0) + jnp.where(in_panel & ~local, block + 1, 0)
    message = jnp.sum(value, axis=2) - 1
    message = jnp.where(local[..., 0] & (part[..., 0] == CAP), 0, message)
    mine = jnp.arange(CAP, dtype=jnp.int32)[:, None]
    stays = panel & (col_index == 0) & (slot == row_index * (col_count * CAP) + mine)
    stay_tiles = jnp.sum(jnp.where(stays, order, 0), axis=1)
    stay_blocks = jnp.sum(jnp.where(stays, block + 1, 0), axis=1) - 1
    where = jnp.stack([row_index, col_index]).astype(jnp.int32)
    return slot, panel_tiles, message, jnp.concatenate([where, stay_tiles, stay_blocks])


def pack_panel_kernel(panel_tiles, local, tiles, front, out, held, corner, block, load_sem, corner_sem, sem):
    parts, rows, size = block.shape
    slots = held.shape[0]
    row_count = out.shape[0]
    load_corner = pltpu.make_async_copy(front.at[pl.ds(0, 2 * parts * rows)], corner, corner_sem)
    load_corner.start()
    loads = [
        pltpu.make_async_copy(tiles.at[panel_tiles[i]], held.at[i], load_sem.at[i])
        for i in range(slots)
    ]
    for load in loads:
        load.start()
    load_corner.wait()
    block[...] = corner[pl.ds(0, parts * rows, stride=2), :].reshape(block.shape)
    for r in range(row_count):
        mine = (local[0] == r) & (local[1] == 0)
        for s in range(CAP):
            loads[r * CAP + s].wait()

        @pl.when(mine)
        def _():
            for s in range(CAP):

                @pl.when(local[2 + CAP + s] == 0)
                def _():
                    block[...] += held[r * CAP + s]

            held[r * CAP] = block[...]

        for s in range(CAP):
            pltpu.make_async_copy(held.at[r * CAP + s], out.at[r, :, s], sem).start()
    whole = pltpu.make_async_copy(out, out, sem)
    whole.wait()


def pack_panel(panel_tiles, local, tiles, front, row_count):
    count, parts, rows, size = tiles.shape
    slots = row_count * CAP
    return pl.pallas_call(
        pack_panel_kernel,
        out_shape=jax.ShapeDtypeStruct((row_count, parts, CAP, rows, size), jnp.float32),
        in_specs=[pl.BlockSpec(memory_space=SMEM)] * 2 + [pl.BlockSpec(memory_space=ANY)] * 2,
        out_specs=pl.BlockSpec(memory_space=ANY),
        scratch_shapes=[
            VMEM((slots, parts, rows, size), jnp.float32),
            VMEM((2 * parts * rows, size), jnp.float32),
            VMEM((parts, rows, size), jnp.float32),
            pltpu.SemaphoreType.DMA((slots,)),
            pltpu.SemaphoreType.DMA,
            pltpu.SemaphoreType.DMA,
        ],
        compiler_params=LIMIT,
        name="pack_panel",
    )(panel_tiles, local, tiles, front)


def pack_kernel(chunks, slot, tiles, first, second, held, load_sem, main_sem):
    count = tiles.shape[0]
    step = count // chunks

    def load(i):
        part = pl.ds(i * step, step)
        return pltpu.make_async_copy(tiles.at[part], held.at[part], load_sem.at[i])

    for i in range(chunks):
        load(i).start()
    for i in range(chunks):
        load(i).wait()

        def send(k, carry):
            where = slot[k]
            owner = where // CAP

            @pl.when(where % CAP == 0)
            def _():
                pltpu.make_async_copy(held.at[k], first.at[owner], main_sem).start()

            @pl.when(where % CAP == 1)
            def _():
                pltpu.make_async_copy(held.at[k], second.at[owner], main_sem).start()

            return carry

        lax.fori_loop(i * step, (i + 1) * step, send, 0)
    pltpu.make_async_copy(held, second, main_sem).wait()


def pack(slot, tiles, devices):
    chunks = 8
    out = jax.ShapeDtypeStruct((devices,) + tiles.shape[1:], jnp.float32)
    return pl.pallas_call(
        functools.partial(pack_kernel, chunks),
        out_shape=[out, out],
        in_specs=[pl.BlockSpec(memory_space=SMEM), pl.BlockSpec(memory_space=ANY)],
        out_specs=[pl.BlockSpec(memory_space=ANY)] * 2,
        scratch_shapes=[
            VMEM(tiles.shape, jnp.float32),
            pltpu.SemaphoreType.DMA((chunks,)),
            pltpu.SemaphoreType.DMA,
        ],
        compiler_params=LIMIT,
        name="pack",
    )(slot, tiles)


def split_kernel(rows, local, front, tiles, *refs):
    outs, (held, sem) = refs[:-2], refs[-2:]
    col_count = len(outs)
    for s in range(CAP):
        copy = pltpu.make_async_copy(tiles.at[local[2 + s]], held.at[s], sem.at[s])
        copy.start()
        copy.wait()

    def block(a, carry):
        for q in range(col_count):
            start = (a * col_count + q) * rows * 2
            outs[q][a] = front[pl.ds(start, rows, stride=2), :]
        return carry

    lax.fori_loop(0, outs[0].shape[0], block, 0, unroll=4)
    for s in range(CAP):
        place = local[2 + CAP + s]

        @pl.when(place >= 0)
        def _():
            for q in range(col_count):
                outs[q][place] += held[s, q]

    for q in range(col_count):
        outs[q][0] = jnp.zeros_like(outs[q][0])


def split_front(local, front, tiles, row_blocks):
    col_count, rows, size = tiles.shape[1:]
    return pl.pallas_call(
        functools.partial(split_kernel, rows),
        out_shape=[jax.ShapeDtypeStruct((row_blocks, rows, size), jnp.float32)] * col_count,
        in_specs=[
            pl.BlockSpec(memory_space=SMEM),
            pl.BlockSpec(memory_space=VMEM),
            pl.BlockSpec(memory_space=ANY),
        ],
        out_specs=[pl.BlockSpec(memory_space=VMEM)] * col_count,
        scratch_shapes=[
            VMEM((CAP, col_count, rows, size), jnp.float32),
            pltpu.SemaphoreType.DMA((CAP,)),
        ],
        compiler_params=LIMIT,
        name="split_front",
    )(local, front, tiles)


def slices_kernel(row_blocks, part_0, part_1, arrived, windows, column, total):
    total[...] = jnp.zeros_like(total)
    parts = (part_0, part_1)

    def source(d, carry):
        for s in range(CAP):
            block = parts[s][d]
            total[jnp.where(block < 0, row_blocks, block)] += arrived[d, s]
        return carry

    lax.fori_loop(0, arrived.shape[0], source, 0, unroll=8)
    column[...] = total[pl.ds(0, row_blocks)]
    windows[...] = jnp.broadcast_to(total[0][None], windows.shape)


def sum_slices(parts, arrived, row_count, row_blocks):
    devices, _, rows, size = arrived.shape
    outs = [
        jax.ShapeDtypeStruct((row_count, rows, size), jnp.float32),
        jax.ShapeDtypeStruct((row_blocks, rows, size), jnp.float32),
    ]
    return pl.pallas_call(
        functools.partial(slices_kernel, row_blocks),
        out_shape=outs,
        grid=(1,),
        in_specs=[pl.BlockSpec(memory_space=SMEM)] * 2
        + [pl.BlockSpec((devices, CAP, rows, size), lambda i: (0, 0, 0, 0))],
        out_specs=[pl.BlockSpec(out.shape, lambda i: (0, 0, 0)) for out in outs],
        scratch_shapes=[VMEM((row_blocks + 1, rows, size), jnp.float32)],
        compiler_params=LIMIT,
        name="sum_slices",
    )(*parts, arrived)


def join_kernel(local, windows, column, *refs):
    own, (out, held, sem) = refs[:-3], refs[-3:]
    row_blocks = column.shape[0]
    for k in range(len(own)):

        @pl.when(local[1] == k)
        def _():
            copy = pltpu.make_async_copy(own[k], held, sem)
            copy.start()
            copy.wait()

    out[pl.ds(0, row_blocks)] = column[...] + held[...]
    out[pl.ds(row_blocks, windows.shape[0])] = windows[...]


def join(local, windows, column, own):
    row_blocks, rows, size = column.shape
    out = jax.ShapeDtypeStruct((row_blocks + windows.shape[0], rows, size), jnp.float32)
    return pl.pallas_call(
        join_kernel,
        out_shape=out,
        in_specs=[pl.BlockSpec(memory_space=SMEM)]
        + [pl.BlockSpec(memory_space=VMEM)] * 2
        + [pl.BlockSpec(memory_space=ANY)] * len(own),
        out_specs=pl.BlockSpec(memory_space=VMEM),
        scratch_shapes=[VMEM(column.shape, jnp.float32), pltpu.SemaphoreType.DMA],
        compiler_params=LIMIT,
        name="join",
    )(local, windows, column, *own)


def add_kernel(chunks, places, base, tiles, out, total, held, base_sem, tile_sem):
    slots, parts, rows, size = held.shape
    step = slots // chunks
    last = base.shape[0]
    whole = pl.ds(0, last)
    load_base = pltpu.make_async_copy(base, total.at[whole], base_sem)
    load_base.start()

    def load(i):
        some = pl.ds(i * step, step)
        return pltpu.make_async_copy(tiles.at[some], held.at[some], tile_sem.at[i])

    for i in range(chunks):
        load(i).start()
    load_base.wait()

    def add(j, carry):
        place = places[j]
        start = jnp.where(place < 0, last, place)
        total[pl.ds(start, size, stride=2), :] += held[j].reshape(size, size)
        return carry

    for i in range(chunks):
        load(i).wait()
        lax.fori_loop(i * step, (i + 1) * step, add, 0, unroll=4)
    store = pltpu.make_async_copy(total.at[whole], out, base_sem)
    store.start()
    store.wait()


def add_tiles(places, base, tiles):
    slots, parts, rows, size = tiles.shape
    chunks = 8
    return pl.pallas_call(
        functools.partial(add_kernel, chunks),
        out_shape=jax.ShapeDtypeStruct(base.shape, jnp.float32),
        in_specs=[
            pl.BlockSpec(memory_space=SMEM),
            pl.BlockSpec(memory_space=ANY),
            pl.BlockSpec(memory_space=ANY),
        ],
        out_specs=pl.BlockSpec(memory_space=ANY),
        scratch_shapes=[
            VMEM((base.shape[0] + 2 * size, size), jnp.float32),
            VMEM(tiles.shape, jnp.float32),
            pltpu.SemaphoreType.DMA,
            pltpu.SemaphoreType.DMA((chunks,)),
        ],
        compiler_params=LIMIT,
        name="add_tiles",
    )(places, base, tiles)


def update_kernel(shape, where, front, inverse_t, window, column, base):
    row_count, row_blocks = shape
    row_index, col_index = where[0], where[1]
    size = inverse_t.shape[0]
    held = jnp.dot(
        window[...], inverse_t[...], precision=HIGH, preferred_element_type=jnp.float32
    )
    contract = (((1,), (1,)), ((), ()))

    def block(a, carry):
        rows = jnp.dot(
            column[:, a].reshape(size, size),
            inverse_t[...],
            precision=HIGH,
            preferred_element_type=jnp.float32,
        )
        update = lax.dot_general(
            rows, held, contract, precision=HIGH, preferred_element_type=jnp.float32
        )
        below = a * row_count + row_index > 0
        update = jnp.where(below, update, jnp.zeros_like(update))
        even = pl.ds(a * 2 * size, size, stride=2)
        odd = pl.ds(a * 2 * size + 1, size, stride=2)
        base[even, :] = jnp.where(col_index == 0, rows, front[even, :] - update[:, :size])
        base[odd, :] = front[odd, :] - update[:, size:]
        return carry

    lax.fori_loop(0, row_blocks, block, 0)


def update_front(where, front, inverse_t, window, column, row_count, row_blocks):
    return pl.pallas_call(
        functools.partial(update_kernel, (row_count, row_blocks)),
        out_shape=jax.ShapeDtypeStruct(front.shape, jnp.float32),
        in_specs=[pl.BlockSpec(memory_space=SMEM)] + [pl.BlockSpec(memory_space=VMEM)] * 4,
        out_specs=pl.BlockSpec(memory_space=VMEM),
        compiler_params=LIMIT,
        name="update_front",
    )(where, front, inverse_t, window, column)


def after_kernel(*refs):
    pass


def after(value, *others):
    return pl.pallas_call(
        after_kernel,
        out_shape=jax.ShapeDtypeStruct(value.shape, value.dtype),
        in_specs=[pl.BlockSpec(memory_space=ANY)] * (1 + len(others)),
        out_specs=pl.BlockSpec(memory_space=ANY),
        input_output_aliases={0: 0},
        name="after",
    )(value, *others)


def per_device(front, child_tiles, child_rows, child_cols):
    row_count = lax.axis_size("row")
    col_count = lax.axis_size("col")
    row_index = lax.axis_index("row")
    col_index = lax.axis_index("col")
    both = ("row", "col")
    row_blocks, size, col_blocks = (front.shape[0], front.shape[2], front.shape[3])
    rows = size // col_count
    devices = row_count * col_count
    flat_front = front.reshape(row_blocks * size * col_blocks, size)
    tiles = child_tiles.reshape(-1, col_count, rows, size)
    slot, panel_tiles, message, local = send_tables(
        child_rows.reshape(-1),
        child_cols.reshape(-1),
        row_index,
        col_index,
        row_count,
        col_count,
        size,
    )
    message = lax.all_to_all(message, both, split_axis=0, concat_axis=0, tiled=True)
    main, part = ([message[:, h * CAP + s] for s in range(CAP)] for h in range(2))
    sliced = pack_panel(panel_tiles, local, tiles, flat_front, row_count)
    sliced = sliced.reshape((devices,) + sliced.shape[2:])
    sliced = lax.all_to_all(sliced, both, split_axis=0, concat_axis=0, tiled=True)
    first, second = pack(slot, tiles, devices)
    own = list(split_front(local, flat_front, tiles, row_blocks))
    order = (1, 7, 4, 5, 2, 3, 6)
    for k in order:
        late = order.index(k) >= 5
        own[k] = lax.ppermute(after(own[k], sliced) if late else own[k], "col", [(0, k)])
    sliced = after(sliced, first)
    windows, column = sum_slices(part, sliced, row_count, row_blocks)
    windows = lax.all_to_all(windows, "row", split_axis=0, concat_axis=0, tiled=True)
    column = join(local, windows, column, own)
    first = after(first, column)
    column = lax.all_gather(column, "col", axis=0)
    first = lax.all_to_all(first, both, split_axis=0, concat_axis=0, tiled=True)
    second = after(second, first)
    second = lax.all_to_all(second, both, split_axis=0, concat_axis=0, tiled=True)

    def block_of(j):
        found = lax.dynamic_index_in_dim(column, row_blocks + j, axis=1, keepdims=False)
        return found.reshape(size, size)

    corner = block_of(0)
    window = jnp.concatenate(
        [block_of(m * col_count + col_index) for m in range(col_blocks)], axis=0
    )
    factor = jnp.linalg.cholesky(0.5 * (corner + corner.T))
    inverse = jax.scipy.linalg.solve_triangular(
        factor, jnp.eye(size, dtype=jnp.float32), lower=True
    )
    total = add_tiles(main[0], flat_front, first)
    base = update_front(local, total, inverse.T, window, column, row_count, row_blocks)
    return add_tiles(main[1], base, second).reshape(front.shape)


def solution(mesh):
    in_specs = (
        P(None, "row", None, None, "col", None),
        P("row", "col", None, None, None),
        P("row", "col", None),
        P("row", "col", None),
    )
    out_specs = P(None, "row", None, None, "col", None)
    return jax.shard_map(
        per_device, mesh=mesh, in_specs=in_specs, out_specs=out_specs, check_vma=False
    )
```

```python
import functools

import jax
import jax.numpy as jnp
from jax import lax
from jax.experimental import pallas as pl
from jax.experimental.pallas import tpu as pltpu
from jax.sharding import PartitionSpec as P

CAP = 2
HIGH = lax.Precision.HIGHEST
SMEM = pltpu.SMEM
VMEM = pltpu.VMEM
ANY = pl.ANY
LIMIT = pltpu.CompilerParams(vmem_limit_bytes=58 << 20)


def send_tables(parent_rows, parent_cols, row_index, col_index, row_count, col_count, size):
    tiles = parent_rows.shape[0]
    order = jnp.arange(tiles, dtype=jnp.int32)
    row_of = parent_rows % row_count
    owners = row_of * col_count + parent_cols % col_count
    same = (owners[:, None] == owners[None, :]) & (order[None, :] < order[:, None])
    slot = owners * CAP + jnp.sum(same.astype(jnp.int32), axis=1)
    block = parent_rows // row_count
    place = block * (2 * size) + parent_cols // col_count
    panel = parent_cols == 0
    wanted = jnp.arange(row_count * CAP, dtype=jnp.int32)[:, None]
    chosen = panel & (slot == wanted // CAP * (col_count * CAP) + wanted % CAP)
    panel_tiles = jnp.sum(jnp.where(chosen, order, 0), axis=1)
    dest = jnp.arange(row_count * col_count, dtype=jnp.int32)[:, None, None]
    part = jnp.arange(2 * CAP, dtype=jnp.int32)[None, :, None]
    in_main = (part < CAP) & (slot == dest * CAP + part) & ~panel
    dest_row = dest // col_count
    local = (dest_row == row_index) & (col_index == 0)
    in_panel = (part >= CAP) & (slot == dest_row * (col_count * CAP) + part - CAP) & panel
    value = jnp.where(in_main, place + 1, 0) + jnp.where(in_panel & ~local, block + 1, 0)
    message = jnp.sum(value, axis=2) - 1
    message = jnp.where(local[..., 0] & (part[..., 0] == CAP), 0, message)
    mine = jnp.arange(CAP, dtype=jnp.int32)[:, None]
    stays = panel & (col_index == 0) & (slot == row_index * (col_count * CAP) + mine)
    stay_tiles = jnp.sum(jnp.where(stays, order, 0), axis=1)
    stay_blocks = jnp.sum(jnp.where(stays, block + 1, 0), axis=1) - 1
    where = jnp.stack([row_index, col_index]).astype(jnp.int32)
    return slot, panel_tiles, message, jnp.concatenate([where, stay_tiles, stay_blocks])


def pack_panel_kernel(
    panel_tiles, local, places, tiles, front, out, held, corner, block, load_sem, corner_sem, sem
):
    size = block.shape[-1]
    slots = held.shape[0]
    row_count = out.shape[0]
    groups = block.shape[1]
    pltpu.make_async_copy(places, out.at[:, :, CAP * groups], sem).start()
    load_corner = pltpu.make_async_copy(front.at[pl.ds(0, 2 * size)], corner, corner_sem)
    load_corner.start()
    loads = [
        pltpu.make_async_copy(tiles.at[panel_tiles[i]], held.at[i], load_sem.at[i])
        for i in range(slots)
    ]
    for load in loads:
        load.start()
    load_corner.wait()
    block[...] = corner[pl.ds(0, size, stride=2), :].reshape(block.shape)
    for r in range(row_count):
        mine = (local[0] == r) & (local[1] == 0)
        for s in range(CAP):
            loads[r * CAP + s].wait()

        @pl.when(mine)
        def _():
            for s in range(CAP):

                @pl.when(local[2 + CAP + s] == 0)
                def _():
                    block[...] += held[r * CAP + s]

            held[r * CAP] = block[...]

        for s in range(CAP):
            pltpu.make_async_copy(
                held.at[r * CAP + s], out.at[r, :, pl.ds(s * groups, groups)], sem
            ).start()
    pltpu.make_async_copy(out, out, sem).wait()


def pack_panel(panel_tiles, local, message, tiles, front, row_count, col_count):
    size = tiles.shape[-1]
    rows = size // col_count
    groups = rows // 8
    slots = row_count * CAP
    view = (col_count, groups, 8, size)
    places = jnp.pad(
        message.astype(jnp.float32)[:, None, :], ((0, 0), (0, 7), (0, size - message.shape[1]))
    ).reshape(row_count, col_count, 8, size)
    sent = pl.pallas_call(
        pack_panel_kernel,
        out_shape=jax.ShapeDtypeStruct(
            (row_count, col_count, CAP * groups + 1, 8, size), jnp.float32
        ),
        in_specs=[pl.BlockSpec(memory_space=SMEM)] * 2
        + [pl.BlockSpec(memory_space=VMEM)]
        + [pl.BlockSpec(memory_space=ANY)] * 2,
        out_specs=pl.BlockSpec(memory_space=ANY),
        scratch_shapes=[
            VMEM((slots,) + view, jnp.float32),
            VMEM((2 * size, size), jnp.float32),
            VMEM(view, jnp.float32),
            pltpu.SemaphoreType.DMA((slots,)),
            pltpu.SemaphoreType.DMA,
            pltpu.SemaphoreType.DMA,
        ],
        compiler_params=LIMIT,
        name="pack_panel",
    )(panel_tiles, local, places, tiles.reshape((-1,) + view), front)
    return sent.reshape((row_count * col_count,) + sent.shape[2:])


def pack_kernel(chunks, slot, tiles, first, second, held, load_sem, main_sem):
    count = tiles.shape[0]
    step = count // chunks

    def load(i):
        part = pl.ds(i * step, step)
        return pltpu.make_async_copy(tiles.at[part], held.at[part], load_sem.at[i])

    for i in range(chunks):
        load(i).start()
    for i in range(chunks):
        load(i).wait()

        def send(k, carry):
            where = slot[k]
            owner = where // CAP

            @pl.when(where % CAP == 0)
            def _():
                pltpu.make_async_copy(held.at[k], first.at[owner], main_sem).start()

            @pl.when(where % CAP == 1)
            def _():
                pltpu.make_async_copy(held.at[k], second.at[owner], main_sem).start()

            return carry

        lax.fori_loop(i * step, (i + 1) * step, send, 0)
    pltpu.make_async_copy(held, second, main_sem).wait()


def pack(slot, tiles, devices):
    chunks = 8
    out = jax.ShapeDtypeStruct((devices,) + tiles.shape[1:], jnp.float32)
    return pl.pallas_call(
        functools.partial(pack_kernel, chunks),
        out_shape=[out, out],
        in_specs=[pl.BlockSpec(memory_space=SMEM), pl.BlockSpec(memory_space=ANY)],
        out_specs=[pl.BlockSpec(memory_space=ANY)] * 2,
        scratch_shapes=[
            VMEM(tiles.shape, jnp.float32),
            pltpu.SemaphoreType.DMA((chunks,)),
            pltpu.SemaphoreType.DMA,
        ],
        compiler_params=LIMIT,
        name="pack",
    )(slot, tiles)


def split_kernel(rows, local, front, tiles, *refs):
    outs, (held, sem) = refs[:-2], refs[-2:]
    col_count = len(outs)
    for s in range(CAP):
        copy = pltpu.make_async_copy(tiles.at[local[2 + s]], held.at[s], sem.at[s])
        copy.start()
        copy.wait()

    def block(a, carry):
        for q in range(col_count):
            start = (a * col_count + q) * rows * 2
            outs[q][a] = front[pl.ds(start, rows, stride=2), :]
        return carry

    lax.fori_loop(0, outs[0].shape[0], block, 0, unroll=4)
    for s in range(CAP):
        place = local[2 + CAP + s]

        @pl.when(place >= 0)
        def _():
            for q in range(col_count):
                outs[q][place] += held[s, q]

    for q in range(col_count):
        outs[q][0] = jnp.zeros_like(outs[q][0])


def split_front(local, front, tiles, row_blocks):
    col_count, rows, size = tiles.shape[1:]
    return pl.pallas_call(
        functools.partial(split_kernel, rows),
        out_shape=[jax.ShapeDtypeStruct((row_blocks, rows, size), jnp.float32)] * col_count,
        in_specs=[
            pl.BlockSpec(memory_space=SMEM),
            pl.BlockSpec(memory_space=VMEM),
            pl.BlockSpec(memory_space=ANY),
        ],
        out_specs=[pl.BlockSpec(memory_space=VMEM)] * col_count,
        scratch_shapes=[
            VMEM((CAP, col_count, rows, size), jnp.float32),
            pltpu.SemaphoreType.DMA((CAP,)),
        ],
        compiler_params=LIMIT,
        name="split_front",
    )(local, front, tiles)


def slices_kernel(row_blocks, part_0, part_1, arrived, windows, column, total):
    total[...] = jnp.zeros_like(total)
    parts = (part_0, part_1)
    groups = arrived.shape[1] // CAP
    rows, size = total.shape[1:]

    def source(d, carry):
        for s in range(CAP):
            block = parts[s][d]
            piece = arrived[d, pl.ds(s * groups, groups)].reshape(rows, size)
            total[jnp.where(block < 0, row_blocks, block)] += piece
        return carry

    lax.fori_loop(0, arrived.shape[0], source, 0, unroll=8)
    column[...] = total[pl.ds(0, row_blocks)]
    windows[...] = jnp.broadcast_to(total[0][None], windows.shape)


def sum_slices(parts, arrived, row_count, row_blocks):
    devices, groups, _, size = arrived.shape
    groups = groups // CAP
    rows = groups * 8
    outs = [
        jax.ShapeDtypeStruct((row_count, rows, size), jnp.float32),
        jax.ShapeDtypeStruct((row_blocks, rows, size), jnp.float32),
    ]
    return pl.pallas_call(
        functools.partial(slices_kernel, row_blocks),
        out_shape=outs,
        grid=(1,),
        in_specs=[pl.BlockSpec(memory_space=SMEM)] * 2
        + [pl.BlockSpec((devices, CAP * groups, 8, size), lambda i: (0, 0, 0, 0))],
        out_specs=[pl.BlockSpec(out.shape, lambda i: (0, 0, 0)) for out in outs],
        scratch_shapes=[VMEM((row_blocks + 1, rows, size), jnp.float32)],
        compiler_params=LIMIT,
        name="sum_slices",
    )(*parts, arrived)


def spread_kernel(local, windows, column, *refs):
    own, (out, held, load_sem, sem, few_sem) = refs[:-5], refs[-5:]
    col_count = len(own)
    row_blocks = column.shape[0]
    few = []
    for k in range(col_count):
        for i, j in enumerate((0, *range(k, windows.shape[0], col_count))):
            few.append(
                pltpu.make_async_copy(
                    windows.at[j], out.at[k, row_blocks + i], few_sem.at[len(few)]
                )
            )
    for copy in few:
        copy.start()
    for k in range(col_count):

        @pl.when(local[1] == k)
        def _():
            load = pltpu.make_async_copy(own[k], held, load_sem)
            load.start()
            load.wait()

    held[...] += column[...]
    copies = [
        pltpu.make_async_copy(held, out.at[k, pl.ds(0, row_blocks)], sem.at[k])
        for k in range(col_count)
    ]
    for copy in copies:
        copy.start()
    for copy in copies + few:
        copy.wait()


def spread(local, windows, column, own):
    row_blocks, rows, size = column.shape
    col_count = len(own)
    extra = 1 + windows.shape[0] // col_count
    out = jax.ShapeDtypeStruct((col_count, row_blocks + extra, rows, size), jnp.float32)
    return pl.pallas_call(
        spread_kernel,
        out_shape=out,
        in_specs=[pl.BlockSpec(memory_space=SMEM)]
        + [pl.BlockSpec(memory_space=VMEM)] * 2
        + [pl.BlockSpec(memory_space=ANY)] * col_count,
        out_specs=pl.BlockSpec(memory_space=ANY),
        scratch_shapes=[
            VMEM(column.shape, jnp.float32),
            pltpu.SemaphoreType.DMA,
            pltpu.SemaphoreType.DMA((col_count,)),
            pltpu.SemaphoreType.DMA((col_count * extra,)),
        ],
        compiler_params=LIMIT,
        name="spread",
    )(local, windows, column, *own)


def add_kernel(chunks, places, base, tiles, out, total, held, base_sem, tile_sem):
    slots, parts, rows, size = held.shape
    step = slots // chunks
    last = base.shape[0]
    whole = pl.ds(0, last)
    load_base = pltpu.make_async_copy(base, total.at[whole], base_sem)
    load_base.start()

    def load(i):
        some = pl.ds(i * step, step)
        return pltpu.make_async_copy(tiles.at[some], held.at[some], tile_sem.at[i])

    for i in range(chunks):
        load(i).start()
    load_base.wait()

    def add(j, carry):
        place = places[j]
        start = jnp.where(place < 0, last, place)
        total[pl.ds(start, size, stride=2), :] += held[j].reshape(size, size)
        return carry

    for i in range(chunks):
        load(i).wait()
        lax.fori_loop(i * step, (i + 1) * step, add, 0, unroll=4)
    store = pltpu.make_async_copy(total.at[whole], out, base_sem)
    store.start()
    store.wait()


def add_tiles(places, base, tiles):
    slots, parts, rows, size = tiles.shape
    chunks = 8
    return pl.pallas_call(
        functools.partial(add_kernel, chunks),
        out_shape=jax.ShapeDtypeStruct(base.shape, jnp.float32),
        in_specs=[
            pl.BlockSpec(memory_space=SMEM),
            pl.BlockSpec(memory_space=ANY),
            pl.BlockSpec(memory_space=ANY),
        ],
        out_specs=pl.BlockSpec(memory_space=ANY),
        scratch_shapes=[
            VMEM((base.shape[0] + 2 * size, size), jnp.float32),
            VMEM(tiles.shape, jnp.float32),
            pltpu.SemaphoreType.DMA,
            pltpu.SemaphoreType.DMA((chunks,)),
        ],
        compiler_params=LIMIT,
        name="add_tiles",
    )(places, base, tiles)


def update_kernel(shape, where, front, inverse_t, window, column, base):
    row_count, row_blocks = shape
    row_index, col_index = where[0], where[1]
    size = inverse_t.shape[0]
    held = jnp.dot(
        window[...], inverse_t[...], precision=HIGH, preferred_element_type=jnp.float32
    )
    contract = (((1,), (1,)), ((), ()))

    def block(a, carry):
        rows = jnp.dot(
            column[:, a].reshape(size, size),
            inverse_t[...],
            precision=HIGH,
            preferred_element_type=jnp.float32,
        )
        update = lax.dot_general(
            rows, held, contract, precision=HIGH, preferred_element_type=jnp.float32
        )
        below = a * row_count + row_index > 0
        update = jnp.where(below, update, jnp.zeros_like(update))
        even = pl.ds(a * 2 * size, size, stride=2)
        odd = pl.ds(a * 2 * size + 1, size, stride=2)
        base[even, :] = jnp.where(col_index == 0, rows, front[even, :] - update[:, :size])
        base[odd, :] = front[odd, :] - update[:, size:]
        return carry

    lax.fori_loop(0, row_blocks, block, 0)


def update_front(where, front, inverse_t, window, column, row_count, row_blocks):
    return pl.pallas_call(
        functools.partial(update_kernel, (row_count, row_blocks)),
        out_shape=jax.ShapeDtypeStruct(front.shape, jnp.float32),
        in_specs=[pl.BlockSpec(memory_space=SMEM)] + [pl.BlockSpec(memory_space=VMEM)] * 4,
        out_specs=pl.BlockSpec(memory_space=VMEM),
        compiler_params=LIMIT,
        name="update_front",
    )(where, front, inverse_t, window, column)


def after_kernel(*refs):
    pass


def after(value, *others):
    return pl.pallas_call(
        after_kernel,
        out_shape=jax.ShapeDtypeStruct(value.shape, value.dtype),
        in_specs=[pl.BlockSpec(memory_space=ANY)] * (1 + len(others)),
        out_specs=pl.BlockSpec(memory_space=ANY),
        input_output_aliases={0: 0},
        name="after",
    )(value, *others)


def per_device(front, child_tiles, child_rows, child_cols):
    row_count = lax.axis_size("row")
    col_count = lax.axis_size("col")
    row_index = lax.axis_index("row")
    col_index = lax.axis_index("col")
    both = ("row", "col")
    row_blocks, size, col_blocks = (front.shape[0], front.shape[2], front.shape[3])
    rows = size // col_count
    devices = row_count * col_count
    flat_front = front.reshape(row_blocks * size * col_blocks, size)
    tiles = child_tiles.reshape(-1, col_count, rows, size)
    slot, panel_tiles, message, local = send_tables(
        child_rows.reshape(-1),
        child_cols.reshape(-1),
        row_index,
        col_index,
        row_count,
        col_count,
        size,
    )
    first, second = pack(slot, tiles, devices)
    first = lax.all_to_all(first, both, split_axis=0, concat_axis=0, tiled=True)
    own = list(split_front(local, flat_front, tiles, row_blocks))
    for k in (7, 2, 4, 5, 3):
        own[k] = lax.ppermute(own[k], "col", [(0, k)])
    sliced = pack_panel(panel_tiles, local, message, tiles, flat_front, row_count, col_count)
    sliced = after(sliced, first)
    sliced = lax.all_to_all(sliced, both, split_axis=0, concat_axis=0, tiled=True)
    message = sliced[:, -1, 0, : 2 * CAP].astype(jnp.int32)
    main, part = ([message[:, h * CAP + s] for s in range(CAP)] for h in range(2))
    windows, column = sum_slices(part, sliced, row_count, row_blocks)
    for k in (1, 6):
        own[k] = lax.ppermute(after(own[k], column), "col", [(0, k)])
    windows = lax.all_to_all(windows, "row", split_axis=0, concat_axis=0, tiled=True)
    column = spread(local, windows, column, own)
    column = lax.all_to_all(column, "col", split_axis=0, concat_axis=0, tiled=True)
    second = lax.all_to_all(
        after(second, column), both, split_axis=0, concat_axis=0, tiled=True
    )
    corner = column[:, row_blocks].reshape(size, size)
    window = jnp.swapaxes(column[:, row_blocks + 1 :], 0, 1).reshape(-1, size)
    factor = jnp.linalg.cholesky(0.5 * (corner + corner.T))
    inverse = jax.scipy.linalg.solve_triangular(
        factor, jnp.eye(size, dtype=jnp.float32), lower=True
    )
    total = add_tiles(main[0], flat_front, first)
    base = update_front(local, total, inverse.T, window, column, row_count, row_blocks)
    return add_tiles(main[1], base, second).reshape(front.shape)


def solution(mesh):
    in_specs = (
        P(None, "row", None, None, "col", None),
        P("row", "col", None, None, None),
        P("row", "col", None),
        P("row", "col", None),
    )
    out_specs = P(None, "row", None, None, "col", None)
    return jax.shard_map(
        per_device, mesh=mesh, in_specs=in_specs, out_specs=out_specs, check_vma=False
    )
```

```python
import functools

import jax
import jax.numpy as jnp
from jax import lax
from jax.experimental import pallas as pl
from jax.experimental.pallas import tpu as pltpu
from jax.sharding import PartitionSpec as P

CAP = 2
HIGH = lax.Precision.HIGHEST
SMEM = pltpu.SMEM
VMEM = pltpu.VMEM
ANY = pl.ANY
LIMIT = pltpu.CompilerParams(vmem_limit_bytes=58 << 20)


def send_tables(parent_rows, parent_cols, row_index, col_index, row_count, col_count, size):
    tiles = parent_rows.shape[0]
    order = jnp.arange(tiles, dtype=jnp.int32)
    row_of = parent_rows % row_count
    owners = row_of * col_count + parent_cols % col_count
    same = (owners[:, None] == owners[None, :]) & (order[None, :] < order[:, None])
    slot = owners * CAP + jnp.sum(same.astype(jnp.int32), axis=1)
    block = parent_rows // row_count
    place = block * (2 * size) + parent_cols // col_count
    panel = parent_cols == 0
    wanted = jnp.arange(row_count * CAP, dtype=jnp.int32)[:, None]
    chosen = panel & (slot == wanted // CAP * (col_count * CAP) + wanted % CAP)
    panel_tiles = jnp.sum(jnp.where(chosen, order, 0), axis=1)
    dest = jnp.arange(row_count * col_count, dtype=jnp.int32)[:, None, None]
    part = jnp.arange(2 * CAP, dtype=jnp.int32)[None, :, None]
    in_main = (part < CAP) & (slot == dest * CAP + part) & ~panel
    dest_row = dest // col_count
    local = (dest_row == row_index) & (col_index == 0)
    in_panel = (part >= CAP) & (slot == dest_row * (col_count * CAP) + part - CAP) & panel
    value = jnp.where(in_main, place + 1, 0) + jnp.where(in_panel & ~local, block + 1, 0)
    message = jnp.sum(value, axis=2) - 1
    message = jnp.where(local[..., 0] & (part[..., 0] == CAP), 0, message)
    mine = jnp.arange(CAP, dtype=jnp.int32)[:, None]
    stays = panel & (col_index == 0) & (slot == row_index * (col_count * CAP) + mine)
    stay_tiles = jnp.sum(jnp.where(stays, order, 0), axis=1)
    stay_blocks = jnp.sum(jnp.where(stays, block + 1, 0), axis=1) - 1
    where = jnp.stack([row_index, col_index]).astype(jnp.int32)
    return slot, panel_tiles, message, jnp.concatenate([where, stay_tiles, stay_blocks])


def pack_kernel(
    chunks, slot, panel_tiles, local, places, tiles, cut_tiles, front, first, second, *scratch
):
    held, cut, corner, block, load_sem, cut_sem, corner_sem, main_sem, sem = scratch
    count, whole = held.shape[:2]
    step = count // chunks
    size = block.shape[-1]
    slots, groups = cut.shape[0], block.shape[1]
    row_count, col_count = first.shape[:2]
    main_part = pl.ds(CAP * groups, whole)

    def load(i):
        part = pl.ds(i * step, step)
        return pltpu.make_async_copy(tiles.at[part], held.at[part], load_sem.at[i])

    load_corner = pltpu.make_async_copy(front.at[pl.ds(0, 2 * size)], corner, corner_sem)
    loads = [
        pltpu.make_async_copy(cut_tiles.at[panel_tiles[i]], cut.at[i], cut_sem.at[i])
        for i in range(slots)
    ]
    for i in range(chunks):
        load(i).start()
    load_corner.start()
    for copy in loads:
        copy.start()
    all_places = pltpu.make_async_copy(places, first.at[:, :, CAP * groups + whole], sem)
    all_places.start()
    for i in range(chunks):
        load(i).wait()

        def send(k, carry):
            where = slot[k]
            owner = where // CAP

            @pl.when(where % CAP == 0)
            def _():
                pltpu.make_async_copy(
                    held.at[k], first.at[owner // col_count, owner % col_count, main_part], main_sem
                ).start()

            @pl.when(where % CAP == 1)
            def _():
                pltpu.make_async_copy(held.at[k], second.at[owner], main_sem).start()

            return carry

        lax.fori_loop(i * step, (i + 1) * step, send, 0)
    load_corner.wait()
    block[...] = corner[pl.ds(0, size, stride=2), :].reshape(block.shape)
    for r in range(row_count):
        for s in range(CAP):
            loads[r * CAP + s].wait()

        @pl.when((local[0] == r) & (local[1] == 0))
        def _():
            for s in range(CAP):

                @pl.when(local[2 + CAP + s] == 0)
                def _():
                    block[...] += cut[r * CAP + s]

            cut[r * CAP] = block[...]

        for s in range(CAP):
            pltpu.make_async_copy(
                cut.at[r * CAP + s], first.at[r, :, pl.ds(s * groups, groups)], sem
            ).start()
    pltpu.make_async_copy(held, second, main_sem).wait()
    panel_part = first.at[:, :, pl.ds(0, CAP * groups + 1)]
    pltpu.make_async_copy(panel_part, panel_part, sem).wait()


def pack(slot, panel_tiles, local, message, tiles, front, row_count, col_count):
    count, size = tiles.shape[0], tiles.shape[-1]
    groups = size // 8 // col_count
    whole = size // 8
    slots = row_count * CAP
    chunks = 8
    view = (col_count, groups, 8, size)
    places = jnp.pad(
        message.astype(jnp.float32)[:, None, :], ((0, 0), (0, 7), (0, size - message.shape[1]))
    ).reshape(row_count, col_count, 8, size)
    first, second = pl.pallas_call(
        functools.partial(pack_kernel, chunks),
        out_shape=[
            jax.ShapeDtypeStruct(
                (row_count, col_count, CAP * groups + whole + 1, 8, size), jnp.float32
            ),
            jax.ShapeDtypeStruct((row_count * col_count, whole, 8, size), jnp.float32),
        ],
        in_specs=[pl.BlockSpec(memory_space=SMEM)] * 3
        + [pl.BlockSpec(memory_space=VMEM)]
        + [pl.BlockSpec(memory_space=ANY)] * 3,
        out_specs=[pl.BlockSpec(memory_space=ANY)] * 2,
        scratch_shapes=[
            VMEM((count, whole, 8, size), jnp.float32),
            VMEM((slots,) + view, jnp.float32),
            VMEM((2 * size, size), jnp.float32),
            VMEM(view, jnp.float32),
            pltpu.SemaphoreType.DMA((chunks,)),
            pltpu.SemaphoreType.DMA((slots,)),
            pltpu.SemaphoreType.DMA,
            pltpu.SemaphoreType.DMA,
            pltpu.SemaphoreType.DMA,
        ],
        compiler_params=LIMIT,
        name="pack",
    )(
        slot,
        panel_tiles,
        local,
        places,
        tiles.reshape(count, whole, 8, size),
        tiles.reshape((count,) + view),
        front,
    )
    return first.reshape((row_count * col_count,) + first.shape[2:]), second


def split_kernel(rows, local, front, tiles, *refs):
    outs, (held, sem) = refs[:-2], refs[-2:]
    col_count = len(outs)
    for s in range(CAP):
        copy = pltpu.make_async_copy(tiles.at[local[2 + s]], held.at[s], sem.at[s])
        copy.start()
        copy.wait()

    def block(a, carry):
        for q in range(col_count):
            start = (a * col_count + q) * rows * 2
            outs[q][a] = front[pl.ds(start, rows, stride=2), :]
        return carry

    lax.fori_loop(0, outs[0].shape[0], block, 0, unroll=4)
    for s in range(CAP):
        place = local[2 + CAP + s]

        @pl.when(place >= 0)
        def _():
            for q in range(col_count):
                outs[q][place] += held[s, q]

    for q in range(col_count):
        outs[q][0] = jnp.zeros_like(outs[q][0])


def split_front(local, front, tiles, row_blocks):
    col_count, rows, size = tiles.shape[1:]
    return pl.pallas_call(
        functools.partial(split_kernel, rows),
        out_shape=[jax.ShapeDtypeStruct((row_blocks, rows, size), jnp.float32)] * col_count,
        in_specs=[
            pl.BlockSpec(memory_space=SMEM),
            pl.BlockSpec(memory_space=VMEM),
            pl.BlockSpec(memory_space=ANY),
        ],
        out_specs=[pl.BlockSpec(memory_space=VMEM)] * col_count,
        scratch_shapes=[
            VMEM((CAP, col_count, rows, size), jnp.float32),
            pltpu.SemaphoreType.DMA((CAP,)),
        ],
        compiler_params=LIMIT,
        name="split_front",
    )(local, front, tiles)


def slices_kernel(row_blocks, part_0, part_1, arrived, windows, column, total):
    total[...] = jnp.zeros_like(total)
    parts = (part_0, part_1)
    groups = arrived.shape[1] // CAP
    rows, size = total.shape[1:]

    def source(d, carry):
        for s in range(CAP):
            block = parts[s][d]
            piece = arrived[d, pl.ds(s * groups, groups)].reshape(rows, size)
            total[jnp.where(block < 0, row_blocks, block)] += piece
        return carry

    lax.fori_loop(0, arrived.shape[0], source, 0, unroll=8)
    column[...] = total[pl.ds(0, row_blocks)]
    windows[...] = jnp.broadcast_to(total[0][None], windows.shape)


def sum_slices(parts, arrived, row_count, row_blocks, groups):
    devices, _, _, size = arrived.shape
    rows = groups * 8
    outs = [
        jax.ShapeDtypeStruct((row_count, rows, size), jnp.float32),
        jax.ShapeDtypeStruct((row_blocks, rows, size), jnp.float32),
    ]
    return pl.pallas_call(
        functools.partial(slices_kernel, row_blocks),
        out_shape=outs,
        grid=(1,),
        in_specs=[pl.BlockSpec(memory_space=SMEM)] * 2
        + [pl.BlockSpec((devices, CAP * groups, 8, size), lambda i: (0, 0, 0, 0))],
        out_specs=[pl.BlockSpec(out.shape, lambda i: (0, 0, 0)) for out in outs],
        scratch_shapes=[VMEM((row_blocks + 1, rows, size), jnp.float32)],
        compiler_params=LIMIT,
        name="sum_slices",
    )(*parts, arrived)


def spread_kernel(local, windows, column, *refs):
    own, (out, held, load_sem, sem, few_sem) = refs[:-5], refs[-5:]
    col_count = len(own)
    row_blocks = column.shape[0]
    few = []
    for k in range(col_count):
        for i, j in enumerate((0, *range(k, windows.shape[0], col_count))):
            few.append(
                pltpu.make_async_copy(
                    windows.at[j], out.at[k, row_blocks + i], few_sem.at[len(few)]
                )
            )
    for copy in few:
        copy.start()
    for k in range(col_count):

        @pl.when(local[1] == k)
        def _():
            load = pltpu.make_async_copy(own[k], held, load_sem)
            load.start()
            load.wait()

    held[...] += column[...]
    copies = [
        pltpu.make_async_copy(held, out.at[k, pl.ds(0, row_blocks)], sem.at[k])
        for k in range(col_count)
    ]
    for copy in copies:
        copy.start()
    for copy in copies + few:
        copy.wait()


def spread(local, windows, column, own):
    row_blocks, rows, size = column.shape
    col_count = len(own)
    extra = 1 + windows.shape[0] // col_count
    out = jax.ShapeDtypeStruct((col_count, row_blocks + extra, rows, size), jnp.float32)
    return pl.pallas_call(
        spread_kernel,
        out_shape=out,
        in_specs=[pl.BlockSpec(memory_space=SMEM)]
        + [pl.BlockSpec(memory_space=VMEM)] * 2
        + [pl.BlockSpec(memory_space=ANY)] * col_count,
        out_specs=pl.BlockSpec(memory_space=ANY),
        scratch_shapes=[
            VMEM(column.shape, jnp.float32),
            pltpu.SemaphoreType.DMA,
            pltpu.SemaphoreType.DMA((col_count,)),
            pltpu.SemaphoreType.DMA((col_count * extra,)),
        ],
        compiler_params=LIMIT,
        name="spread",
    )(local, windows, column, *own)


def add_kernel(chunks, skip, places, base, tiles, out, total, held, base_sem, tile_sem):
    slots, parts, rows, size = held.shape
    step = slots // chunks
    last = base.shape[0]
    whole = pl.ds(0, last)
    load_base = pltpu.make_async_copy(base, total.at[whole], base_sem)
    load_base.start()

    def load(i):
        some = pl.ds(i * step, step)
        inner = pl.ds(skip, parts)
        return pltpu.make_async_copy(tiles.at[some, inner], held.at[some], tile_sem.at[i])

    for i in range(chunks):
        load(i).start()
    load_base.wait()

    def add(j, carry):
        place = places[j]
        start = jnp.where(place < 0, last, place)
        total[pl.ds(start, size, stride=2), :] += held[j].reshape(size, size)
        return carry

    for i in range(chunks):
        load(i).wait()
        lax.fori_loop(i * step, (i + 1) * step, add, 0, unroll=4)
    store = pltpu.make_async_copy(total.at[whole], out, base_sem)
    store.start()
    store.wait()


def add_tiles(places, base, tiles, skip):
    slots, _, rows, size = tiles.shape
    chunks = 8
    return pl.pallas_call(
        functools.partial(add_kernel, chunks, skip),
        out_shape=jax.ShapeDtypeStruct(base.shape, jnp.float32),
        in_specs=[
            pl.BlockSpec(memory_space=SMEM),
            pl.BlockSpec(memory_space=ANY),
            pl.BlockSpec(memory_space=ANY),
        ],
        out_specs=pl.BlockSpec(memory_space=ANY),
        scratch_shapes=[
            VMEM((base.shape[0] + 2 * size, size), jnp.float32),
            VMEM((slots, size // rows, rows, size), jnp.float32),
            pltpu.SemaphoreType.DMA,
            pltpu.SemaphoreType.DMA((chunks,)),
        ],
        compiler_params=LIMIT,
        name="add_tiles",
    )(places, base, tiles)


def update_kernel(shape, where, front, inverse_t, window, column, base):
    row_count, row_blocks = shape
    row_index, col_index = where[0], where[1]
    size = inverse_t.shape[0]
    held = jnp.dot(
        window[...], inverse_t[...], precision=HIGH, preferred_element_type=jnp.float32
    )
    contract = (((1,), (1,)), ((), ()))

    def block(a, carry):
        rows = jnp.dot(
            column[:, a].reshape(size, size),
            inverse_t[...],
            precision=HIGH,
            preferred_element_type=jnp.float32,
        )
        update = lax.dot_general(
            rows, held, contract, precision=HIGH, preferred_element_type=jnp.float32
        )
        below = a * row_count + row_index > 0
        update = jnp.where(below, update, jnp.zeros_like(update))
        even = pl.ds(a * 2 * size, size, stride=2)
        odd = pl.ds(a * 2 * size + 1, size, stride=2)
        base[even, :] = jnp.where(col_index == 0, rows, front[even, :] - update[:, :size])
        base[odd, :] = front[odd, :] - update[:, size:]
        return carry

    lax.fori_loop(0, row_blocks, block, 0)


def update_front(where, front, inverse_t, window, column, row_count, row_blocks):
    return pl.pallas_call(
        functools.partial(update_kernel, (row_count, row_blocks)),
        out_shape=jax.ShapeDtypeStruct(front.shape, jnp.float32),
        in_specs=[pl.BlockSpec(memory_space=SMEM)] + [pl.BlockSpec(memory_space=VMEM)] * 4,
        out_specs=pl.BlockSpec(memory_space=VMEM),
        compiler_params=LIMIT,
        name="update_front",
    )(where, front, inverse_t, window, column)


def after_kernel(*refs):
    pass


def after(value, *others):
    return pl.pallas_call(
        after_kernel,
        out_shape=jax.ShapeDtypeStruct(value.shape, value.dtype),
        in_specs=[pl.BlockSpec(memory_space=ANY)] * (1 + len(others)),
        out_specs=pl.BlockSpec(memory_space=ANY),
        input_output_aliases={0: 0},
        name="after",
    )(value, *others)


def per_device(front, child_tiles, child_rows, child_cols):
    row_count = lax.axis_size("row")
    col_count = lax.axis_size("col")
    row_index = lax.axis_index("row")
    col_index = lax.axis_index("col")
    both = ("row", "col")
    row_blocks, size, col_blocks = (front.shape[0], front.shape[2], front.shape[3])
    rows = size // col_count
    devices = row_count * col_count
    flat_front = front.reshape(row_blocks * size * col_blocks, size)
    tiles = child_tiles.reshape(-1, col_count, rows, size)
    slot, panel_tiles, message, local = send_tables(
        child_rows.reshape(-1),
        child_cols.reshape(-1),
        row_index,
        col_index,
        row_count,
        col_count,
        size,
    )
    first, second = pack(
        slot, panel_tiles, local, message, tiles, flat_front, row_count, col_count
    )
    first = lax.all_to_all(first, both, split_axis=0, concat_axis=0, tiled=True)
    own = list(split_front(local, flat_front, tiles, row_blocks))
    for k in (7, 2, 4, 5, 3, 1, 6):
        own[k] = lax.ppermute(own[k], "col", [(0, k)])
    message = first[:, -1, 0, : 2 * CAP].astype(jnp.int32)
    main, part = ([message[:, h * CAP + s] for s in range(CAP)] for h in range(2))
    groups = rows // 8
    windows, column = sum_slices(part, first, row_count, row_blocks, groups)
    windows = lax.all_to_all(windows, "row", split_axis=0, concat_axis=0, tiled=True)
    column = spread(local, windows, column, own)
    column = lax.all_to_all(column, "col", split_axis=0, concat_axis=0, tiled=True)
    second = lax.all_to_all(
        after(second, column), both, split_axis=0, concat_axis=0, tiled=True
    )
    corner = column[:, row_blocks].reshape(size, size)
    window = jnp.swapaxes(column[:, row_blocks + 1 :], 0, 1).reshape(-1, size)
    factor = jnp.linalg.cholesky(0.5 * (corner + corner.T))
    inverse = jax.scipy.linalg.solve_triangular(
        factor, jnp.eye(size, dtype=jnp.float32), lower=True
    )
    total = add_tiles(main[0], flat_front, first, CAP * groups)
    base = update_front(local, total, inverse.T, window, column, row_count, row_blocks)
    return add_tiles(main[1], base, second, 0).reshape(front.shape)


def solution(mesh):
    in_specs = (
        P(None, "row", None, None, "col", None),
        P("row", "col", None, None, None),
        P("row", "col", None),
        P("row", "col", None),
    )
    out_specs = P(None, "row", None, None, "col", None)
    return jax.shard_map(
        per_device, mesh=mesh, in_specs=in_specs, out_specs=out_specs, check_vma=False
    )
```

```python
import functools

import jax
import jax.numpy as jnp
from jax import lax
from jax.experimental import pallas as pl
from jax.experimental.pallas import tpu as pltpu
from jax.sharding import PartitionSpec as P

CAP = 2
HIGH = lax.Precision.HIGHEST
SMEM = pltpu.SMEM
VMEM = pltpu.VMEM
ANY = pl.ANY
LIMIT = pltpu.CompilerParams(vmem_limit_bytes=58 << 20)


def send_tables(parent_rows, parent_cols, row_index, col_index, row_count, col_count, size):
    tiles = parent_rows.shape[0]
    order = jnp.arange(tiles, dtype=jnp.int32)
    row_of = parent_rows % row_count
    owners = row_of * col_count + parent_cols % col_count
    same = (owners[:, None] == owners[None, :]) & (order[None, :] < order[:, None])
    slot = owners * CAP + jnp.sum(same.astype(jnp.int32), axis=1)
    block = parent_rows // row_count
    place = block * (2 * size) + parent_cols // col_count
    panel = parent_cols == 0
    wanted = jnp.arange(row_count * CAP, dtype=jnp.int32)[:, None]
    chosen = panel & (slot == wanted // CAP * (col_count * CAP) + wanted % CAP)
    panel_tiles = jnp.sum(jnp.where(chosen, order, 0), axis=1)
    dest = jnp.arange(row_count * col_count, dtype=jnp.int32)[:, None, None]
    part = jnp.arange(2 * CAP, dtype=jnp.int32)[None, :, None]
    in_main = (part < CAP) & (slot == dest * CAP + part) & ~panel
    dest_row = dest // col_count
    local = (dest_row == row_index) & (col_index == 0)
    in_panel = (part >= CAP) & (slot == dest_row * (col_count * CAP) + part - CAP) & panel
    value = jnp.where(in_main, place + 1, 0) + jnp.where(in_panel & ~local, block + 1, 0)
    message = jnp.sum(value, axis=2) - 1
    message = jnp.where(local[..., 0] & (part[..., 0] == CAP), 0, message)
    mine = jnp.arange(CAP, dtype=jnp.int32)[:, None]
    stays = panel & (col_index == 0) & (slot == row_index * (col_count * CAP) + mine)
    stay_tiles = jnp.sum(jnp.where(stays, order, 0), axis=1)
    stay_blocks = jnp.sum(jnp.where(stays, block + 1, 0), axis=1) - 1
    where = jnp.stack([row_index, col_index]).astype(jnp.int32)
    return slot, panel_tiles, message, jnp.concatenate([where, stay_tiles, stay_blocks])


def pack_panel_kernel(
    panel_tiles, local, places, tiles, front, out, held, corner, block, load_sem, corner_sem, sem
):
    size = block.shape[-1]
    slots = held.shape[0]
    row_count = out.shape[0]
    groups = block.shape[1]
    pltpu.make_async_copy(places, out.at[:, :, CAP * groups], sem).start()
    load_corner = pltpu.make_async_copy(front.at[pl.ds(0, 2 * size)], corner, corner_sem)
    load_corner.start()
    loads = [
        pltpu.make_async_copy(tiles.at[panel_tiles[i]], held.at[i], load_sem.at[i])
        for i in range(slots)
    ]
    for load in loads:
        load.start()
    load_corner.wait()
    block[...] = corner[pl.ds(0, size, stride=2), :].reshape(block.shape)
    for r in range(row_count):
        mine = (local[0] == r) & (local[1] == 0)
        for s in range(CAP):
            loads[r * CAP + s].wait()

        @pl.when(mine)
        def _():
            for s in range(CAP):

                @pl.when(local[2 + CAP + s] == 0)
                def _():
                    block[...] += held[r * CAP + s]

            held[r * CAP] = block[...]

        for s in range(CAP):
            pltpu.make_async_copy(
                held.at[r * CAP + s], out.at[r, :, pl.ds(s * groups, groups)], sem
            ).start()
    pltpu.make_async_copy(out, out, sem).wait()


def pack_panel(panel_tiles, local, message, tiles, front, row_count, col_count):
    size = tiles.shape[-1]
    rows = size // col_count
    groups = rows // 8
    slots = row_count * CAP
    view = (col_count, groups, 8, size)
    places = jnp.pad(
        message.astype(jnp.float32)[:, None, :], ((0, 0), (0, 7), (0, size - message.shape[1]))
    ).reshape(row_count, col_count, 8, size)
    sent = pl.pallas_call(
        pack_panel_kernel,
        out_shape=jax.ShapeDtypeStruct(
            (row_count, col_count, CAP * groups + 1, 8, size), jnp.float32
        ),
        in_specs=[pl.BlockSpec(memory_space=SMEM)] * 2
        + [pl.BlockSpec(memory_space=VMEM)]
        + [pl.BlockSpec(memory_space=ANY)] * 2,
        out_specs=pl.BlockSpec(memory_space=ANY),
        scratch_shapes=[
            VMEM((slots,) + view, jnp.float32),
            VMEM((2 * size, size), jnp.float32),
            VMEM(view, jnp.float32),
            pltpu.SemaphoreType.DMA((slots,)),
            pltpu.SemaphoreType.DMA,
            pltpu.SemaphoreType.DMA,
        ],
        compiler_params=LIMIT,
        name="pack_panel",
    )(panel_tiles, local, places, tiles.reshape((-1,) + view), front)
    return sent.reshape((row_count * col_count,) + sent.shape[2:])


def pack_kernel(chunks, slot, tiles, first, second, held, load_sem, main_sem):
    count = tiles.shape[0]
    step = count // chunks

    def load(i):
        part = pl.ds(i * step, step)
        return pltpu.make_async_copy(tiles.at[part], held.at[part], load_sem.at[i])

    for i in range(chunks):
        load(i).start()
    for i in range(chunks):
        load(i).wait()

        def send(k, carry):
            where = slot[k]
            owner = where // CAP

            @pl.when(where % CAP == 0)
            def _():
                pltpu.make_async_copy(held.at[k], first.at[owner], main_sem).start()

            @pl.when(where % CAP == 1)
            def _():
                pltpu.make_async_copy(held.at[k], second.at[owner], main_sem).start()

            return carry

        lax.fori_loop(i * step, (i + 1) * step, send, 0)
    pltpu.make_async_copy(held, second, main_sem).wait()


def pack(slot, tiles, devices):
    chunks = 8
    out = jax.ShapeDtypeStruct((devices,) + tiles.shape[1:], jnp.float32)
    return pl.pallas_call(
        functools.partial(pack_kernel, chunks),
        out_shape=[out, out],
        in_specs=[pl.BlockSpec(memory_space=SMEM), pl.BlockSpec(memory_space=ANY)],
        out_specs=[pl.BlockSpec(memory_space=ANY)] * 2,
        scratch_shapes=[
            VMEM(tiles.shape, jnp.float32),
            pltpu.SemaphoreType.DMA((chunks,)),
            pltpu.SemaphoreType.DMA,
        ],
        compiler_params=LIMIT,
        name="pack",
    )(slot, tiles)


def split_kernel(rows, local, front, tiles, *refs):
    outs, (held, sem) = refs[:-2], refs[-2:]
    col_count = len(outs)
    for s in range(CAP):
        copy = pltpu.make_async_copy(tiles.at[local[2 + s]], held.at[s], sem.at[s])
        copy.start()
        copy.wait()

    def block(a, carry):
        for q in range(col_count):
            start = (a * col_count + q) * rows * 2
            outs[q][a] = front[pl.ds(start, rows, stride=2), :]
        return carry

    lax.fori_loop(0, outs[0].shape[0], block, 0, unroll=4)
    for s in range(CAP):
        place = local[2 + CAP + s]

        @pl.when(place >= 0)
        def _():
            for q in range(col_count):
                outs[q][place] += held[s, q]

    for q in range(col_count):
        outs[q][0] = jnp.zeros_like(outs[q][0])


def split_front(local, front, tiles, row_blocks):
    col_count, rows, size = tiles.shape[1:]
    return pl.pallas_call(
        functools.partial(split_kernel, rows),
        out_shape=[jax.ShapeDtypeStruct((row_blocks, rows, size), jnp.float32)] * col_count,
        in_specs=[
            pl.BlockSpec(memory_space=SMEM),
            pl.BlockSpec(memory_space=VMEM),
            pl.BlockSpec(memory_space=ANY),
        ],
        out_specs=[pl.BlockSpec(memory_space=VMEM)] * col_count,
        scratch_shapes=[
            VMEM((CAP, col_count, rows, size), jnp.float32),
            pltpu.SemaphoreType.DMA((CAP,)),
        ],
        compiler_params=LIMIT,
        name="split_front",
    )(local, front, tiles)


def slices_kernel(row_blocks, part_0, part_1, arrived, windows, column, total):
    total[...] = jnp.zeros_like(total)
    parts = (part_0, part_1)
    groups = arrived.shape[1] // CAP
    rows, size = total.shape[1:]

    def source(d, carry):
        for s in range(CAP):
            block = parts[s][d]
            piece = arrived[d, pl.ds(s * groups, groups)].reshape(rows, size)
            total[jnp.where(block < 0, row_blocks, block)] += piece
        return carry

    lax.fori_loop(0, arrived.shape[0], source, 0, unroll=8)
    column[...] = total[pl.ds(0, row_blocks)]
    windows[...] = jnp.broadcast_to(total[0][None], windows.shape)


def sum_slices(parts, arrived, row_count, row_blocks):
    devices, groups, _, size = arrived.shape
    groups = groups // CAP
    rows = groups * 8
    outs = [
        jax.ShapeDtypeStruct((row_count, rows, size), jnp.float32),
        jax.ShapeDtypeStruct((row_blocks, rows, size), jnp.float32),
    ]
    return pl.pallas_call(
        functools.partial(slices_kernel, row_blocks),
        out_shape=outs,
        grid=(1,),
        in_specs=[pl.BlockSpec(memory_space=SMEM)] * 2
        + [pl.BlockSpec((devices, CAP * groups, 8, size), lambda i: (0, 0, 0, 0))],
        out_specs=[pl.BlockSpec(out.shape, lambda i: (0, 0, 0)) for out in outs],
        scratch_shapes=[VMEM((row_blocks + 1, rows, size), jnp.float32)],
        compiler_params=LIMIT,
        name="sum_slices",
    )(*parts, arrived)


def spread_kernel(local, windows, column, *refs):
    own, (out, held, load_sem, sem, few_sem) = refs[:-5], refs[-5:]
    col_count = len(own)
    row_blocks = column.shape[0]
    few = []
    for k in range(col_count):
        for i, j in enumerate((0, *range(k, windows.shape[0], col_count))):
            few.append(
                pltpu.make_async_copy(
                    windows.at[j], out.at[k, row_blocks + i], few_sem.at[len(few)]
                )
            )
    for copy in few:
        copy.start()
    for k in range(col_count):

        @pl.when(local[1] == k)
        def _():
            load = pltpu.make_async_copy(own[k], held, load_sem)
            load.start()
            load.wait()

    held[...] += column[...]
    copies = [
        pltpu.make_async_copy(held, out.at[k, pl.ds(0, row_blocks)], sem.at[k])
        for k in range(col_count)
    ]
    for copy in copies:
        copy.start()
    for copy in copies + few:
        copy.wait()


def spread(local, windows, column, own):
    row_blocks, rows, size = column.shape
    col_count = len(own)
    extra = 1 + windows.shape[0] // col_count
    out = jax.ShapeDtypeStruct((col_count, row_blocks + extra, rows, size), jnp.float32)
    return pl.pallas_call(
        spread_kernel,
        out_shape=out,
        in_specs=[pl.BlockSpec(memory_space=SMEM)]
        + [pl.BlockSpec(memory_space=VMEM)] * 2
        + [pl.BlockSpec(memory_space=ANY)] * col_count,
        out_specs=pl.BlockSpec(memory_space=ANY),
        scratch_shapes=[
            VMEM(column.shape, jnp.float32),
            pltpu.SemaphoreType.DMA,
            pltpu.SemaphoreType.DMA((col_count,)),
            pltpu.SemaphoreType.DMA((col_count * extra,)),
        ],
        compiler_params=LIMIT,
        name="spread",
    )(local, windows, column, *own)


def add_kernel(chunks, places, base, tiles, out, total, held, base_sem, tile_sem):
    slots, parts, rows, size = held.shape
    step = slots // chunks
    last = base.shape[0]
    whole = pl.ds(0, last)
    load_base = pltpu.make_async_copy(base, total.at[whole], base_sem)
    load_base.start()

    def load(i):
        some = pl.ds(i * step, step)
        return pltpu.make_async_copy(tiles.at[some], held.at[some], tile_sem.at[i])

    for i in range(chunks):
        load(i).start()
    load_base.wait()

    def add(j, carry):
        place = places[j]
        start = jnp.where(place < 0, last, place)
        total[pl.ds(start, size, stride=2), :] += held[j].reshape(size, size)
        return carry

    for i in range(chunks):
        load(i).wait()
        lax.fori_loop(i * step, (i + 1) * step, add, 0, unroll=4)
    store = pltpu.make_async_copy(total.at[whole], out, base_sem)
    store.start()
    store.wait()


def add_tiles(places, base, tiles):
    slots, parts, rows, size = tiles.shape
    chunks = 8
    return pl.pallas_call(
        functools.partial(add_kernel, chunks),
        out_shape=jax.ShapeDtypeStruct(base.shape, jnp.float32),
        in_specs=[
            pl.BlockSpec(memory_space=SMEM),
            pl.BlockSpec(memory_space=ANY),
            pl.BlockSpec(memory_space=ANY),
        ],
        out_specs=pl.BlockSpec(memory_space=ANY),
        scratch_shapes=[
            VMEM((base.shape[0] + 2 * size, size), jnp.float32),
            VMEM(tiles.shape, jnp.float32),
            pltpu.SemaphoreType.DMA,
            pltpu.SemaphoreType.DMA((chunks,)),
        ],
        compiler_params=LIMIT,
        name="add_tiles",
    )(places, base, tiles)


def update_kernel(shape, where, front, inverse_t, window, column, base):
    row_count, row_blocks = shape
    row_index, col_index = where[0], where[1]
    size = inverse_t.shape[0]
    held = jnp.dot(
        window[...], inverse_t[...], precision=HIGH, preferred_element_type=jnp.float32
    )
    contract = (((1,), (1,)), ((), ()))

    def block(a, carry):
        rows = jnp.dot(
            column[:, a].reshape(size, size),
            inverse_t[...],
            precision=HIGH,
            preferred_element_type=jnp.float32,
        )
        update = lax.dot_general(
            rows, held, contract, precision=HIGH, preferred_element_type=jnp.float32
        )
        below = a * row_count + row_index > 0
        update = jnp.where(below, update, jnp.zeros_like(update))
        even = pl.ds(a * 2 * size, size, stride=2)
        odd = pl.ds(a * 2 * size + 1, size, stride=2)
        base[even, :] = jnp.where(col_index == 0, rows, front[even, :] - update[:, :size])
        base[odd, :] = front[odd, :] - update[:, size:]
        return carry

    lax.fori_loop(0, row_blocks, block, 0)


def update_front(where, front, inverse_t, window, column, row_count, row_blocks):
    return pl.pallas_call(
        functools.partial(update_kernel, (row_count, row_blocks)),
        out_shape=jax.ShapeDtypeStruct(front.shape, jnp.float32),
        in_specs=[pl.BlockSpec(memory_space=SMEM)] + [pl.BlockSpec(memory_space=VMEM)] * 4,
        out_specs=pl.BlockSpec(memory_space=VMEM),
        compiler_params=LIMIT,
        name="update_front",
    )(where, front, inverse_t, window, column)


def after_kernel(*refs):
    pass


def after(value, *others):
    return pl.pallas_call(
        after_kernel,
        out_shape=jax.ShapeDtypeStruct(value.shape, value.dtype),
        in_specs=[pl.BlockSpec(memory_space=ANY)] * (1 + len(others)),
        out_specs=pl.BlockSpec(memory_space=ANY),
        input_output_aliases={0: 0},
        name="after",
    )(value, *others)


def per_device(front, child_tiles, child_rows, child_cols):
    row_count = lax.axis_size("row")
    col_count = lax.axis_size("col")
    row_index = lax.axis_index("row")
    col_index = lax.axis_index("col")
    both = ("row", "col")
    row_blocks, size, col_blocks = (front.shape[0], front.shape[2], front.shape[3])
    rows = size // col_count
    devices = row_count * col_count
    flat_front = front.reshape(row_blocks * size * col_blocks, size)
    tiles = child_tiles.reshape(-1, col_count, rows, size)
    slot, panel_tiles, message, local = send_tables(
        child_rows.reshape(-1),
        child_cols.reshape(-1),
        row_index,
        col_index,
        row_count,
        col_count,
        size,
    )
    first, second = pack(slot, tiles, devices)
    first = lax.all_to_all(first, both, split_axis=0, concat_axis=0, tiled=True)
    own = list(split_front(local, flat_front, tiles, row_blocks))
    for k in (4, 5, 2, 3, 7, 6, 1):
        own[k] = lax.ppermute(own[k], "col", [(0, k)])
    sliced = pack_panel(panel_tiles, local, message, tiles, flat_front, row_count, col_count)
    sliced = after(sliced, first, own[4], own[5])
    sliced = lax.all_to_all(sliced, both, split_axis=0, concat_axis=0, tiled=True)
    message = sliced[:, -1, 0, : 2 * CAP].astype(jnp.int32)
    main, part = ([message[:, h * CAP + s] for s in range(CAP)] for h in range(2))
    windows, column = sum_slices(part, sliced, row_count, row_blocks)
    windows = lax.all_to_all(windows, "row", split_axis=0, concat_axis=0, tiled=True)
    column = spread(local, windows, column, own)
    column = lax.all_to_all(column, "col", split_axis=0, concat_axis=0, tiled=True)
    second = lax.all_to_all(
        after(second, column), both, split_axis=0, concat_axis=0, tiled=True
    )
    corner = column[:, row_blocks].reshape(size, size)
    window = jnp.swapaxes(column[:, row_blocks + 1 :], 0, 1).reshape(-1, size)
    factor = jnp.linalg.cholesky(0.5 * (corner + corner.T))
    inverse = jax.scipy.linalg.solve_triangular(
        factor, jnp.eye(size, dtype=jnp.float32), lower=True
    )
    total = add_tiles(main[0], flat_front, first)
    base = update_front(local, total, inverse.T, window, column, row_count, row_blocks)
    return add_tiles(main[1], base, second).reshape(front.shape)


def solution(mesh):
    in_specs = (
        P(None, "row", None, None, "col", None),
        P("row", "col", None, None, None),
        P("row", "col", None),
        P("row", "col", None),
    )
    out_specs = P(None, "row", None, None, "col", None)
    return jax.shard_map(
        per_device, mesh=mesh, in_specs=in_specs, out_specs=out_specs, check_vma=False
    )
```

```python
import functools

import jax
import jax.numpy as jnp
from jax import lax
from jax.experimental import pallas as pl
from jax.experimental.pallas import tpu as pltpu
from jax.sharding import PartitionSpec as P

CAP = 2
HIGH = lax.Precision.HIGHEST
SMEM = pltpu.SMEM
VMEM = pltpu.VMEM
ANY = pl.ANY
LIMIT = pltpu.CompilerParams(vmem_limit_bytes=58 << 20)


def send_tables(parent_rows, parent_cols, row_index, col_index, row_count, col_count, size):
    tiles = parent_rows.shape[0]
    order = jnp.arange(tiles, dtype=jnp.int32)
    row_of = parent_rows % row_count
    owners = row_of * col_count + parent_cols % col_count
    same = (owners[:, None] == owners[None, :]) & (order[None, :] < order[:, None])
    slot = owners * CAP + jnp.sum(same.astype(jnp.int32), axis=1)
    block = parent_rows // row_count
    place = block * (2 * size) + parent_cols // col_count
    panel = parent_cols == 0
    wanted = jnp.arange(row_count * CAP, dtype=jnp.int32)[:, None]
    chosen = panel & (slot == wanted // CAP * (col_count * CAP) + wanted % CAP)
    panel_tiles = jnp.sum(jnp.where(chosen, order, 0), axis=1)
    dest = jnp.arange(row_count * col_count, dtype=jnp.int32)[:, None, None]
    part = jnp.arange(2 * CAP, dtype=jnp.int32)[None, :, None]
    in_main = (part < CAP) & (slot == dest * CAP + part) & ~panel
    dest_row = dest // col_count
    local = (dest_row == row_index) & (col_index == 0)
    in_panel = (part >= CAP) & (slot == dest_row * (col_count * CAP) + part - CAP) & panel
    value = jnp.where(in_main, place + 1, 0) + jnp.where(in_panel & ~local, block + 1, 0)
    message = jnp.sum(value, axis=2) - 1
    message = jnp.where(local[..., 0] & (part[..., 0] == CAP), 0, message)
    mine = jnp.arange(CAP, dtype=jnp.int32)[:, None]
    stays = panel & (col_index == 0) & (slot == row_index * (col_count * CAP) + mine)
    stay_tiles = jnp.sum(jnp.where(stays, order, 0), axis=1)
    stay_blocks = jnp.sum(jnp.where(stays, block + 1, 0), axis=1) - 1
    where = jnp.stack([row_index, col_index]).astype(jnp.int32)
    return slot, panel_tiles, message, jnp.concatenate([where, stay_tiles, stay_blocks])


def pack_panel_kernel(
    panel_tiles, local, places, tiles, front, out, held, corner, block, load_sem, corner_sem, sem
):
    size = block.shape[-1]
    slots = held.shape[0]
    row_count = out.shape[0]
    groups = block.shape[1]
    pltpu.make_async_copy(places, out.at[:, :, CAP * groups], sem).start()
    load_corner = pltpu.make_async_copy(front.at[pl.ds(0, 2 * size)], corner, corner_sem)
    load_corner.start()
    loads = [
        pltpu.make_async_copy(tiles.at[panel_tiles[i]], held.at[i], load_sem.at[i])
        for i in range(slots)
    ]
    for load in loads:
        load.start()
    load_corner.wait()
    block[...] = corner[pl.ds(0, size, stride=2), :].reshape(block.shape)
    for r in range(row_count):
        mine = (local[0] == r) & (local[1] == 0)
        for s in range(CAP):
            loads[r * CAP + s].wait()

        @pl.when(mine)
        def _():
            for s in range(CAP):

                @pl.when(local[2 + CAP + s] == 0)
                def _():
                    block[...] += held[r * CAP + s]

            held[r * CAP] = block[...]

        for s in range(CAP):
            pltpu.make_async_copy(
                held.at[r * CAP + s], out.at[r, :, pl.ds(s * groups, groups)], sem
            ).start()
    pltpu.make_async_copy(out, out, sem).wait()


def pack_panel(panel_tiles, local, message, tiles, front, row_count, col_count):
    size = tiles.shape[-1]
    rows = size // col_count
    groups = rows // 8
    slots = row_count * CAP
    view = (col_count, groups, 8, size)
    places = jnp.pad(
        message.astype(jnp.float32)[:, None, :], ((0, 0), (0, 7), (0, size - message.shape[1]))
    ).reshape(row_count, col_count, 8, size)
    sent = pl.pallas_call(
        pack_panel_kernel,
        out_shape=jax.ShapeDtypeStruct(
            (row_count, col_count, CAP * groups + 1, 8, size), jnp.float32
        ),
        in_specs=[pl.BlockSpec(memory_space=SMEM)] * 2
        + [pl.BlockSpec(memory_space=VMEM)]
        + [pl.BlockSpec(memory_space=ANY)] * 2,
        out_specs=pl.BlockSpec(memory_space=ANY),
        scratch_shapes=[
            VMEM((slots,) + view, jnp.float32),
            VMEM((2 * size, size), jnp.float32),
            VMEM(view, jnp.float32),
            pltpu.SemaphoreType.DMA((slots,)),
            pltpu.SemaphoreType.DMA,
            pltpu.SemaphoreType.DMA,
        ],
        compiler_params=LIMIT,
        name="pack_panel",
    )(panel_tiles, local, places, tiles.reshape((-1,) + view), front)
    return sent.reshape((row_count * col_count,) + sent.shape[2:])


def pack_kernel(chunks, slot, tiles, first, second, held, load_sem, main_sem):
    count = tiles.shape[0]
    step = count // chunks

    def load(i):
        part = pl.ds(i * step, step)
        return pltpu.make_async_copy(tiles.at[part], held.at[part], load_sem.at[i])

    for i in range(chunks):
        load(i).start()
    for i in range(chunks):
        load(i).wait()

        def send(k, carry):
            where = slot[k]
            owner = where // CAP

            @pl.when(where % CAP == 0)
            def _():
                pltpu.make_async_copy(held.at[k], first.at[owner], main_sem).start()

            @pl.when(where % CAP == 1)
            def _():
                pltpu.make_async_copy(held.at[k], second.at[owner], main_sem).start()

            return carry

        lax.fori_loop(i * step, (i + 1) * step, send, 0)
    pltpu.make_async_copy(held, second, main_sem).wait()


def pack(slot, tiles, devices):
    chunks = 8
    out = jax.ShapeDtypeStruct((devices,) + tiles.shape[1:], jnp.float32)
    return pl.pallas_call(
        functools.partial(pack_kernel, chunks),
        out_shape=[out, out],
        in_specs=[pl.BlockSpec(memory_space=SMEM), pl.BlockSpec(memory_space=ANY)],
        out_specs=[pl.BlockSpec(memory_space=ANY)] * 2,
        scratch_shapes=[
            VMEM(tiles.shape, jnp.float32),
            pltpu.SemaphoreType.DMA((chunks,)),
            pltpu.SemaphoreType.DMA,
        ],
        compiler_params=LIMIT,
        name="pack",
    )(slot, tiles)


def split_kernel(rows, local, front, tiles, *refs):
    outs, (held, sem) = refs[:-2], refs[-2:]
    col_count = len(outs)
    for s in range(CAP):
        copy = pltpu.make_async_copy(tiles.at[local[2 + s]], held.at[s], sem.at[s])
        copy.start()
        copy.wait()

    def block(a, carry):
        for q in range(col_count):
            start = (a * col_count + q) * rows * 2
            outs[q][a] = front[pl.ds(start, rows, stride=2), :]
        return carry

    lax.fori_loop(0, outs[0].shape[0], block, 0, unroll=4)
    for s in range(CAP):
        place = local[2 + CAP + s]

        @pl.when(place >= 0)
        def _():
            for q in range(col_count):
                outs[q][place] += held[s, q]

    for q in range(col_count):
        outs[q][0] = jnp.zeros_like(outs[q][0])


def split_front(local, front, tiles, row_blocks):
    col_count, rows, size = tiles.shape[1:]
    return pl.pallas_call(
        functools.partial(split_kernel, rows),
        out_shape=[jax.ShapeDtypeStruct((row_blocks, rows, size), jnp.float32)] * col_count,
        in_specs=[
            pl.BlockSpec(memory_space=SMEM),
            pl.BlockSpec(memory_space=VMEM),
            pl.BlockSpec(memory_space=ANY),
        ],
        out_specs=[pl.BlockSpec(memory_space=VMEM)] * col_count,
        scratch_shapes=[
            VMEM((CAP, col_count, rows, size), jnp.float32),
            pltpu.SemaphoreType.DMA((CAP,)),
        ],
        compiler_params=LIMIT,
        name="split_front",
    )(local, front, tiles)


def slices_kernel(row_blocks, part_0, part_1, arrived, windows, column, total):
    total[...] = jnp.zeros_like(total)
    parts = (part_0, part_1)
    groups = arrived.shape[1] // CAP
    rows, size = total.shape[1:]

    def source(d, carry):
        for s in range(CAP):
            block = parts[s][d]
            piece = arrived[d, pl.ds(s * groups, groups)].reshape(rows, size)
            total[jnp.where(block < 0, row_blocks, block)] += piece
        return carry

    lax.fori_loop(0, arrived.shape[0], source, 0, unroll=8)
    column[...] = total[pl.ds(0, row_blocks)]
    windows[...] = jnp.broadcast_to(total[0][None], windows.shape)


def sum_slices(parts, arrived, row_count, row_blocks):
    devices, groups, _, size = arrived.shape
    groups = groups // CAP
    rows = groups * 8
    outs = [
        jax.ShapeDtypeStruct((row_count, rows, size), jnp.float32),
        jax.ShapeDtypeStruct((row_blocks, rows, size), jnp.float32),
    ]
    return pl.pallas_call(
        functools.partial(slices_kernel, row_blocks),
        out_shape=outs,
        grid=(1,),
        in_specs=[pl.BlockSpec(memory_space=SMEM)] * 2
        + [pl.BlockSpec((devices, CAP * groups, 8, size), lambda i: (0, 0, 0, 0))],
        out_specs=[pl.BlockSpec(out.shape, lambda i: (0, 0, 0)) for out in outs],
        scratch_shapes=[VMEM((row_blocks + 1, rows, size), jnp.float32)],
        compiler_params=LIMIT,
        name="sum_slices",
    )(*parts, arrived)


def spread_kernel(local, windows, column, *refs):
    own, (out, held, load_sem, sem, few_sem) = refs[:-5], refs[-5:]
    col_count = len(own)
    row_blocks = column.shape[0]
    few = []
    for k in range(col_count):
        for i, j in enumerate((0, *range(k, windows.shape[0], col_count))):
            few.append(
                pltpu.make_async_copy(
                    windows.at[j], out.at[k, row_blocks + i], few_sem.at[len(few)]
                )
            )
    for copy in few:
        copy.start()
    for k in range(col_count):

        @pl.when(local[1] == k)
        def _():
            load = pltpu.make_async_copy(own[k], held, load_sem)
            load.start()
            load.wait()

    held[...] += column[...]
    copies = [
        pltpu.make_async_copy(held, out.at[k, pl.ds(0, row_blocks)], sem.at[k])
        for k in range(col_count)
    ]
    for copy in copies:
        copy.start()
    for copy in copies + few:
        copy.wait()


def spread(local, windows, column, own):
    row_blocks, rows, size = column.shape
    col_count = len(own)
    extra = 1 + windows.shape[0] // col_count
    out = jax.ShapeDtypeStruct((col_count, row_blocks + extra, rows, size), jnp.float32)
    return pl.pallas_call(
        spread_kernel,
        out_shape=out,
        in_specs=[pl.BlockSpec(memory_space=SMEM)]
        + [pl.BlockSpec(memory_space=VMEM)] * 2
        + [pl.BlockSpec(memory_space=ANY)] * col_count,
        out_specs=pl.BlockSpec(memory_space=ANY),
        scratch_shapes=[
            VMEM(column.shape, jnp.float32),
            pltpu.SemaphoreType.DMA,
            pltpu.SemaphoreType.DMA((col_count,)),
            pltpu.SemaphoreType.DMA((col_count * extra,)),
        ],
        compiler_params=LIMIT,
        name="spread",
    )(local, windows, column, *own)


def add_kernel(chunks, places, base, tiles, out, total, held, base_sem, tile_sem):
    slots, parts, rows, size = held.shape
    step = slots // chunks
    last = base.shape[0]
    whole = pl.ds(0, last)
    load_base = pltpu.make_async_copy(base, total.at[whole], base_sem)
    load_base.start()

    def load(i):
        some = pl.ds(i * step, step)
        return pltpu.make_async_copy(tiles.at[some], held.at[some], tile_sem.at[i])

    for i in range(chunks):
        load(i).start()
    load_base.wait()

    def add(j, carry):
        place = places[j]
        start = jnp.where(place < 0, last, place)
        total[pl.ds(start, size, stride=2), :] += held[j].reshape(size, size)
        return carry

    for i in range(chunks):
        load(i).wait()
        lax.fori_loop(i * step, (i + 1) * step, add, 0, unroll=4)
    store = pltpu.make_async_copy(total.at[whole], out, base_sem)
    store.start()
    store.wait()


def add_tiles(places, base, tiles):
    slots, parts, rows, size = tiles.shape
    chunks = 8
    return pl.pallas_call(
        functools.partial(add_kernel, chunks),
        out_shape=jax.ShapeDtypeStruct(base.shape, jnp.float32),
        in_specs=[
            pl.BlockSpec(memory_space=SMEM),
            pl.BlockSpec(memory_space=ANY),
            pl.BlockSpec(memory_space=ANY),
        ],
        out_specs=pl.BlockSpec(memory_space=ANY),
        scratch_shapes=[
            VMEM((base.shape[0] + 2 * size, size), jnp.float32),
            VMEM(tiles.shape, jnp.float32),
            pltpu.SemaphoreType.DMA,
            pltpu.SemaphoreType.DMA((chunks,)),
        ],
        compiler_params=LIMIT,
        name="add_tiles",
    )(places, base, tiles)


def update_kernel(shape, where, front, inverse_t, window, column, base):
    row_count, row_blocks = shape
    row_index, col_index = where[0], where[1]
    size = inverse_t.shape[0]
    held = jnp.dot(
        window[...], inverse_t[...], precision=HIGH, preferred_element_type=jnp.float32
    )
    contract = (((1,), (1,)), ((), ()))

    def block(a, carry):
        rows = jnp.dot(
            column[:, a].reshape(size, size),
            inverse_t[...],
            precision=HIGH,
            preferred_element_type=jnp.float32,
        )
        update = lax.dot_general(
            rows, held, contract, precision=HIGH, preferred_element_type=jnp.float32
        )
        below = a * row_count + row_index > 0
        update = jnp.where(below, update, jnp.zeros_like(update))
        even = pl.ds(a * 2 * size, size, stride=2)
        odd = pl.ds(a * 2 * size + 1, size, stride=2)
        base[even, :] = jnp.where(col_index == 0, rows, front[even, :] - update[:, :size])
        base[odd, :] = front[odd, :] - update[:, size:]
        return carry

    lax.fori_loop(0, row_blocks, block, 0)


def update_front(where, front, inverse_t, window, column, row_count, row_blocks):
    return pl.pallas_call(
        functools.partial(update_kernel, (row_count, row_blocks)),
        out_shape=jax.ShapeDtypeStruct(front.shape, jnp.float32),
        in_specs=[pl.BlockSpec(memory_space=SMEM)] + [pl.BlockSpec(memory_space=VMEM)] * 4,
        out_specs=pl.BlockSpec(memory_space=VMEM),
        compiler_params=LIMIT,
        name="update_front",
    )(where, front, inverse_t, window, column)


def after_kernel(*refs):
    pass


def after(value, *others):
    return pl.pallas_call(
        after_kernel,
        out_shape=jax.ShapeDtypeStruct(value.shape, value.dtype),
        in_specs=[pl.BlockSpec(memory_space=ANY)] * (1 + len(others)),
        out_specs=pl.BlockSpec(memory_space=ANY),
        input_output_aliases={0: 0},
        name="after",
    )(value, *others)


def per_device(front, child_tiles, child_rows, child_cols):
    row_count = lax.axis_size("row")
    col_count = lax.axis_size("col")
    row_index = lax.axis_index("row")
    col_index = lax.axis_index("col")
    both = ("row", "col")
    row_blocks, size, col_blocks = (front.shape[0], front.shape[2], front.shape[3])
    rows = size // col_count
    devices = row_count * col_count
    flat_front = front.reshape(row_blocks * size * col_blocks, size)
    tiles = child_tiles.reshape(-1, col_count, rows, size)
    slot, panel_tiles, message, local = send_tables(
        child_rows.reshape(-1),
        child_cols.reshape(-1),
        row_index,
        col_index,
        row_count,
        col_count,
        size,
    )
    sliced = pack_panel(panel_tiles, local, message, tiles, flat_front, row_count, col_count)
    sliced = lax.all_to_all(sliced, both, split_axis=0, concat_axis=0, tiled=True)
    own = list(split_front(local, flat_front, tiles, row_blocks))
    for k in (7, 2, 4, 5, 3):
        own[k] = lax.ppermute(own[k], "col", [(0, k)])
    first, second = pack(slot, tiles, devices)
    sliced = after(sliced, first)
    message = sliced[:, -1, 0, : 2 * CAP].astype(jnp.int32)
    main, part = ([message[:, h * CAP + s] for s in range(CAP)] for h in range(2))
    windows, column = sum_slices(part, sliced, row_count, row_blocks)
    for k in (6, 1):
        own[k] = lax.ppermute(after(own[k], column), "col", [(0, k)])
    windows = lax.all_to_all(windows, "row", split_axis=0, concat_axis=0, tiled=True)
    first = after(first, windows, *(own[k] for k in (7, 2, 4, 5, 3, 6, 1)))
    first = lax.all_to_all(first, both, split_axis=0, concat_axis=0, tiled=True)
    column = after(spread(local, windows, column, own), first)
    column = lax.all_to_all(column, "col", split_axis=0, concat_axis=0, tiled=True)
    second = lax.all_to_all(
        after(second, column), both, split_axis=0, concat_axis=0, tiled=True
    )
    corner = column[:, row_blocks].reshape(size, size)
    window = jnp.swapaxes(column[:, row_blocks + 1 :], 0, 1).reshape(-1, size)
    factor = jnp.linalg.cholesky(0.5 * (corner + corner.T))
    inverse = jax.scipy.linalg.solve_triangular(
        factor, jnp.eye(size, dtype=jnp.float32), lower=True
    )
    total = add_tiles(main[0], flat_front, first)
    base = update_front(local, total, inverse.T, window, column, row_count, row_blocks)
    return add_tiles(main[1], base, second).reshape(front.shape)


def solution(mesh):
    in_specs = (
        P(None, "row", None, None, "col", None),
        P("row", "col", None, None, None),
        P("row", "col", None),
        P("row", "col", None),
    )
    out_specs = P(None, "row", None, None, "col", None)
    return jax.shard_map(
        per_device, mesh=mesh, in_specs=in_specs, out_specs=out_specs, check_vma=False
    )
```

```python
import functools

import jax
import jax.numpy as jnp
from jax import lax
from jax.experimental import pallas as pl
from jax.experimental.pallas import tpu as pltpu
from jax.sharding import PartitionSpec as P

CAP = 2
HIGH = lax.Precision.HIGHEST
SMEM = pltpu.SMEM
VMEM = pltpu.VMEM
ANY = pl.ANY
RELAY = {5: 7, 3: 1}
LIMIT = pltpu.CompilerParams(vmem_limit_bytes=58 << 20)


def send_tables(parent_rows, parent_cols, row_index, col_index, row_count, col_count, size):
    tiles = parent_rows.shape[0]
    order = jnp.arange(tiles, dtype=jnp.int32)
    row_of = parent_rows % row_count
    owners = row_of * col_count + parent_cols % col_count
    same = (owners[:, None] == owners[None, :]) & (order[None, :] < order[:, None])
    slot = owners * CAP + jnp.sum(same.astype(jnp.int32), axis=1)
    block = parent_rows // row_count
    place = block * (2 * size) + parent_cols // col_count
    panel = parent_cols == 0
    wanted = jnp.arange(row_count * CAP, dtype=jnp.int32)[:, None]
    chosen = panel & (slot == wanted // CAP * (col_count * CAP) + wanted % CAP)
    panel_tiles = jnp.sum(jnp.where(chosen, order, 0), axis=1)
    dest = jnp.arange(row_count * col_count, dtype=jnp.int32)[:, None, None]
    part = jnp.arange(2 * CAP, dtype=jnp.int32)[None, :, None]
    in_main = (part < CAP) & (slot == dest * CAP + part) & ~panel
    dest_row = dest // col_count
    local = (dest_row == row_index) & (col_index == 0)
    in_panel = (part >= CAP) & (slot == dest_row * (col_count * CAP) + part - CAP) & panel
    value = jnp.where(in_main, place + 1, 0) + jnp.where(in_panel & ~local, block + 1, 0)
    message = jnp.sum(value, axis=2) - 1
    message = jnp.where(local[..., 0] & (part[..., 0] == CAP), 0, message)
    mine = jnp.arange(CAP, dtype=jnp.int32)[:, None]
    stays = panel & (col_index == 0) & (slot == row_index * (col_count * CAP) + mine)
    stay_tiles = jnp.sum(jnp.where(stays, order, 0), axis=1)
    stay_blocks = jnp.sum(jnp.where(stays, block + 1, 0), axis=1) - 1
    where = jnp.stack([row_index, col_index]).astype(jnp.int32)
    return slot, panel_tiles, message, jnp.concatenate([where, stay_tiles, stay_blocks])


def pack_panel_kernel(
    panel_tiles, local, places, tiles, front, out, held, corner, block, load_sem, corner_sem, sem
):
    size = block.shape[-1]
    slots = held.shape[0]
    row_count = out.shape[0]
    groups = block.shape[1]
    pltpu.make_async_copy(places, out.at[:, :, CAP * groups], sem).start()
    load_corner = pltpu.make_async_copy(front.at[pl.ds(0, 2 * size)], corner, corner_sem)
    load_corner.start()
    loads = [
        pltpu.make_async_copy(tiles.at[panel_tiles[i]], held.at[i], load_sem.at[i])
        for i in range(slots)
    ]
    for load in loads:
        load.start()
    load_corner.wait()
    block[...] = corner[pl.ds(0, size, stride=2), :].reshape(block.shape)
    for r in range(row_count):
        mine = (local[0] == r) & (local[1] == 0)
        for s in range(CAP):
            loads[r * CAP + s].wait()

        @pl.when(mine)
        def _():
            for s in range(CAP):

                @pl.when(local[2 + CAP + s] == 0)
                def _():
                    block[...] += held[r * CAP + s]

            held[r * CAP] = block[...]

        for s in range(CAP):
            pltpu.make_async_copy(
                held.at[r * CAP + s], out.at[r, :, pl.ds(s * groups, groups)], sem
            ).start()
    pltpu.make_async_copy(out, out, sem).wait()


def pack_panel(panel_tiles, local, message, tiles, front, row_count, col_count):
    size = tiles.shape[-1]
    rows = size // col_count
    groups = rows // 8
    slots = row_count * CAP
    view = (col_count, groups, 8, size)
    places = jnp.pad(
        message.astype(jnp.float32)[:, None, :], ((0, 0), (0, 7), (0, size - message.shape[1]))
    ).reshape(row_count, col_count, 8, size)
    sent = pl.pallas_call(
        pack_panel_kernel,
        out_shape=jax.ShapeDtypeStruct(
            (row_count, col_count, CAP * groups + 1, 8, size), jnp.float32
        ),
        in_specs=[pl.BlockSpec(memory_space=SMEM)] * 2
        + [pl.BlockSpec(memory_space=VMEM)]
        + [pl.BlockSpec(memory_space=ANY)] * 2,
        out_specs=pl.BlockSpec(memory_space=ANY),
        scratch_shapes=[
            VMEM((slots,) + view, jnp.float32),
            VMEM((2 * size, size), jnp.float32),
            VMEM(view, jnp.float32),
            pltpu.SemaphoreType.DMA((slots,)),
            pltpu.SemaphoreType.DMA,
            pltpu.SemaphoreType.DMA,
        ],
        compiler_params=LIMIT,
        name="pack_panel",
    )(panel_tiles, local, places, tiles.reshape((-1,) + view), front)
    return sent.reshape((row_count * col_count,) + sent.shape[2:])


def pack_kernel(chunks, slot, tiles, first, second, held, load_sem, main_sem):
    count = tiles.shape[0]
    step = count // chunks

    def load(i):
        part = pl.ds(i * step, step)
        return pltpu.make_async_copy(tiles.at[part], held.at[part], load_sem.at[i])

    for i in range(chunks):
        load(i).start()
    for i in range(chunks):
        load(i).wait()

        def send(k, carry):
            where = slot[k]
            owner = where // CAP

            @pl.when(where % CAP == 0)
            def _():
                pltpu.make_async_copy(held.at[k], first.at[owner], main_sem).start()

            @pl.when(where % CAP == 1)
            def _():
                pltpu.make_async_copy(held.at[k], second.at[owner], main_sem).start()

            return carry

        lax.fori_loop(i * step, (i + 1) * step, send, 0)
    pltpu.make_async_copy(held, second, main_sem).wait()


def pack(slot, tiles, devices):
    chunks = 8
    out = jax.ShapeDtypeStruct((devices,) + tiles.shape[1:], jnp.float32)
    return pl.pallas_call(
        functools.partial(pack_kernel, chunks),
        out_shape=[out, out],
        in_specs=[pl.BlockSpec(memory_space=SMEM), pl.BlockSpec(memory_space=ANY)],
        out_specs=[pl.BlockSpec(memory_space=ANY)] * 2,
        scratch_shapes=[
            VMEM(tiles.shape, jnp.float32),
            pltpu.SemaphoreType.DMA((chunks,)),
            pltpu.SemaphoreType.DMA,
        ],
        compiler_params=LIMIT,
        name="pack",
    )(slot, tiles)


def split_kernel(rows, row_blocks, local, front, tiles, *refs):
    outs, (held, sem) = refs[:-2], refs[-2:]
    col_count = len(outs) + len(RELAY)
    kept = [q for q in range(col_count) if q not in RELAY]
    target = {q: (outs[kept.index(RELAY.get(q, q))], row_blocks * (q in RELAY)) for q in range(col_count)}
    for s in range(CAP):
        copy = pltpu.make_async_copy(tiles.at[local[2 + s]], held.at[s], sem.at[s])
        copy.start()
        copy.wait()

    def block(a, carry):
        for q, (out, base) in target.items():
            start = (a * col_count + q) * rows * 2
            out[base + a] = front[pl.ds(start, rows, stride=2), :]
        return carry

    lax.fori_loop(0, row_blocks, block, 0, unroll=4)
    for s in range(CAP):
        place = local[2 + CAP + s]

        @pl.when(place >= 0)
        def _():
            for q, (out, base) in target.items():
                out[base + place] += held[s, q]

    for out, base in target.values():
        out[base] = jnp.zeros_like(out[base])


def split_front(local, front, tiles, row_blocks):
    col_count, rows, size = tiles.shape[1:]
    kept = [q for q in range(col_count) if q not in RELAY]
    depth = [row_blocks * (1 + list(RELAY.values()).count(q)) for q in kept]
    outs = pl.pallas_call(
        functools.partial(split_kernel, rows, row_blocks),
        out_shape=[jax.ShapeDtypeStruct((d, rows, size), jnp.float32) for d in depth],
        in_specs=[
            pl.BlockSpec(memory_space=SMEM),
            pl.BlockSpec(memory_space=VMEM),
            pl.BlockSpec(memory_space=ANY),
        ],
        out_specs=[pl.BlockSpec(memory_space=VMEM)] * len(kept),
        scratch_shapes=[
            VMEM((CAP, col_count, rows, size), jnp.float32),
            pltpu.SemaphoreType.DMA((CAP,)),
        ],
        compiler_params=LIMIT,
        name="split_front",
    )(local, front, tiles)
    return dict(zip(kept, outs))


def slices_kernel(row_blocks, part_0, part_1, arrived, windows, column, total):
    total[...] = jnp.zeros_like(total)
    parts = (part_0, part_1)
    groups = arrived.shape[1] // CAP
    rows, size = total.shape[1:]

    def source(d, carry):
        for s in range(CAP):
            block = parts[s][d]
            piece = arrived[d, pl.ds(s * groups, groups)].reshape(rows, size)
            total[jnp.where(block < 0, row_blocks, block)] += piece
        return carry

    lax.fori_loop(0, arrived.shape[0], source, 0, unroll=8)
    column[...] = total[pl.ds(0, row_blocks)]
    windows[...] = jnp.broadcast_to(total[0][None], windows.shape)


def sum_slices(parts, arrived, row_count, row_blocks):
    devices, groups, _, size = arrived.shape
    groups = groups // CAP
    rows = groups * 8
    outs = [
        jax.ShapeDtypeStruct((row_count, rows, size), jnp.float32),
        jax.ShapeDtypeStruct((row_blocks, rows, size), jnp.float32),
    ]
    return pl.pallas_call(
        functools.partial(slices_kernel, row_blocks),
        out_shape=outs,
        grid=(1,),
        in_specs=[pl.BlockSpec(memory_space=SMEM)] * 2
        + [pl.BlockSpec((devices, CAP * groups, 8, size), lambda i: (0, 0, 0, 0))],
        out_specs=[pl.BlockSpec(out.shape, lambda i: (0, 0, 0)) for out in outs],
        scratch_shapes=[VMEM((row_blocks + 1, rows, size), jnp.float32)],
        compiler_params=LIMIT,
        name="sum_slices",
    )(*parts, arrived)


def spread_kernel(local, windows, column, *refs):
    own, (out, held, load_sem, sem, few_sem) = refs[:-5], refs[-5:]
    col_count = len(own)
    row_blocks = column.shape[0]
    few = []
    for k in range(col_count):
        for i, j in enumerate((0, *range(k, windows.shape[0], col_count))):
            few.append(
                pltpu.make_async_copy(
                    windows.at[j], out.at[k, row_blocks + i], few_sem.at[len(few)]
                )
            )
    for copy in few:
        copy.start()
    for k in range(col_count):

        @pl.when(local[1] == k)
        def _():
            load = pltpu.make_async_copy(own[k].at[pl.ds(0, row_blocks)], held, load_sem)
            load.start()
            load.wait()

    held[...] += column[...]
    copies = [
        pltpu.make_async_copy(held, out.at[k, pl.ds(0, row_blocks)], sem.at[k])
        for k in range(col_count)
    ]
    for copy in copies:
        copy.start()
    for copy in copies + few:
        copy.wait()


def spread(local, windows, column, own):
    row_blocks, rows, size = column.shape
    col_count = len(own)
    extra = 1 + windows.shape[0] // col_count
    out = jax.ShapeDtypeStruct((col_count, row_blocks + extra, rows, size), jnp.float32)
    return pl.pallas_call(
        spread_kernel,
        out_shape=out,
        in_specs=[pl.BlockSpec(memory_space=SMEM)]
        + [pl.BlockSpec(memory_space=VMEM)] * 2
        + [pl.BlockSpec(memory_space=ANY)] * col_count,
        out_specs=pl.BlockSpec(memory_space=ANY),
        scratch_shapes=[
            VMEM(column.shape, jnp.float32),
            pltpu.SemaphoreType.DMA,
            pltpu.SemaphoreType.DMA((col_count,)),
            pltpu.SemaphoreType.DMA((col_count * extra,)),
        ],
        compiler_params=LIMIT,
        name="spread",
    )(local, windows, column, *own)


def add_kernel(chunks, places, base, tiles, out, total, held, base_sem, tile_sem):
    slots, parts, rows, size = held.shape
    step = slots // chunks
    last = base.shape[0]
    whole = pl.ds(0, last)
    load_base = pltpu.make_async_copy(base, total.at[whole], base_sem)
    load_base.start()

    def load(i):
        some = pl.ds(i * step, step)
        return pltpu.make_async_copy(tiles.at[some], held.at[some], tile_sem.at[i])

    for i in range(chunks):
        load(i).start()
    load_base.wait()

    def add(j, carry):
        place = places[j]
        start = jnp.where(place < 0, last, place)
        total[pl.ds(start, size, stride=2), :] += held[j].reshape(size, size)
        return carry

    for i in range(chunks):
        load(i).wait()
        lax.fori_loop(i * step, (i + 1) * step, add, 0, unroll=4)
    store = pltpu.make_async_copy(total.at[whole], out, base_sem)
    store.start()
    store.wait()


def add_tiles(places, base, tiles):
    slots, parts, rows, size = tiles.shape
    chunks = 8
    return pl.pallas_call(
        functools.partial(add_kernel, chunks),
        out_shape=jax.ShapeDtypeStruct(base.shape, jnp.float32),
        in_specs=[
            pl.BlockSpec(memory_space=SMEM),
            pl.BlockSpec(memory_space=ANY),
            pl.BlockSpec(memory_space=ANY),
        ],
        out_specs=pl.BlockSpec(memory_space=ANY),
        scratch_shapes=[
            VMEM((base.shape[0] + 2 * size, size), jnp.float32),
            VMEM(tiles.shape, jnp.float32),
            pltpu.SemaphoreType.DMA,
            pltpu.SemaphoreType.DMA((chunks,)),
        ],
        compiler_params=LIMIT,
        name="add_tiles",
    )(places, base, tiles)


def update_kernel(shape, where, front, inverse_t, window, column, base):
    row_count, row_blocks = shape
    row_index, col_index = where[0], where[1]
    size = inverse_t.shape[0]
    held = jnp.dot(
        window[...], inverse_t[...], precision=HIGH, preferred_element_type=jnp.float32
    )
    contract = (((1,), (1,)), ((), ()))

    def block(a, carry):
        rows = jnp.dot(
            column[:, a].reshape(size, size),
            inverse_t[...],
            precision=HIGH,
            preferred_element_type=jnp.float32,
        )
        update = lax.dot_general(
            rows, held, contract, precision=HIGH, preferred_element_type=jnp.float32
        )
        below = a * row_count + row_index > 0
        update = jnp.where(below, update, jnp.zeros_like(update))
        even = pl.ds(a * 2 * size, size, stride=2)
        odd = pl.ds(a * 2 * size + 1, size, stride=2)
        base[even, :] = jnp.where(col_index == 0, rows, front[even, :] - update[:, :size])
        base[odd, :] = front[odd, :] - update[:, size:]
        return carry

    lax.fori_loop(0, row_blocks, block, 0)


def update_front(where, front, inverse_t, window, column, row_count, row_blocks):
    return pl.pallas_call(
        functools.partial(update_kernel, (row_count, row_blocks)),
        out_shape=jax.ShapeDtypeStruct(front.shape, jnp.float32),
        in_specs=[pl.BlockSpec(memory_space=SMEM)] + [pl.BlockSpec(memory_space=VMEM)] * 4,
        out_specs=pl.BlockSpec(memory_space=VMEM),
        compiler_params=LIMIT,
        name="update_front",
    )(where, front, inverse_t, window, column)


def after_kernel(*refs):
    pass


def after(value, *others):
    return pl.pallas_call(
        after_kernel,
        out_shape=jax.ShapeDtypeStruct(value.shape, value.dtype),
        in_specs=[pl.BlockSpec(memory_space=ANY)] * (1 + len(others)),
        out_specs=pl.BlockSpec(memory_space=ANY),
        input_output_aliases={0: 0},
        name="after",
    )(value, *others)


def per_device(front, child_tiles, child_rows, child_cols):
    row_count = lax.axis_size("row")
    col_count = lax.axis_size("col")
    row_index = lax.axis_index("row")
    col_index = lax.axis_index("col")
    both = ("row", "col")
    row_blocks, size, col_blocks = (front.shape[0], front.shape[2], front.shape[3])
    rows = size // col_count
    devices = row_count * col_count
    flat_front = front.reshape(row_blocks * size * col_blocks, size)
    tiles = child_tiles.reshape(-1, col_count, rows, size)
    slot, panel_tiles, message, local = send_tables(
        child_rows.reshape(-1),
        child_cols.reshape(-1),
        row_index,
        col_index,
        row_count,
        col_count,
        size,
    )
    sliced = pack_panel(panel_tiles, local, message, tiles, flat_front, row_count, col_count)
    sliced = lax.all_to_all(sliced, both, split_axis=0, concat_axis=0, tiled=True)
    own = split_front(local, flat_front, tiles, row_blocks)
    for k in (7, 1, 2, 4, 6):
        own[k] = lax.ppermute(own[k], "col", [(0, k)])
    first, second = pack(slot, tiles, devices)
    sliced = after(sliced, first)
    message = sliced[:, -1, 0, : 2 * CAP].astype(jnp.int32)
    main, part = ([message[:, h * CAP + s] for s in range(CAP)] for h in range(2))
    windows, column = sum_slices(part, sliced, row_count, row_blocks)
    handed = own[7][row_blocks:] + own[1][row_blocks:]
    handed = lax.ppermute(after(handed, column), "col", [(via, k) for k, via in RELAY.items()])
    own.update({k: handed for k in RELAY})
    windows = lax.all_to_all(windows, "row", split_axis=0, concat_axis=0, tiled=True)
    first = after(first, windows, *(own[k] for k in (7, 1, 2, 4, 6, 5)))
    first = lax.all_to_all(first, both, split_axis=0, concat_axis=0, tiled=True)
    own = [own[k] for k in range(col_count)]
    column = after(spread(local, windows, column, own), first)
    column = lax.all_to_all(column, "col", split_axis=0, concat_axis=0, tiled=True)
    second = lax.all_to_all(
        after(second, column), both, split_axis=0, concat_axis=0, tiled=True
    )
    corner = column[:, row_blocks].reshape(size, size)
    window = jnp.swapaxes(column[:, row_blocks + 1 :], 0, 1).reshape(-1, size)
    factor = jnp.linalg.cholesky(0.5 * (corner + corner.T))
    inverse = jax.scipy.linalg.solve_triangular(
        factor, jnp.eye(size, dtype=jnp.float32), lower=True
    )
    total = add_tiles(main[0], flat_front, first)
    base = update_front(local, total, inverse.T, window, column, row_count, row_blocks)
    return add_tiles(main[1], base, second).reshape(front.shape)


def solution(mesh):
    in_specs = (
        P(None, "row", None, None, "col", None),
        P("row", "col", None, None, None),
        P("row", "col", None),
        P("row", "col", None),
    )
    out_specs = P(None, "row", None, None, "col", None)
    return jax.shard_map(
        per_device, mesh=mesh, in_specs=in_specs, out_specs=out_specs, check_vma=False
    )
```

```python
import functools

import jax
import jax.numpy as jnp
from jax import lax
from jax.experimental import pallas as pl
from jax.experimental.pallas import tpu as pltpu
from jax.sharding import PartitionSpec as P

CAP = 2
HIGH = lax.Precision.HIGHEST
SMEM = pltpu.SMEM
VMEM = pltpu.VMEM
ANY = pl.ANY
RELAY = {5: 7, 3: 1}
LIMIT = pltpu.CompilerParams(vmem_limit_bytes=58 << 20)


def send_tables(parent_rows, parent_cols, row_index, col_index, row_count, col_count, size):
    tiles = parent_rows.shape[0]
    order = jnp.arange(tiles, dtype=jnp.int32)
    row_of = parent_rows % row_count
    owners = row_of * col_count + parent_cols % col_count
    same = (owners[:, None] == owners[None, :]) & (order[None, :] < order[:, None])
    slot = owners * CAP + jnp.sum(same.astype(jnp.int32), axis=1)
    block = parent_rows // row_count
    place = block * (2 * size) + parent_cols // col_count
    panel = parent_cols == 0
    wanted = jnp.arange(row_count * CAP, dtype=jnp.int32)[:, None]
    chosen = panel & (slot == wanted // CAP * (col_count * CAP) + wanted % CAP)
    panel_tiles = jnp.sum(jnp.where(chosen, order, 0), axis=1)
    dest = jnp.arange(row_count * col_count, dtype=jnp.int32)[:, None, None]
    part = jnp.arange(2 * CAP, dtype=jnp.int32)[None, :, None]
    in_main = (part < CAP) & (slot == dest * CAP + part) & ~panel
    dest_row = dest // col_count
    local = (dest_row == row_index) & (col_index == 0)
    in_panel = (part >= CAP) & (slot == dest_row * (col_count * CAP) + part - CAP) & panel
    value = jnp.where(in_main, place + 1, 0) + jnp.where(in_panel & ~local, block + 1, 0)
    message = jnp.sum(value, axis=2) - 1
    message = jnp.where(local[..., 0] & (part[..., 0] == CAP), 0, message)
    mine = jnp.arange(CAP, dtype=jnp.int32)[:, None]
    stays = panel & (col_index == 0) & (slot == row_index * (col_count * CAP) + mine)
    stay_tiles = jnp.sum(jnp.where(stays, order, 0), axis=1)
    stay_blocks = jnp.sum(jnp.where(stays, block + 1, 0), axis=1) - 1
    where = jnp.stack([row_index, col_index]).astype(jnp.int32)
    return slot, panel_tiles, message, jnp.concatenate([where, stay_tiles, stay_blocks])


def pack_kernel(chunks, slot, panel_tiles, local, tiles, front, first, second, *scratch):
    held, corner, block, load_sem, main_sem, panel_sem, corner_sem = scratch
    count, parts, rows, size = tiles.shape
    step = count // chunks
    row_count, col_count = first.shape[:2]
    row_index, col_index = local[0], local[1]

    def load(i):
        part = pl.ds(i * step, step)
        return pltpu.make_async_copy(tiles.at[part], held.at[part], load_sem.at[i])

    load_corner = pltpu.make_async_copy(front.at[pl.ds(0, 2 * parts * rows)], corner, corner_sem)
    for i in range(chunks):
        load(i).start()
    load_corner.start()
    for i in range(chunks):
        load(i).wait()

        def send(k, carry):
            where = slot[k]
            owner = where // CAP

            @pl.when(where % CAP == 0)
            def _():
                pltpu.make_async_copy(
                    held.at[k],
                    first.at[owner // col_count, owner % col_count, pl.ds(CAP, parts)],
                    main_sem,
                ).start()

            @pl.when(where % CAP == 1)
            def _():
                pltpu.make_async_copy(held.at[k], second.at[owner], main_sem).start()

            return carry

        lax.fori_loop(i * step, (i + 1) * step, send, 0)
    load_corner.wait()
    block[...] = corner[pl.ds(0, parts * rows, stride=2), :].reshape(block.shape)
    for s in range(CAP):

        @pl.when(local[2 + CAP + s] == 0)
        def _():
            block[...] += held[local[2 + s]]

    for r in range(row_count):
        for s in range(CAP):
            own = (row_index == r) & (col_index == 0) & (s == 0)

            @pl.when(own)
            def _():
                pltpu.make_async_copy(block, first.at[r, :, s], panel_sem).start()

            @pl.when(jnp.logical_not(own))
            def _():
                pltpu.make_async_copy(
                    held.at[panel_tiles[r * CAP + s]], first.at[r, :, s], panel_sem
                ).start()

    pltpu.make_async_copy(held, second, main_sem).wait()
    some = pl.ds(0, row_count * CAP)
    pltpu.make_async_copy(held.at[some], second.at[some], panel_sem).wait()


def pack(slot, panel_tiles, local, tiles, front, row_count, col_count):
    count, parts, rows, size = tiles.shape
    chunks = 8
    return pl.pallas_call(
        functools.partial(pack_kernel, chunks),
        out_shape=[
            jax.ShapeDtypeStruct((row_count, col_count, CAP + parts, rows, size), jnp.float32),
            jax.ShapeDtypeStruct((row_count * col_count, parts, rows, size), jnp.float32),
        ],
        in_specs=[pl.BlockSpec(memory_space=SMEM)] * 3 + [pl.BlockSpec(memory_space=ANY)] * 2,
        out_specs=[pl.BlockSpec(memory_space=ANY)] * 2,
        scratch_shapes=[
            VMEM(tiles.shape, jnp.float32),
            VMEM((2 * parts * rows, size), jnp.float32),
            VMEM((parts, rows, size), jnp.float32),
            pltpu.SemaphoreType.DMA((chunks,)),
            pltpu.SemaphoreType.DMA,
            pltpu.SemaphoreType.DMA,
            pltpu.SemaphoreType.DMA,
        ],
        compiler_params=LIMIT,
        name="pack",
    )(slot, panel_tiles, local, tiles, front)


def split_kernel(rows, row_blocks, local, front, tiles, *refs):
    outs, (held, sem) = refs[:-2], refs[-2:]
    col_count = len(outs) + len(RELAY)
    kept = [q for q in range(col_count) if q not in RELAY]
    target = {q: (outs[kept.index(RELAY.get(q, q))], row_blocks * (q in RELAY)) for q in range(col_count)}
    for s in range(CAP):
        copy = pltpu.make_async_copy(tiles.at[local[2 + s]], held.at[s], sem.at[s])
        copy.start()
        copy.wait()

    def block(a, carry):
        for q, (out, base) in target.items():
            start = (a * col_count + q) * rows * 2
            out[base + a] = front[pl.ds(start, rows, stride=2), :]
        return carry

    lax.fori_loop(0, row_blocks, block, 0, unroll=4)
    for s in range(CAP):
        place = local[2 + CAP + s]

        @pl.when(place >= 0)
        def _():
            for q, (out, base) in target.items():
                out[base + place] += held[s, q]

    for out, base in target.values():
        out[base] = jnp.zeros_like(out[base])


def split_front(local, front, tiles, row_blocks):
    col_count, rows, size = tiles.shape[1:]
    kept = [q for q in range(col_count) if q not in RELAY]
    depth = [row_blocks * (1 + list(RELAY.values()).count(q)) for q in kept]
    outs = pl.pallas_call(
        functools.partial(split_kernel, rows, row_blocks),
        out_shape=[jax.ShapeDtypeStruct((d, rows, size), jnp.float32) for d in depth],
        in_specs=[
            pl.BlockSpec(memory_space=SMEM),
            pl.BlockSpec(memory_space=VMEM),
            pl.BlockSpec(memory_space=ANY),
        ],
        out_specs=[pl.BlockSpec(memory_space=VMEM)] * len(kept),
        scratch_shapes=[
            VMEM((CAP, col_count, rows, size), jnp.float32),
            pltpu.SemaphoreType.DMA((CAP,)),
        ],
        compiler_params=LIMIT,
        name="split_front",
    )(local, front, tiles)
    return dict(zip(kept, outs))


def slices_kernel(row_blocks, part_0, part_1, arrived, windows, column, total):
    total[...] = jnp.zeros_like(total)
    parts = (part_0, part_1)

    def source(d, carry):
        for s in range(CAP):
            block = parts[s][d]
            total[jnp.where(block < 0, row_blocks, block)] += arrived[d, s]
        return carry

    lax.fori_loop(0, arrived.shape[0], source, 0, unroll=8)
    column[...] = total[pl.ds(0, row_blocks)]
    windows[...] = jnp.broadcast_to(total[0][None], windows.shape)


def sum_slices(parts, arrived, row_count, row_blocks):
    devices, _, rows, size = arrived.shape
    outs = [
        jax.ShapeDtypeStruct((row_count, rows, size), jnp.float32),
        jax.ShapeDtypeStruct((row_blocks, rows, size), jnp.float32),
    ]
    return pl.pallas_call(
        functools.partial(slices_kernel, row_blocks),
        out_shape=outs,
        grid=(1,),
        in_specs=[pl.BlockSpec(memory_space=SMEM)] * 2
        + [pl.BlockSpec((devices, CAP, rows, size), lambda i: (0, 0, 0, 0))],
        out_specs=[pl.BlockSpec(out.shape, lambda i: (0, 0, 0)) for out in outs],
        scratch_shapes=[VMEM((row_blocks + 1, rows, size), jnp.float32)],
        compiler_params=LIMIT,
        name="sum_slices",
    )(*parts, arrived)


def spread_kernel(local, windows, column, *refs):
    col_count = len(refs) - 3
    own, (out, held, sem) = refs[:col_count], refs[col_count:]
    row_blocks = column.shape[0]
    for k in range(col_count):

        @pl.when(local[1] == k)
        def _():
            copy = pltpu.make_async_copy(own[k].at[pl.ds(0, row_blocks)], held, sem)
            copy.start()
            copy.wait()

    total = column[...] + held[...]
    for k in range(col_count):
        out[k, pl.ds(0, row_blocks)] = total
        for i, j in enumerate((0, *range(k, windows.shape[0], col_count))):
            out[k, row_blocks + i] = windows[j]


def spread(local, windows, column, own):
    row_blocks, rows, size = column.shape
    extra = 1 + windows.shape[0] // len(own)
    out = jax.ShapeDtypeStruct((len(own), row_blocks + extra, rows, size), jnp.float32)
    return pl.pallas_call(
        spread_kernel,
        out_shape=out,
        in_specs=[pl.BlockSpec(memory_space=SMEM)]
        + [pl.BlockSpec(memory_space=VMEM)] * 2
        + [pl.BlockSpec(memory_space=ANY)] * len(own),
        out_specs=pl.BlockSpec(memory_space=VMEM),
        scratch_shapes=[VMEM(column.shape, jnp.float32), pltpu.SemaphoreType.DMA],
        compiler_params=LIMIT,
        name="spread",
    )(local, windows, column, *own)


def add_kernel(chunks, places, base, tiles, out, total, held, base_sem, tile_sem):
    slots, parts, rows, size = held.shape
    step = slots // chunks
    last = base.shape[0]
    whole = pl.ds(0, last)
    load_base = pltpu.make_async_copy(base, total.at[whole], base_sem)
    load_base.start()

    def load(i):
        some = pl.ds(i * step, step)
        skip = pl.ds(tiles.shape[1] - parts, parts)
        return pltpu.make_async_copy(tiles.at[some, skip], held.at[some], tile_sem.at[i])

    for i in range(chunks):
        load(i).start()
    load_base.wait()

    def add(j, carry):
        place = places[j]
        start = jnp.where(place < 0, last, place)
        total[pl.ds(start, size, stride=2), :] += held[j].reshape(size, size)
        return carry

    for i in range(chunks):
        load(i).wait()
        lax.fori_loop(i * step, (i + 1) * step, add, 0, unroll=4)
    store = pltpu.make_async_copy(total.at[whole], out, base_sem)
    store.start()
    store.wait()


def add_tiles(places, base, tiles, skip):
    slots, parts, rows, size = tiles.shape
    chunks = 8
    return pl.pallas_call(
        functools.partial(add_kernel, chunks),
        out_shape=jax.ShapeDtypeStruct(base.shape, jnp.float32),
        in_specs=[
            pl.BlockSpec(memory_space=SMEM),
            pl.BlockSpec(memory_space=ANY),
            pl.BlockSpec(memory_space=ANY),
        ],
        out_specs=pl.BlockSpec(memory_space=ANY),
        scratch_shapes=[
            VMEM((base.shape[0] + 2 * size, size), jnp.float32),
            VMEM((slots, parts - skip, rows, size), jnp.float32),
            pltpu.SemaphoreType.DMA,
            pltpu.SemaphoreType.DMA((chunks,)),
        ],
        compiler_params=LIMIT,
        name="add_tiles",
    )(places, base, tiles)


def update_kernel(shape, where, front, inverse_t, window, column, base):
    row_count, row_blocks = shape
    row_index, col_index = where[0], where[1]
    size = inverse_t.shape[0]
    held = jnp.dot(
        window[...], inverse_t[...], precision=HIGH, preferred_element_type=jnp.float32
    )
    contract = (((1,), (1,)), ((), ()))

    def block(a, carry):
        rows = jnp.dot(
            column[:, a].reshape(size, size),
            inverse_t[...],
            precision=HIGH,
            preferred_element_type=jnp.float32,
        )
        update = lax.dot_general(
            rows, held, contract, precision=HIGH, preferred_element_type=jnp.float32
        )
        below = a * row_count + row_index > 0
        update = jnp.where(below, update, jnp.zeros_like(update))
        even = pl.ds(a * 2 * size, size, stride=2)
        odd = pl.ds(a * 2 * size + 1, size, stride=2)
        base[even, :] = jnp.where(col_index == 0, rows, front[even, :] - update[:, :size])
        base[odd, :] = front[odd, :] - update[:, size:]
        return carry

    lax.fori_loop(0, row_blocks, block, 0)


def update_front(where, front, inverse_t, window, column, row_count, row_blocks):
    return pl.pallas_call(
        functools.partial(update_kernel, (row_count, row_blocks)),
        out_shape=jax.ShapeDtypeStruct(front.shape, jnp.float32),
        in_specs=[pl.BlockSpec(memory_space=SMEM)] + [pl.BlockSpec(memory_space=VMEM)] * 4,
        out_specs=pl.BlockSpec(memory_space=VMEM),
        compiler_params=LIMIT,
        name="update_front",
    )(where, front, inverse_t, window, column)


def after_kernel(*refs):
    pass


def after(value, *others):
    return pl.pallas_call(
        after_kernel,
        out_shape=jax.ShapeDtypeStruct(value.shape, value.dtype),
        in_specs=[pl.BlockSpec(memory_space=ANY)] * (1 + len(others)),
        out_specs=pl.BlockSpec(memory_space=ANY),
        input_output_aliases={0: 0},
        name="after",
    )(value, *others)


def per_device(front, child_tiles, child_rows, child_cols):
    row_count = lax.axis_size("row")
    col_count = lax.axis_size("col")
    row_index = lax.axis_index("row")
    col_index = lax.axis_index("col")
    both = ("row", "col")
    row_blocks, size, col_blocks = (front.shape[0], front.shape[2], front.shape[3])
    rows = size // col_count
    devices = row_count * col_count
    flat_front = front.reshape(row_blocks * size * col_blocks, size)
    tiles = child_tiles.reshape(-1, col_count, rows, size)
    slot, panel_tiles, message, local = send_tables(
        child_rows.reshape(-1),
        child_cols.reshape(-1),
        row_index,
        col_index,
        row_count,
        col_count,
        size,
    )
    message = lax.all_to_all(message, both, split_axis=0, concat_axis=0, tiled=True)
    main, part = ([message[:, h * CAP + s] for s in range(CAP)] for h in range(2))
    first, second = pack(slot, panel_tiles, local, tiles, flat_front, row_count, col_count)
    first = first.reshape((devices,) + first.shape[2:])
    own = split_front(local, flat_front, tiles, row_blocks)
    for k in (7, 1, 2, 4, 6):
        own[k] = lax.ppermute(own[k], "col", [(0, k)])
    handed = own[7][row_blocks:] + own[1][row_blocks:]
    handed = lax.ppermute(handed, "col", [(via, k) for k, via in RELAY.items()])
    own.update({k: handed for k in RELAY})
    own = [own[k] for k in range(col_count)]
    arrived = lax.all_to_all(first, both, split_axis=0, concat_axis=0, tiled=True)
    windows, column = sum_slices(part, arrived, row_count, row_blocks)
    windows = lax.all_to_all(windows, "row", split_axis=0, concat_axis=0, tiled=True)
    column = spread(local, windows, column, own)
    column = lax.all_to_all(column, "col", split_axis=0, concat_axis=0, tiled=True)
    second = lax.all_to_all(
        after(second, column), both, split_axis=0, concat_axis=0, tiled=True
    )
    corner = column[:, row_blocks].reshape(size, size)
    window = jnp.swapaxes(column[:, row_blocks + 1 :], 0, 1).reshape(-1, size)
    factor = jnp.linalg.cholesky(0.5 * (corner + corner.T))
    inverse = jax.scipy.linalg.solve_triangular(
        factor, jnp.eye(size, dtype=jnp.float32), lower=True
    )
    total = add_tiles(main[0], flat_front, arrived, CAP)
    base = update_front(local, total, inverse.T, window, column, row_count, row_blocks)
    return add_tiles(main[1], base, second, 0).reshape(front.shape)


def solution(mesh):
    in_specs = (
        P(None, "row", None, None, "col", None),
        P("row", "col", None, None, None),
        P("row", "col", None),
        P("row", "col", None),
    )
    out_specs = P(None, "row", None, None, "col", None)
    return jax.shard_map(
        per_device, mesh=mesh, in_specs=in_specs, out_specs=out_specs, check_vma=False
    )
```
